32 devices in a mesh: dp: 2 (over y), blk: 4 (over z), head: 4 (over x, core).
Axes of the slice: x: 2, y: 2, z: 4, core: 2. Of those that a mesh axis runs over, the one named last changes fastest.
Arguments:
- queries: bfloat16 [2048, 2048], P(('dp', 'blk', 'head')), parts along dimension 0, may hold values from -5 to 5
- key_states: bfloat16 [2048, 2048], P(('dp', 'blk', 'head')), parts along dimension 0, may hold values from -5 to 5
- value_states: bfloat16 [2048, 2048], P(('dp', 'blk', 'head')), parts along dimension 0, may hold values from -6 to 6
- upstream: bfloat16 [2048, 2048], P(('dp', 'blk'), 'head'), parts along dimension 0, may hold values from -6 to 6
- clip_lengths: int32 [8], P('dp'), parts along dimension 0, may hold values from 1 to 512, 1024 in all
Outputs:
- attended: bfloat16 [2048, 2048], P(('dp', 'blk'), 'head'), parts along dimension 0
- query_grads: bfloat16 [2048, 2048], P(('dp', 'blk'), 'head'), parts along dimension 0
- key_grads: bfloat16 [2048, 2048], P(('dp', 'blk'), 'head'), parts along dimension 0
- value_grads: bfloat16 [2048, 2048], P(('dp', 'blk'), 'head'), parts along dimension 0
The draws below stay inside these ranges and needn't reach their ends.
There are 2 independent parts, one for each index of `dp`. The reference program is written for one: setup_inputs(seed, part) draws one part's arguments, and reference() takes and returns one part's arrays. A program takes and returns all parts, laid end to end along the dimension named above; each array names one. Nothing has to cross between parts.
Inputs may be any that keep to these rules, and one draw needn't show every extreme that they name: `clip_lengths`: 4 clip lengths that sum to 1024; the longest has exactly 512 tokens.
All inputs are finite; a program needn't handle non-finite values.
Results may differ from the reference program's by a relative error of at most 0.015.
Values may be sent and summed in bfloat16 or wider, within the bound.
No kernel may reach another device: no remote copies, remote signals or barrier semaphores. Data moves between devices by JAX's collectives and lax.ppermute only.
A program may use at most 64 MiB of HBM per device.

```python
import math
import jax
import jax.numpy as jnp
import numpy as np
from jax import lax

HEADS = 16
HEAD_DIM = 128
BLOCK = 256
SEQ = 1024
MOST = 512
CLIPS = 4


def draw_queries(key, part):
    noise_key = jax.random.fold_in(jax.random.fold_in(key, 1), 0)
    drawn = jnp.clip(jax.random.normal(noise_key, (SEQ, HEADS * HEAD_DIM), jnp.float32), -5.0, 5.0)
    return drawn.astype(jnp.bfloat16)


def draw_key_states(key, part):
    noise_key = jax.random.fold_in(jax.random.fold_in(key, 2), 0)
    drawn = jnp.clip(jax.random.normal(noise_key, (SEQ, HEADS * HEAD_DIM), jnp.float32), -5.0, 5.0)
    return drawn.astype(jnp.bfloat16)


def steps_of(key, shape, shards, smallest, largest):
    factor_of, own = 1.0, jax.random.fold_in(key, 6)
    for dim, parts in shards:
        steps = jnp.exp(jax.random.uniform(jax.random.fold_in(own, dim), (parts,), jnp.float32, smallest / len(shards), largest / len(shards)))
        factor_of = factor_of * jnp.repeat(steps, shape[dim] // parts).reshape([-1 if axis == dim else 1 for axis in range(len(shape))])
    return factor_of


def length_profile(amount, total, limit, skew):
    portions = [(1 << 20) // math.isqrt(rank ** skew) + 1 for rank in range(2, amount + 1)]
    spare, given = total - limit - (amount - 1), [1] * (amount - 1)
    while spare > 0:
        movable = [i for i in range(amount - 1) if given[i] < limit]
        whole, remaining = sum([portions[i] for i in movable]), spare
        for i in movable:
            extra = min(limit - given[i], max(1, remaining * portions[i] // whole), spare)
            given[i] = given[i] + extra
            spare = spare - extra
    return np.array([limit] + given)


def uneven_parts(own_key, amount, total, bound, skew):
    if amount == 2:
        one = jax.random.randint(own_key, (), max(1, total - bound), min(bound, total - 1) + 1)
        return jnp.stack([one, total - one])
    lengths = jnp.asarray(length_profile(amount, total, bound, skew), jnp.int32)
    couples = (amount - 1) // 2
    source_of, taker = lengths[1:1 + 2 * couples:2], lengths[2:2 + 2 * couples:2]
    margin = jnp.minimum(source_of - 1, bound - taker)
    passed = jax.random.randint(jax.random.fold_in(own_key, 1), (couples,), 0, 1 << 20) % (margin + 1)
    lengths = lengths.at[1:1 + 2 * couples:2].set(source_of - passed).at[2:2 + 2 * couples:2].set(taker + passed)
    return lengths[jax.random.permutation(jax.random.fold_in(own_key, 2), amount)]


def noise(stream_key, shape, spread, reach, shards=(), held_as=jnp.bfloat16):
    result = spread * jax.random.normal(stream_key, shape, jnp.float32)
    if shards:
        result = result * steps_of(stream_key, shape, shards, -0.22, 0.18)
    return jnp.clip(result, -reach, reach).astype(held_as)


def setup_inputs(seed: int = 0, part: int = 0) -> dict:
    seeds = jax.random.split(jax.random.key(seed), 6)
    part_keys = jax.random.split(jax.random.fold_in(seeds[5], part), 6)
    return {
        "queries": draw_queries(jax.random.fold_in(jax.random.fold_in(seeds[5], part), 71), part),
        "key_states": draw_key_states(jax.random.fold_in(jax.random.fold_in(seeds[5], part), 71), part),
        "value_states": noise(part_keys[2], (SEQ, HEADS * HEAD_DIM), 1.0, 6.0, ((0, 16),)),
        "upstream": noise(part_keys[3], (SEQ, HEADS * HEAD_DIM), 1.0, 6.0, ((0, 4), (1, 4))),
        "clip_lengths": uneven_parts(part_keys[4], CLIPS, SEQ, MOST, 1).astype(jnp.int32),
    }


masked_fill = -1.0e30


def clip_index(clip_ends, positions, seq_total):
    counted = jnp.sum((positions[:, None] >= clip_ends[None, :]).astype(jnp.int32), axis=1)
    inside = (positions >= 0) & (positions < seq_total)
    return jnp.where(inside, counted, -1).astype(jnp.int32)


def rounded(values_in):
    return lax.optimization_barrier(values_in.astype(jnp.bfloat16)).astype(jnp.float32)


def window_pass(query_tile, key_tile, value_tile, upstream_tile, query_ids, key_ids):
    score_scale = HEAD_DIM ** -0.5
    query_wide = query_tile.astype(jnp.float32)
    key_wide = key_tile.astype(jnp.float32)
    value_wide = value_tile.astype(jnp.float32)
    upstream_wide = upstream_tile.astype(jnp.float32)
    same_clip = (query_ids[:, None] == key_ids[None, :])[None]
    scores = score_scale * jnp.einsum("qhe,khe->hqk", query_wide, key_wide)
    scores = jnp.where(same_clip, scores, masked_fill)
    row_max = jnp.max(scores, axis=2, keepdims=True)
    totals = jnp.sum(jnp.where(same_clip, jnp.exp(scores - row_max), 0.0), axis=2, keepdims=True)
    log_norm = row_max + jnp.log(totals)
    chances = jnp.where(same_clip, jnp.exp(scores - log_norm), 0.0)
    weights = rounded(chances)
    attended = rounded(jnp.einsum("hqk,khe->qhe", weights, value_wide))
    offsets = jnp.sum(upstream_wide * attended, axis=2)
    dchances = jnp.einsum("qhe,khe->hqk", upstream_wide, value_wide)
    dscores = rounded(chances * (dchances - jnp.transpose(offsets)[:, :, None]))
    query_part = score_scale * jnp.einsum("hqk,khe->qhe", dscores, key_wide)
    key_part = score_scale * jnp.einsum("hqk,qhe->khe", dscores, query_wide)
    value_part = jnp.einsum("hqk,qhe->khe", weights, upstream_wide)
    return attended, query_part, key_part, value_part


def reference(queries, key_states, value_states, upstream, clip_lengths):
    feature_width = HEADS * HEAD_DIM
    block_count = SEQ // BLOCK
    clip_ends = jnp.cumsum(clip_lengths).astype(jnp.int32)
    padded_keys = jnp.pad(key_states, ((BLOCK, 0), (0, 0)))
    padded_values = jnp.pad(value_states, ((BLOCK, 0), (0, 0)))
    positions = jnp.arange(SEQ + BLOCK, dtype=jnp.int32) - BLOCK
    padded_ids = clip_index(clip_ends, positions, SEQ)

    def advance(totals, block_index):
        row_start = (block_index * BLOCK).astype(jnp.int32)
        query_tile = lax.dynamic_slice_in_dim(queries, row_start, BLOCK, 0).reshape(BLOCK, HEADS, HEAD_DIM)
        upstream_tile = lax.dynamic_slice_in_dim(upstream, row_start, BLOCK, 0).reshape(BLOCK, HEADS, HEAD_DIM)
        key_tile = lax.dynamic_slice_in_dim(padded_keys, row_start, 2 * BLOCK, 0).reshape(2 * BLOCK, HEADS, HEAD_DIM)
        value_tile = lax.dynamic_slice_in_dim(padded_values, row_start, 2 * BLOCK, 0).reshape(2 * BLOCK, HEADS, HEAD_DIM)
        query_ids = lax.dynamic_slice_in_dim(padded_ids, row_start + BLOCK, BLOCK, 0)
        key_ids = lax.dynamic_slice_in_dim(padded_ids, row_start, 2 * BLOCK, 0)
        attended, query_part, key_part, value_part = window_pass(query_tile, key_tile, value_tile, upstream_tile, query_ids, key_ids)
        update = jnp.stack([key_part, value_part]).reshape(2, 2 * BLOCK, feature_width)
        window = lax.dynamic_slice_in_dim(totals, row_start, 2 * BLOCK, 1)
        totals = lax.dynamic_update_slice_in_dim(totals, window + update, row_start, 1)
        return totals, (attended.reshape(BLOCK, feature_width), query_part.reshape(BLOCK, feature_width))

    start_totals = jnp.zeros((2, SEQ + BLOCK, feature_width), jnp.float32)
    totals, collected = lax.scan(advance, start_totals, jnp.arange(block_count, dtype=jnp.int32))
    attended = collected[0].reshape(SEQ, feature_width).astype(jnp.bfloat16)
    query_grads = collected[1].reshape(SEQ, feature_width).astype(jnp.bfloat16)
    grad_pairs = totals[:, BLOCK:]
    return attended, query_grads, grad_pairs[0].astype(jnp.bfloat16), grad_pairs[1].astype(jnp.bfloat16)
```

```python
import math

import jax
import jax.numpy as jnp
from jax import lax
from jax.experimental import pallas as pl
from jax.experimental.pallas import tpu as pltpu
from jax.sharding import PartitionSpec as P

HEAD_DIM = 128

masked_fill = -1e30
score_scale = HEAD_DIM ** (-0.5)
exp2_scale = score_scale * math.log2(math.e)

VMEM = pl.BlockSpec(memory_space=pltpu.VMEM)
SMEM = pl.BlockSpec(memory_space=pltpu.SMEM)
ANY = pl.BlockSpec(memory_space=pl.ANY)


def bf16(*shape):
    return jax.ShapeDtypeStruct(shape, jnp.bfloat16)


def partner_exchange(rows, step):
    route = [(i, i ^ step) for i in range(lax.axis_size("head"))]
    return lax.ppermute(rows, "head", route)


def block_exchange(rows, parity):
    parts, blocks = lax.axis_size("dp"), lax.axis_size("blk")
    route = []
    for part in range(parts):
        for block in range(blocks):
            other = block + 1 if block % 2 == parity else block - 1
            if 0 <= other < blocks:
                route.append((part * blocks + block, part * blocks + other))
            elif part ^ 1 < parts:
                route.append((part * blocks + block, (part ^ 1) * blocks + block))
    return lax.ppermute(rows, ("dp", "blk"), route)


def to_previous(rows):
    blocks = lax.axis_size("blk")
    return lax.ppermute(rows, "blk", [(i, i - 1) for i in range(1, blocks)])


def is_even():
    return lax.rem(lax.axis_index("blk"), 2) == 0


def place(step, size):
    owner = jnp.bitwise_xor(lax.axis_index("head"), step)
    return pl.ds(pl.multiple_of(owner * size, size), size)


def cut_pieces(queries, key_states, value_states, upstream):
    sharers = lax.axis_size("head")
    rows, features = queries.shape
    width = features // sharers
    block_rows = rows * sharers

    def kernel(q, k, v, u, *rest):
        pairs, singles = rest[:sharers], rest[sharers : 2 * sharers]
        first, second, sems = rest[2 * sharers :]
        copies = []

        def copy(source, target):
            copies.append(pltpu.make_async_copy(source, target, sems.at[len(copies)]))

        for step in range(sharers):
            columns = place(step, width)
            copy(k.at[:, columns], pairs[step].at[pl.ds(0, rows)])
            copy(q.at[:, columns], pairs[step].at[pl.ds(rows, rows)])
            copy(v.at[:, columns], singles[step])

        def swap(forward, backward):
            made = []
            for step in range(sharers):
                made.append(
                    pltpu.make_async_copy(
                        v.at[:, pl.ds(step * width, width)],
                        forward.at[pl.ds(step * rows, rows)],
                        sems.at[len(copies) + step],
                    )
                )
            made.append(pltpu.make_async_copy(u, backward, sems.at[len(copies) + sharers]))
            return made

        for c in copies:
            c.start()

        @pl.when(is_even())
        def _():
            for c in swap(first, second):
                c.start()
            for c in swap(first, second):
                c.wait()

        @pl.when(jnp.logical_not(is_even()))
        def _():
            for c in swap(second, first):
                c.start()
            for c in swap(second, first):
                c.wait()

        for c in copies:
            c.wait()

    out = pl.pallas_call(
        kernel,
        out_shape=[bf16(2 * rows, width)] * sharers
        + [bf16(rows, width)] * sharers
        + [bf16(block_rows, width)] * 2,
        in_specs=[ANY] * 4,
        out_specs=[VMEM] * (2 * sharers + 2),
        scratch_shapes=[pltpu.SemaphoreType.DMA((4 * sharers + 1,))],
        name="cut_pieces",
    )(queries, key_states, value_states, upstream)
    return out[:sharers], out[sharers : 2 * sharers], out[2 * sharers], out[2 * sharers + 1]


def join_keys_queries(pairs):
    sharers = len(pairs)
    rows, width = pairs[0].shape[0] // 2, pairs[0].shape[1]
    block_rows = rows * sharers

    def kernel(*refs):
        pairs_in = refs[:sharers]
        keys, queries, first, second = refs[sharers:]
        for step in range(sharers):
            where = place(step, rows)
            keys[where, :] = pairs_in[step][pl.ds(0, rows), :]
            queries[where, :] = pairs_in[step][pl.ds(rows, rows), :]

        @pl.when(is_even())
        def _():
            first[...] = keys[...]
            second[...] = queries[...]

        @pl.when(jnp.logical_not(is_even()))
        def _():
            first[...] = queries[...]
            second[...] = keys[...]

    return pl.pallas_call(
        kernel,
        out_shape=[bf16(block_rows, width)] * 4,
        in_specs=[VMEM] * sharers,
        out_specs=[VMEM] * 4,
        name="join_keys_queries",
    )(*pairs)


def cut_previous_values(first_got, second_got, sharers):
    block_rows, width = first_got.shape
    rows = block_rows // sharers

    def kernel(first, second, *out):
        def split(forward, backward):
            for step in range(sharers):
                out[step][...] = forward[place(step, rows), :]
            out[sharers][...] = backward[...]

        @pl.when(is_even())
        def _():
            split(second, first)

        @pl.when(jnp.logical_not(is_even()))
        def _():
            split(first, second)

    out = pl.pallas_call(
        kernel,
        out_shape=[bf16(rows, width)] * sharers + [bf16(block_rows, width)],
        in_specs=[VMEM] * 2,
        out_specs=[VMEM] * (sharers + 1),
        name="cut_previous_values",
    )(first_got, second_got)
    return out[:sharers], out[sharers]


def clip_ids(lengths, shape, axis, block, blocks):
    position = block * shape[axis] + lax.broadcasted_iota(jnp.int32, shape, axis)
    ids, end = jnp.zeros(shape, jnp.int32), jnp.int32(0)
    for clip in range(lengths.shape[0]):
        end = end + lengths[clip]
        ids = ids + (position >= end).astype(jnp.int32)
    return jnp.where(jnp.logical_and(block >= 0, block < blocks), ids, -1)


def mask_bias(key_ids, query_ids):
    return jnp.where(key_ids == query_ids, 0.0, masked_fill).astype(jnp.float32)


def by_rows(a, b):
    return lax.dot_general(a, b, (((1,), (1,)), ((), ())), preferred_element_type=jnp.float32)


def by_columns(a, b):
    return lax.dot_general(a, b, (((0,), (0,)), ((), ())), preferred_element_type=jnp.float32)


def product(a, b):
    return jnp.dot(a, b, preferred_element_type=jnp.float32)


def own_part(keys, queries, singles, upstream, clip_lengths):
    sharers = len(singles)
    block_rows, width = keys.shape
    rows = block_rows // sharers
    heads = width // HEAD_DIM

    def kernel(k, q, u, lengths, *rest):
        singles_in = rest[:sharers]
        values, stats, bias = rest[sharers:]
        block, blocks = lax.axis_index("blk"), lax.axis_size("blk")
        for step in range(sharers):
            values[place(step, rows), :] = singles_in[step][...]
        bias[...] = mask_bias(
            clip_ids(lengths, (block_rows, 1), 0, block, blocks),
            clip_ids(lengths, (1, block_rows), 1, block, blocks),
        )
        for head in range(heads):
            columns = pl.ds(head * HEAD_DIM, HEAD_DIM)
            scores = by_rows(k[:, columns], q[:, columns]) * exp2_scale + bias[...]
            row_max = jnp.max(scores, axis=0, keepdims=True)
            grown = jnp.exp2(scores - row_max)
            totals = jnp.sum(grown, axis=0, keepdims=True)
            dchances = by_rows(values[:, columns], u[:, columns])
            offset = jnp.sum(grown * dchances, axis=0, keepdims=True) / totals
            stats[pl.ds(head, 1), :] = row_max + jnp.log2(totals)
            stats[pl.ds(heads + head, 1), :] = offset

    return pl.pallas_call(
        kernel,
        out_shape=[bf16(block_rows, width), jax.ShapeDtypeStruct((2 * heads, block_rows), jnp.float32)],
        in_specs=[VMEM] * 3 + [SMEM] + [VMEM] * sharers,
        out_specs=[VMEM] * 2,
        scratch_shapes=[pltpu.VMEM((block_rows, block_rows), jnp.float32)],
        compiler_params=pltpu.CompilerParams(vmem_limit_bytes=24 * 2**20),
        name="own_part",
    )(keys, queries, upstream, clip_lengths, *singles)


def window(keys, queries, values, upstream, first_got, second_got, previous_values, next_upstream, next_stats, clip_lengths):
    sharers = len(previous_values)
    block_rows, width = keys.shape
    rows = block_rows // sharers
    heads = width // HEAD_DIM
    square = (block_rows, block_rows)

    def kernel(k, q, v, u, first, second, nu, stats, lengths, *rest):
        pieces = rest[:sharers]
        attended, query_grads, key_grads, value_grads = rest[sharers : sharers + 4]
        pk, nq, pv, own_bias, previous_bias, next_bias = rest[sharers + 4 :]
        block, blocks = lax.axis_index("blk"), lax.axis_size("blk")

        @pl.when(is_even())
        def _():
            pk[...] = second[...]
            nq[...] = first[...]

        @pl.when(jnp.logical_not(is_even()))
        def _():
            pk[...] = first[...]
            nq[...] = second[...]

        for step in range(sharers):
            pv[place(step, rows), :] = pieces[step][...]

        tall, wide = (block_rows, 1), (1, block_rows)
        key_ids = clip_ids(lengths, tall, 0, block, blocks)
        query_ids = clip_ids(lengths, wide, 1, block, blocks)
        own_bias[...] = mask_bias(key_ids, query_ids)
        previous_bias[...] = mask_bias(clip_ids(lengths, tall, 0, block - 1, blocks), query_ids)
        next_bias[...] = mask_bias(key_ids, clip_ids(lengths, wide, 1, block + 1, blocks))

        for head in range(heads):
            columns = pl.ds(head * HEAD_DIM, HEAD_DIM)
            key, query, value, up = k[:, columns], q[:, columns], v[:, columns], u[:, columns]
            past_key, past_value = pk[:, columns], pv[:, columns]
            later_query, later_up = nq[:, columns], nu[:, columns]

            scores = by_rows(key, query) * exp2_scale + own_bias[...]
            past_scores = by_rows(past_key, query) * exp2_scale + previous_bias[...]
            row_max = jnp.maximum(
                jnp.max(scores, axis=0, keepdims=True), jnp.max(past_scores, axis=0, keepdims=True)
            )
            grown = jnp.exp2(scores - row_max)
            past_grown = jnp.exp2(past_scores - row_max)
            share = 1.0 / (
                jnp.sum(grown, axis=0, keepdims=True) + jnp.sum(past_grown, axis=0, keepdims=True)
            )
            chances = grown * share
            past_chances = past_grown * share
            dchances = by_rows(value, up)
            past_dchances = by_rows(past_value, up)
            offset = jnp.sum(chances * dchances, axis=0, keepdims=True) + jnp.sum(
                past_chances * past_dchances, axis=0, keepdims=True
            )
            dscores = (chances * (dchances - offset)).astype(jnp.bfloat16)
            past_dscores = (past_chances * (past_dchances - offset)).astype(jnp.bfloat16)
            weights = chances.astype(jnp.bfloat16)
            past_weights = past_chances.astype(jnp.bfloat16)
            attended[:, columns] = (
                by_columns(weights, value) + by_columns(past_weights, past_value)
            ).astype(jnp.bfloat16)
            query_grads[:, columns] = (
                score_scale * (by_columns(dscores, key) + by_columns(past_dscores, past_key))
            ).astype(jnp.bfloat16)

            later_scores = by_rows(key, later_query) * exp2_scale + next_bias[...]
            later_max = jnp.max(later_scores, axis=0, keepdims=True)
            later_grown = jnp.exp2(later_scores - later_max)
            later_total = jnp.sum(later_grown, axis=0, keepdims=True)
            later_dchances = by_rows(value, later_up)
            later_offset = jnp.sum(later_grown * later_dchances, axis=0, keepdims=True) / later_total
            far_norm, far_offset = stats[pl.ds(head, 1), :], stats[pl.ds(heads + head, 1), :]
            near_norm = later_max + jnp.log2(later_total)
            top = jnp.maximum(far_norm, near_norm)
            far_part, near_part = jnp.exp2(far_norm - top), jnp.exp2(near_norm - top)
            whole = 1.0 / (far_part + near_part)
            full_offset = (far_part * far_offset + near_part * later_offset) * whole
            later_chances = later_grown * (jnp.exp2(later_max - top) * whole)
            later_dscores = (later_chances * (later_dchances - full_offset)).astype(jnp.bfloat16)
            later_weights = later_chances.astype(jnp.bfloat16)
            key_grads[:, columns] = (
                score_scale * (product(dscores, query) + product(later_dscores, later_query))
            ).astype(jnp.bfloat16)
            value_grads[:, columns] = (
                product(weights, up) + product(later_weights, later_up)
            ).astype(jnp.bfloat16)

    return pl.pallas_call(
        kernel,
        out_shape=[bf16(block_rows, width)] * 4,
        in_specs=[VMEM] * 8 + [SMEM] + [VMEM] * sharers,
        out_specs=[VMEM] * 4,
        scratch_shapes=[pltpu.VMEM((block_rows, width), jnp.bfloat16)] * 3
        + [pltpu.VMEM(square, jnp.float32)] * 3,
        compiler_params=pltpu.CompilerParams(vmem_limit_bytes=40 * 2**20),
        name="window",
    )(keys, queries, values, upstream, first_got, second_got, next_upstream, next_stats, clip_lengths, *previous_values)


def on_device(queries, key_states, value_states, upstream, clip_lengths):
    sharers = lax.axis_size("head")
    steps = range(1, sharers)
    pairs, singles, first, second = cut_pieces(queries, key_states, value_states, upstream)
    pairs = [pairs[0]] + [partner_exchange(pairs[step], step) for step in steps]
    first_got, second_got = block_exchange(first, 0), block_exchange(second, 1)
    keys, query_rows, first, second = join_keys_queries(pairs)
    singles = [singles[0]] + [partner_exchange(singles[step], step) for step in steps]
    later_first, later_second = block_exchange(first, 0), block_exchange(second, 1)
    previous, next_upstream = cut_previous_values(first_got, second_got, sharers)
    previous = [previous[0]] + [partner_exchange(previous[step], step) for step in steps]
    values, stats = own_part(keys, query_rows, singles, upstream, clip_lengths)
    next_stats = to_previous(stats)
    return tuple(
        window(
            keys, query_rows, values, upstream, later_first, later_second,
            previous, next_upstream, next_stats, clip_lengths,
        )
    )


def solution(mesh):
    return jax.shard_map(
        on_device,
        mesh=mesh,
        in_specs=(
            P(("dp", "blk", "head"), None),
            P(("dp", "blk", "head"), None),
            P(("dp", "blk", "head"), None),
            P(("dp", "blk"), "head"),
            P("dp"),
        ),
        out_specs=(
            P(("dp", "blk"), "head"),
            P(("dp", "blk"), "head"),
            P(("dp", "blk"), "head"),
            P(("dp", "blk"), "head"),
        ),
        check_vma=False,
    )
```

```python
import math

import jax
import jax.numpy as jnp
from jax import lax
from jax.experimental import pallas as pl
from jax.experimental.pallas import tpu as pltpu
from jax.sharding import PartitionSpec as P

HEAD_DIM = 128

masked_fill = -1e30
score_scale = HEAD_DIM ** (-0.5)
exp2_scale = score_scale * math.log2(math.e)

VMEM = pl.BlockSpec(memory_space=pltpu.VMEM)
SMEM = pl.BlockSpec(memory_space=pltpu.SMEM)
ANY = pl.BlockSpec(memory_space=pl.ANY)


def bf16(*shape):
    return jax.ShapeDtypeStruct(shape, jnp.bfloat16)


def partner_exchange(rows, step):
    route = [(i, i ^ step) for i in range(lax.axis_size("head"))]
    return lax.ppermute(rows, "head", route)


def block_exchange(rows, parity):
    parts, blocks = lax.axis_size("dp"), lax.axis_size("blk")
    route = []
    for part in range(parts):
        for block in range(blocks):
            other = block + 1 if block % 2 == parity else block - 1
            if 0 <= other < blocks:
                route.append((part * blocks + block, part * blocks + other))
            elif part ^ 1 < parts:
                route.append((part * blocks + block, (part ^ 1) * blocks + block))
    return lax.ppermute(rows, ("dp", "blk"), route)


def to_previous(rows):
    blocks = lax.axis_size("blk")
    return lax.ppermute(rows, "blk", [(i, i - 1) for i in range(1, blocks)])


def is_even():
    return lax.rem(lax.axis_index("blk"), 2) == 0


def place(step, size):
    owner = jnp.bitwise_xor(lax.axis_index("head"), step)
    return pl.ds(pl.multiple_of(owner * size, size), size)


def small_kernel():
    return pltpu.CompilerParams(vmem_limit_bytes=4 * 2**20)


def weighed(flops):
    return pl.CostEstimate(flops=int(flops), bytes_accessed=0, transcendentals=0)


def cut_pieces(queries, key_states, value_states, upstream):
    sharers = lax.axis_size("head")
    rows, features = queries.shape
    width = features // sharers
    block_rows = rows * sharers
    heights = [(2 + sharers // 2) * rows if step < 2 else 2 * rows for step in range(sharers)]

    def kernel(q, k, v, u, *rest):
        pieces = rest[:sharers]
        first, second, sems = rest[sharers:]
        copies = []

        def copy(source, target):
            copies.append(pltpu.make_async_copy(source, target, sems.at[len(copies)]))

        for step in range(sharers):
            columns = place(step, width)
            copy(k.at[:, columns], pieces[step].at[pl.ds(0, rows)])
            copy(q.at[:, columns], pieces[step].at[pl.ds(rows, rows)])
            copy(v.at[:, columns], pieces[step % 2].at[pl.ds((2 + step // 2) * rows, rows)])

        def swap(forward, backward):
            made = []
            for step in range(sharers):
                made.append(
                    pltpu.make_async_copy(
                        v.at[:, pl.ds(step * width, width)],
                        forward.at[pl.ds(step * rows, rows)],
                        sems.at[len(copies) + step],
                    )
                )
            made.append(pltpu.make_async_copy(u, backward, sems.at[len(copies) + sharers]))
            return made

        for c in copies:
            c.start()

        @pl.when(is_even())
        def _():
            for c in swap(first, second):
                c.start()
            for c in swap(first, second):
                c.wait()

        @pl.when(jnp.logical_not(is_even()))
        def _():
            for c in swap(second, first):
                c.start()
            for c in swap(second, first):
                c.wait()

        for c in copies:
            c.wait()

    out = pl.pallas_call(
        kernel,
        out_shape=[bf16(height, width) for height in heights] + [bf16(block_rows, width)] * 2,
        in_specs=[ANY] * 4,
        out_specs=[VMEM] * (sharers + 2),
        scratch_shapes=[pltpu.SemaphoreType.DMA((4 * sharers + 1,))],
        compiler_params=pltpu.CompilerParams(vmem_limit_bytes=53 * 2**20),
        name="cut_pieces",
    )(queries, key_states, value_states, upstream)
    return out[:sharers], out[sharers], out[sharers + 1]


def stack_values(own, got, rows):
    pairs = own.shape[0] // rows - 2
    width = own.shape[1]

    def kernel(mine, theirs, *out):
        for pair in range(1, pairs):
            where = pl.ds((2 + pair) * rows, rows)
            out[pair - 1][pl.ds(0, rows), :] = mine[where, :]
            out[pair - 1][pl.ds(rows, rows), :] = theirs[where, :]

    return pl.pallas_call(
        kernel,
        out_shape=[bf16(2 * rows, width)] * (pairs - 1),
        in_specs=[VMEM] * 2,
        out_specs=[VMEM] * (pairs - 1),
        compiler_params=small_kernel(),
        cost_estimate=weighed(5e9),
        name="stack_values",
    )(own, got)


def join_keys_queries(pieces, rows):
    sharers = len(pieces)
    width = pieces[0].shape[1]
    block_rows = rows * sharers

    def kernel(*refs):
        pieces_in = refs[:sharers]
        keys, queries, first, second = refs[sharers:]
        for step in range(sharers):
            where = place(step, rows)
            keys[where, :] = pieces_in[step][pl.ds(0, rows), :]
            queries[where, :] = pieces_in[step][pl.ds(rows, rows), :]

        @pl.when(is_even())
        def _():
            first[...] = keys[...]
            second[...] = queries[...]

        @pl.when(jnp.logical_not(is_even()))
        def _():
            first[...] = queries[...]
            second[...] = keys[...]

    return pl.pallas_call(
        kernel,
        out_shape=[bf16(block_rows, width)] * 4,
        in_specs=[VMEM] * sharers,
        out_specs=[VMEM] * 4,
        compiler_params=small_kernel(),
        cost_estimate=weighed(5e9),
        name="join_keys_queries",
    )(*pieces)


def cut_previous_values(first_got, second_got, sharers, far):
    block_rows, width = first_got.shape
    rows = block_rows // sharers

    def kernel(first, second, *out):
        out = out[len(far) :]
        def split(forward, backward):
            for step in range(sharers):
                out[step][...] = forward[place(step, rows), :]
            out[sharers][...] = backward[...]

        @pl.when(is_even())
        def _():
            split(second, first)

        @pl.when(jnp.logical_not(is_even()))
        def _():
            split(first, second)

    out = pl.pallas_call(
        kernel,
        out_shape=[bf16(rows, width)] * sharers + [bf16(block_rows, width)],
        in_specs=[VMEM] * (2 + len(far)),
        out_specs=[VMEM] * (sharers + 1),
        compiler_params=small_kernel(),
        cost_estimate=weighed(0),
        name="cut_previous_values",
    )(first_got, second_got, *far)
    return out[:sharers], out[sharers]


def clip_ids(lengths, shape, axis, block, blocks):
    position = block * shape[axis] + lax.broadcasted_iota(jnp.int32, shape, axis)
    ids, end = jnp.zeros(shape, jnp.int32), jnp.int32(0)
    for clip in range(lengths.shape[0]):
        end = end + lengths[clip]
        ids = ids + (position >= end).astype(jnp.int32)
    return jnp.where(jnp.logical_and(block >= 0, block < blocks), ids, -1)


def mask_bias(key_ids, query_ids):
    return jnp.where(key_ids == query_ids, 0.0, masked_fill).astype(jnp.float32)


def by_rows(a, b):
    return lax.dot_general(a, b, (((1,), (1,)), ((), ())), preferred_element_type=jnp.float32)


def by_columns(a, b):
    return lax.dot_general(a, b, (((0,), (0,)), ((), ())), preferred_element_type=jnp.float32)


def product(a, b):
    return jnp.dot(a, b, preferred_element_type=jnp.float32)


def own_part(keys, queries, chip_values, far_values, upstream, clip_lengths):
    sharers = 2 + 2 * len(far_values)
    block_rows, width = keys.shape
    rows = block_rows // sharers
    heads = width // HEAD_DIM

    def kernel(k, q, u, lengths, *rest):
        values_in = [ref.at[pl.ds(2 * rows, rows)] for ref in rest[:2]]
        for ref in rest[2 : 1 + sharers // 2]:
            values_in += [ref.at[pl.ds(0, rows)], ref.at[pl.ds(rows, rows)]]
        values, stats, bias = rest[1 + sharers // 2 :]
        block, blocks = lax.axis_index("blk"), lax.axis_size("blk")
        for step in range(sharers):
            values[place(step, rows), :] = values_in[step][...]
        bias[...] = mask_bias(
            clip_ids(lengths, (block_rows, 1), 0, block, blocks),
            clip_ids(lengths, (1, block_rows), 1, block, blocks),
        )
        for head in range(heads):
            columns = pl.ds(head * HEAD_DIM, HEAD_DIM)
            scores = by_rows(k[:, columns], q[:, columns]) * exp2_scale + bias[...]
            row_max = jnp.max(scores, axis=0, keepdims=True)
            grown = jnp.exp2(scores - row_max)
            totals = jnp.sum(grown, axis=0, keepdims=True)
            dchances = by_rows(values[:, columns], u[:, columns])
            offset = jnp.sum(grown * dchances, axis=0, keepdims=True) / totals
            stats[pl.ds(head, 1), :] = row_max + jnp.log2(totals)
            stats[pl.ds(heads + head, 1), :] = offset

    return pl.pallas_call(
        kernel,
        out_shape=[bf16(block_rows, width), jax.ShapeDtypeStruct((2 * heads, block_rows), jnp.float32)],
        in_specs=[VMEM] * 3 + [SMEM] + [VMEM] * (1 + sharers // 2),
        out_specs=[VMEM] * 2,
        scratch_shapes=[pltpu.VMEM((block_rows, block_rows), jnp.float32)],
        compiler_params=pltpu.CompilerParams(vmem_limit_bytes=8 * 2**20),
        cost_estimate=weighed(2e10),
        name="own_part",
    )(keys, queries, upstream, clip_lengths, *chip_values, *far_values)


def own_rows(keys, queries, values, upstream, first_got, second_got, previous_values, clip_lengths):
    sharers = len(previous_values)
    block_rows, width = keys.shape
    rows = block_rows // sharers
    heads = width // HEAD_DIM
    square = (block_rows, block_rows)

    def kernel(k, q, v, u, first, second, lengths, *rest):
        pieces = rest[:sharers]
        attended, query_grads, key_part, value_part = rest[sharers : sharers + 4]
        pk, pv, own_bias, previous_bias = rest[sharers + 4 :]
        block, blocks = lax.axis_index("blk"), lax.axis_size("blk")

        @pl.when(is_even())
        def _():
            pk[...] = second[...]

        @pl.when(jnp.logical_not(is_even()))
        def _():
            pk[...] = first[...]

        for step in range(sharers):
            pv[place(step, rows), :] = pieces[step][...]

        tall, wide = (block_rows, 1), (1, block_rows)
        query_ids = clip_ids(lengths, wide, 1, block, blocks)
        own_bias[...] = mask_bias(clip_ids(lengths, tall, 0, block, blocks), query_ids)
        previous_bias[...] = mask_bias(clip_ids(lengths, tall, 0, block - 1, blocks), query_ids)

        for head in range(heads):
            columns = pl.ds(head * HEAD_DIM, HEAD_DIM)
            key, query, value, up = k[:, columns], q[:, columns], v[:, columns], u[:, columns]
            past_key, past_value = pk[:, columns], pv[:, columns]
            scores = by_rows(key, query) * exp2_scale + own_bias[...]
            past_scores = by_rows(past_key, query) * exp2_scale + previous_bias[...]
            row_max = jnp.maximum(
                jnp.max(scores, axis=0, keepdims=True), jnp.max(past_scores, axis=0, keepdims=True)
            )
            grown = jnp.exp2(scores - row_max)
            past_grown = jnp.exp2(past_scores - row_max)
            share = 1.0 / (
                jnp.sum(grown, axis=0, keepdims=True) + jnp.sum(past_grown, axis=0, keepdims=True)
            )
            chances = grown * share
            past_chances = past_grown * share
            dchances = by_rows(value, up)
            past_dchances = by_rows(past_value, up)
            offset = jnp.sum(chances * dchances, axis=0, keepdims=True) + jnp.sum(
                past_chances * past_dchances, axis=0, keepdims=True
            )
            dscores = (chances * (dchances - offset)).astype(jnp.bfloat16)
            past_dscores = (past_chances * (past_dchances - offset)).astype(jnp.bfloat16)
            weights = chances.astype(jnp.bfloat16)
            past_weights = past_chances.astype(jnp.bfloat16)
            attended[:, columns] = (
                by_columns(weights, value) + by_columns(past_weights, past_value)
            ).astype(jnp.bfloat16)
            query_grads[:, columns] = (
                score_scale * (by_columns(dscores, key) + by_columns(past_dscores, past_key))
            ).astype(jnp.bfloat16)
            key_part[:, columns] = product(dscores, query)
            value_part[:, columns] = product(weights, up)

    return pl.pallas_call(
        kernel,
        out_shape=[bf16(block_rows, width)] * 2
        + [jax.ShapeDtypeStruct((block_rows, width), jnp.float32)] * 2,
        in_specs=[VMEM] * 6 + [SMEM] + [VMEM] * sharers,
        out_specs=[VMEM] * 4,
        scratch_shapes=[pltpu.VMEM((block_rows, width), jnp.bfloat16)] * 2
        + [pltpu.VMEM(square, jnp.float32)] * 2,
        compiler_params=pltpu.CompilerParams(vmem_limit_bytes=16 * 2**20),
        name="own_rows",
    )(keys, queries, values, upstream, first_got, second_got, clip_lengths, *previous_values)


def next_rows(keys, values, first_got, second_got, next_upstream, next_stats, key_part, value_part, clip_lengths):
    block_rows, width = keys.shape
    heads = width // HEAD_DIM
    square = (block_rows, block_rows)

    def kernel(k, v, first, second, nu, stats, key_part, value_part, lengths, key_grads, value_grads, nq, bias):
        block, blocks = lax.axis_index("blk"), lax.axis_size("blk")

        @pl.when(is_even())
        def _():
            nq[...] = first[...]

        @pl.when(jnp.logical_not(is_even()))
        def _():
            nq[...] = second[...]

        bias[...] = mask_bias(
            clip_ids(lengths, (block_rows, 1), 0, block, blocks),
            clip_ids(lengths, (1, block_rows), 1, block + 1, blocks),
        )
        for head in range(heads):
            columns = pl.ds(head * HEAD_DIM, HEAD_DIM)
            key, value, query, up = k[:, columns], v[:, columns], nq[:, columns], nu[:, columns]
            scores = by_rows(key, query) * exp2_scale + bias[...]
            row_max = jnp.max(scores, axis=0, keepdims=True)
            grown = jnp.exp2(scores - row_max)
            total = jnp.sum(grown, axis=0, keepdims=True)
            dchances = by_rows(value, up)
            offset = jnp.sum(grown * dchances, axis=0, keepdims=True) / total
            far_norm, far_offset = stats[pl.ds(head, 1), :], stats[pl.ds(heads + head, 1), :]
            near_norm = row_max + jnp.log2(total)
            top = jnp.maximum(far_norm, near_norm)
            far_part, near_part = jnp.exp2(far_norm - top), jnp.exp2(near_norm - top)
            whole = 1.0 / (far_part + near_part)
            full_offset = (far_part * far_offset + near_part * offset) * whole
            chances = grown * (jnp.exp2(row_max - top) * whole)
            dscores = (chances * (dchances - full_offset)).astype(jnp.bfloat16)
            weights = chances.astype(jnp.bfloat16)
            key_grads[:, columns] = (
                score_scale * (key_part[:, columns] + product(dscores, query))
            ).astype(jnp.bfloat16)
            value_grads[:, columns] = (value_part[:, columns] + product(weights, up)).astype(jnp.bfloat16)

    return pl.pallas_call(
        kernel,
        out_shape=[bf16(block_rows, width)] * 2,
        in_specs=[VMEM] * 8 + [SMEM],
        out_specs=[VMEM] * 2,
        scratch_shapes=[pltpu.VMEM((block_rows, width), jnp.bfloat16), pltpu.VMEM(square, jnp.float32)],
        compiler_params=pltpu.CompilerParams(vmem_limit_bytes=16 * 2**20),
        name="next_rows",
    )(keys, values, first_got, second_got, next_upstream, next_stats, key_part, value_part, clip_lengths)


def on_device(queries, key_states, value_states, upstream, clip_lengths):
    sharers = lax.axis_size("head")
    steps = range(1, sharers)
    rows = queries.shape[0]
    pieces, first, second = cut_pieces(queries, key_states, value_states, upstream)
    pieces = [pieces[0]] + [partner_exchange(pieces[step], step) for step in steps]
    first_got, second_got = block_exchange(first, 0), block_exchange(second, 1)
    stacked = stack_values(pieces[0], pieces[1], rows)
    far_values = [partner_exchange(stack, 2 * pair + 2) for pair, stack in enumerate(stacked)]
    keys, query_rows, first, second = join_keys_queries(pieces, rows)
    previous, next_upstream = cut_previous_values(first_got, second_got, sharers, far_values)
    first_got, second_got = block_exchange(first, 0), block_exchange(second, 1)
    previous = [previous[0]] + [partner_exchange(previous[step], step) for step in steps]
    values, stats = own_part(keys, query_rows, pieces[:2], far_values, upstream, clip_lengths)
    next_stats = to_previous(stats)
    attended, query_grads, key_part, value_part = own_rows(
        keys, query_rows, values, upstream, first_got, second_got, previous, clip_lengths
    )
    key_grads, value_grads = next_rows(
        keys, values, first_got, second_got, next_upstream, next_stats, key_part, value_part, clip_lengths
    )
    return attended, query_grads, key_grads, value_grads


def solution(mesh):
    return jax.shard_map(
        on_device,
        mesh=mesh,
        in_specs=(
            P(("dp", "blk", "head"), None),
            P(("dp", "blk", "head"), None),
            P(("dp", "blk", "head"), None),
            P(("dp", "blk"), "head"),
            P("dp"),
        ),
        out_specs=(
            P(("dp", "blk"), "head"),
            P(("dp", "blk"), "head"),
            P(("dp", "blk"), "head"),
            P(("dp", "blk"), "head"),
        ),
        check_vma=False,
    )
```

```python
import math

import jax
import jax.numpy as jnp
from jax import lax
from jax.experimental import pallas as pl
from jax.experimental.pallas import tpu as pltpu
from jax.sharding import PartitionSpec as P

HEAD_DIM = 128

masked_fill = -1e30
score_scale = HEAD_DIM ** (-0.5)
exp2_scale = score_scale * math.log2(math.e)

VMEM = pl.BlockSpec(memory_space=pltpu.VMEM)
SMEM = pl.BlockSpec(memory_space=pltpu.SMEM)
ANY = pl.BlockSpec(memory_space=pl.ANY)


def bf16(*shape):
    return jax.ShapeDtypeStruct(shape, jnp.bfloat16)


def partner_exchange(rows, step):
    route = [(i, i ^ step) for i in range(lax.axis_size("head"))]
    return lax.ppermute(rows, "head", route)


def block_exchange(rows, parity):
    parts, blocks = lax.axis_size("dp"), lax.axis_size("blk")
    route = []
    for part in range(parts):
        for block in range(blocks):
            other = block + 1 if block % 2 == parity else block - 1
            if 0 <= other < blocks:
                route.append((part * blocks + block, part * blocks + other))
            elif part ^ 1 < parts:
                route.append((part * blocks + block, (part ^ 1) * blocks + block))
    return lax.ppermute(rows, ("dp", "blk"), route)


def to_previous(rows):
    blocks = lax.axis_size("blk")
    return lax.ppermute(rows, "blk", [(i, i - 1) for i in range(1, blocks)])


def is_even():
    return lax.rem(lax.axis_index("blk"), 2) == 0


def place(step, size):
    owner = jnp.bitwise_xor(lax.axis_index("head"), step)
    return pl.ds(pl.multiple_of(owner * size, size), size)


def small_kernel():
    return pltpu.CompilerParams(vmem_limit_bytes=4 * 2**20)


def weighed(flops):
    return pl.CostEstimate(flops=int(flops), bytes_accessed=0, transcendentals=0)


def cut_pieces(queries, key_states, value_states):
    sharers = lax.axis_size("head")
    rows, features = queries.shape
    width = features // sharers
    heights = [(2 + sharers // 2) * rows if step < 2 else 2 * rows for step in range(sharers)]

    def kernel(q, k, v, *rest):
        pieces, sems = rest[:sharers], rest[sharers]
        copies = []

        def copy(source, target):
            copies.append(pltpu.make_async_copy(source, target, sems.at[len(copies)]))

        for step in range(sharers):
            columns = place(step, width)
            copy(k.at[:, columns], pieces[step].at[pl.ds(0, rows)])
            copy(q.at[:, columns], pieces[step].at[pl.ds(rows, rows)])
            copy(v.at[:, columns], pieces[step % 2].at[pl.ds((2 + step // 2) * rows, rows)])
        for c in copies:
            c.start()
        for c in copies:
            c.wait()

    return pl.pallas_call(
        kernel,
        out_shape=[bf16(height, width) for height in heights],
        in_specs=[ANY] * 3,
        out_specs=[VMEM] * sharers,
        scratch_shapes=[pltpu.SemaphoreType.DMA((3 * sharers,))],
        compiler_params=pltpu.CompilerParams(vmem_limit_bytes=53 * 2**20),
        name="cut_pieces",
    )(queries, key_states, value_states)


def stack_values(own, got, upstream, rows):
    pairs = own.shape[0] // rows - 2
    width = own.shape[1]
    block_rows = upstream.shape[0]

    def kernel(mine, theirs, u, *out):
        first, second = out[pairs - 1 :]

        def stack(target, pair, start):
            where = pl.ds((2 + pair) * rows, rows)
            target[pl.ds(start, rows), :] = mine[where, :]
            target[pl.ds(start + rows, rows), :] = theirs[where, :]

        for pair in range(1, pairs):
            stack(out[pair - 1], pair, 0)

        def spread(forward, backward):
            for pair in range(pairs):
                stack(forward, pair, 2 * rows * pair)
            backward[...] = u[...]

        @pl.when(is_even())
        def _():
            spread(first, second)

        @pl.when(jnp.logical_not(is_even()))
        def _():
            spread(second, first)

    out = pl.pallas_call(
        kernel,
        out_shape=[bf16(2 * rows, width)] * (pairs - 1) + [bf16(block_rows, width)] * 2,
        in_specs=[VMEM] * 3,
        out_specs=[VMEM] * (pairs + 1),
        compiler_params=small_kernel(),
        cost_estimate=weighed(5e9),
        name="stack_values",
    )(own, got, upstream)
    return out[: pairs - 1], out[-2], out[-1]


def join_keys_queries(pieces, rows):
    sharers = len(pieces)
    width = pieces[0].shape[1]
    block_rows = rows * sharers

    def kernel(*refs):
        pieces_in = refs[:sharers]
        keys, queries, first, second = refs[sharers:]
        for step in range(sharers):
            where = place(step, rows)
            keys[where, :] = pieces_in[step][pl.ds(0, rows), :]
            queries[where, :] = pieces_in[step][pl.ds(rows, rows), :]

        @pl.when(is_even())
        def _():
            first[...] = keys[...]
            second[...] = queries[...]

        @pl.when(jnp.logical_not(is_even()))
        def _():
            first[...] = queries[...]
            second[...] = keys[...]

    return pl.pallas_call(
        kernel,
        out_shape=[bf16(block_rows, width)] * 4,
        in_specs=[VMEM] * sharers,
        out_specs=[VMEM] * 4,
        compiler_params=small_kernel(),
        cost_estimate=weighed(5e9),
        name="join_keys_queries",
    )(*pieces)


def cut_previous_values(first_got, second_got, pairs, far):
    block_rows, width = first_got.shape
    rows = block_rows // pairs

    def kernel(first, second, *out):
        out = out[len(far) :]

        def split(forward, backward):
            for pair in range(pairs):
                out[pair][...] = forward[pl.ds(pair * rows, rows), :]
            out[pairs][...] = backward[...]

        @pl.when(is_even())
        def _():
            split(second, first)

        @pl.when(jnp.logical_not(is_even()))
        def _():
            split(first, second)

    out = pl.pallas_call(
        kernel,
        out_shape=[bf16(rows, width)] * pairs + [bf16(block_rows, width)],
        in_specs=[VMEM] * (2 + len(far)),
        out_specs=[VMEM] * (pairs + 1),
        compiler_params=small_kernel(),
        cost_estimate=weighed(0),
        name="cut_previous_values",
    )(first_got, second_got, *far)
    return out[:pairs], out[pairs]


def clip_ids(lengths, shape, axis, block, blocks):
    position = block * shape[axis] + lax.broadcasted_iota(jnp.int32, shape, axis)
    ids, end = jnp.zeros(shape, jnp.int32), jnp.int32(0)
    for clip in range(lengths.shape[0]):
        end = end + lengths[clip]
        ids = ids + (position >= end).astype(jnp.int32)
    return jnp.where(jnp.logical_and(block >= 0, block < blocks), ids, -1)


def mask_bias(key_ids, query_ids):
    return jnp.where(key_ids == query_ids, 0.0, masked_fill).astype(jnp.float32)


def by_rows(a, b):
    return lax.dot_general(a, b, (((1,), (1,)), ((), ())), preferred_element_type=jnp.float32)


def by_columns(a, b):
    return lax.dot_general(a, b, (((0,), (0,)), ((), ())), preferred_element_type=jnp.float32)


def product(a, b):
    return jnp.dot(a, b, preferred_element_type=jnp.float32)


def masks(clip_lengths, block_rows):
    square = jax.ShapeDtypeStruct((block_rows, block_rows), jnp.float32)

    def kernel(lengths, own, past, ahead):
        block, blocks = lax.axis_index("blk"), lax.axis_size("blk")
        tall, wide = (block_rows, 1), (1, block_rows)
        key_ids, row_ids = clip_ids(lengths, tall, 0, block, blocks), clip_ids(lengths, wide, 1, block, blocks)
        own[...] = mask_bias(key_ids, row_ids)
        past[...] = mask_bias(clip_ids(lengths, tall, 0, block - 1, blocks), row_ids)
        ahead[...] = mask_bias(key_ids, clip_ids(lengths, wide, 1, block + 1, blocks))

    return pl.pallas_call(
        kernel,
        out_shape=[square] * 3,
        in_specs=[SMEM],
        out_specs=[VMEM] * 3,
        compiler_params=small_kernel(),
        cost_estimate=weighed(0),
        name="masks",
    )(clip_lengths)


def own_scores(keys, queries, chip_values, far_values, upstream, bias):
    sharers = 2 + 2 * len(far_values)
    block_rows, width = keys.shape
    rows = block_rows // sharers
    heads = width // HEAD_DIM

    def kernel(k, q, u, bias, *rest):
        values_in = [ref.at[pl.ds(2 * rows, rows)] for ref in rest[:2]]
        for ref in rest[2 : 1 + sharers // 2]:
            values_in += [ref.at[pl.ds(0, rows)], ref.at[pl.ds(rows, rows)]]
        values, stats, tops, grown_t, slopes_t = rest[1 + sharers // 2 :]
        for step in range(sharers):
            values[place(step, rows), :] = values_in[step][...]
        for head in range(heads):
            columns = pl.ds(head * HEAD_DIM, HEAD_DIM)
            scores = by_rows(k[:, columns], q[:, columns]) * exp2_scale + bias[...]
            row_max = jnp.max(scores, axis=0, keepdims=True)
            grown = jnp.exp2(scores - row_max)
            total = jnp.sum(grown, axis=0, keepdims=True)
            dchances = by_rows(values[:, columns], u[:, columns])
            offset = jnp.sum(grown * dchances, axis=0, keepdims=True) / total
            stats[pl.ds(head, 1), :] = row_max + jnp.log2(total)
            stats[pl.ds(heads + head, 1), :] = offset
            tops[pl.ds(head, 1), :] = row_max
            grown_t[head] = grown.astype(jnp.bfloat16)
            slopes_t[head] = (grown * (dchances - offset)).astype(jnp.bfloat16)

    square = bf16(heads, block_rows, block_rows)
    return pl.pallas_call(
        kernel,
        out_shape=[
            bf16(block_rows, width),
            jax.ShapeDtypeStruct((2 * heads, block_rows), jnp.float32),
            jax.ShapeDtypeStruct((heads, block_rows), jnp.float32),
            square,
            square,
        ],
        in_specs=[VMEM] * (5 + sharers // 2),
        out_specs=[VMEM] * 5,
        compiler_params=pltpu.CompilerParams(vmem_limit_bytes=12 * 2**20),
        cost_estimate=weighed(2e10),
        name="own_scores",
    )(keys, queries, upstream, bias, *chip_values, *far_values)


def own_products(keys, values, grown_t, slopes_t, next_upstream):
    block_rows, width = keys.shape
    heads = width // HEAD_DIM

    def kernel(k, v, grown_t, slopes_t, nu, summed, grown_keys, slope_keys, later):
        for head in range(heads):
            columns = pl.ds(head * HEAD_DIM, HEAD_DIM)
            key, value = k[:, columns], v[:, columns]
            both = by_columns(grown_t[head], jnp.concatenate([value, key], axis=1))
            summed[:, columns] = both[:, :HEAD_DIM]
            grown_keys[:, columns] = both[:, HEAD_DIM:]
            slope_keys[:, columns] = by_columns(slopes_t[head], key)
            later[head] = by_rows(value, nu[:, columns])

    wide = jax.ShapeDtypeStruct((block_rows, width), jnp.float32)
    return pl.pallas_call(
        kernel,
        out_shape=[wide, wide, wide, jax.ShapeDtypeStruct((heads, block_rows, block_rows), jnp.float32)],
        in_specs=[VMEM] * 5,
        out_specs=[VMEM] * 4,
        compiler_params=pltpu.CompilerParams(vmem_limit_bytes=16 * 2**20),
        cost_estimate=weighed(2e10),
        name="own_products",
    )(keys, values, grown_t, slopes_t, next_upstream)


def finish(keys, queries, upstream, first_got, second_got, next_upstream, stats, next_stats, own, previous_values):
    pairs = len(previous_values)
    block_rows, width = keys.shape
    rows = block_rows // pairs // 2
    heads = width // HEAD_DIM

    def kernel(
        k, q, u, first, second, nu, own_stats, stats,
        tops, grown_t, slopes_t, summed, grown_keys, slope_keys, later, past_bias, next_bias, *rest
    ):
        pieces = rest[:pairs]
        attended, query_grads, key_grads, value_grads = rest[pairs : pairs + 4]
        pv, factors = rest[pairs + 4 :]
        even = is_even()
        for step in range(2 * pairs):
            pv[place(step, rows), :] = pieces[step // 2][pl.ds(step % 2 * rows, rows), :]
        factors[...] = jnp.zeros(factors.shape, jnp.float32)

        past, ahead = [], []
        for head in range(heads):
            columns = pl.ds(head * HEAD_DIM, HEAD_DIM)
            query, up, past_value = q[:, columns], u[:, columns], pv[:, columns]
            past_key = jnp.where(even, second[:, columns], first[:, columns])
            own_norm, own_offset = own_stats[pl.ds(head, 1), :], own_stats[pl.ds(heads + head, 1), :]
            own_max = tops[pl.ds(head, 1), :]
            scores = by_rows(past_key, query) * exp2_scale + past_bias[...]
            row_max = jnp.maximum(own_max, jnp.max(scores, axis=0, keepdims=True))
            grown = jnp.exp2(scores - row_max)
            own_total = jnp.exp2(own_norm - row_max)
            share = 1.0 / (own_total + jnp.sum(grown, axis=0, keepdims=True))
            dchances = by_rows(past_value, up)
            offset = share * (own_offset * own_total + jnp.sum(grown * dchances, axis=0, keepdims=True))
            chances = grown * share
            dscores = (chances * (dchances - offset)).astype(jnp.bfloat16)
            factor = jnp.exp2(own_max - row_max) * share
            factors[pl.ds(head, 1), :] = factor
            factors[pl.ds(heads + head, 1), :] = factor * (offset - own_offset)
            past.append((past_key, past_value, chances.astype(jnp.bfloat16), dscores))

        for head in range(heads):
            columns = pl.ds(head * HEAD_DIM, HEAD_DIM)
            key = k[:, columns]
            query = jnp.where(even, first[:, columns], second[:, columns])
            scores = by_rows(key, query) * exp2_scale + next_bias[...]
            row_max = jnp.max(scores, axis=0, keepdims=True)
            grown = jnp.exp2(scores - row_max)
            total = jnp.sum(grown, axis=0, keepdims=True)
            dchances = later[head]
            offset = jnp.sum(grown * dchances, axis=0, keepdims=True) / total
            far_norm, far_offset = stats[pl.ds(head, 1), :], stats[pl.ds(heads + head, 1), :]
            near_norm = row_max + jnp.log2(total)
            top = jnp.maximum(far_norm, near_norm)
            far_part, near_part = jnp.exp2(far_norm - top), jnp.exp2(near_norm - top)
            whole = 1.0 / (far_part + near_part)
            offset = (far_part * far_offset + near_part * offset) * whole
            chances = grown * (jnp.exp2(row_max - top) * whole)
            dscores = (chances * (dchances - offset)).astype(jnp.bfloat16)
            weights = chances.astype(jnp.bfloat16)
            ahead.append((product(dscores, query), product(weights, nu[:, columns])))

        turned = jnp.transpose(factors[...])
        for head in range(heads):
            columns = pl.ds(head * HEAD_DIM, HEAD_DIM)
            past_key, past_value, weights, dscores = past[head]
            factor, shift = turned[:, head : head + 1], turned[:, heads + head : heads + head + 1]
            attended[:, columns] = (
                factor * summed[:, columns] + by_columns(weights, past_value)
            ).astype(jnp.bfloat16)
            query_grads[:, columns] = (
                score_scale
                * (factor * slope_keys[:, columns] - shift * grown_keys[:, columns] + by_columns(dscores, past_key))
            ).astype(jnp.bfloat16)
            wide_query = q[:, columns].astype(jnp.float32)
            scaled_query = (wide_query * factor).astype(jnp.bfloat16)
            shifted_query = (wide_query * shift).astype(jnp.bfloat16)
            scaled_up = (u[:, columns].astype(jnp.float32) * factor).astype(jnp.bfloat16)
            key_grads[:, columns] = (
                score_scale
                * (
                    product(slopes_t[head], scaled_query)
                    - product(grown_t[head], shifted_query)
                    + ahead[head][0]
                )
            ).astype(jnp.bfloat16)
            value_grads[:, columns] = (product(grown_t[head], scaled_up) + ahead[head][1]).astype(jnp.bfloat16)

    return pl.pallas_call(
        kernel,
        out_shape=[bf16(block_rows, width)] * 4,
        in_specs=[VMEM] * (17 + pairs),
        out_specs=[VMEM] * 4,
        scratch_shapes=[
            pltpu.VMEM((block_rows, width), jnp.bfloat16),
            pltpu.VMEM((HEAD_DIM, block_rows), jnp.float32),
        ],
        compiler_params=pltpu.CompilerParams(vmem_limit_bytes=20 * 2**20),
        name="finish",
    )(
        keys, queries, upstream, first_got, second_got, next_upstream, stats, next_stats, *own, *previous_values,
    )


def on_device(queries, key_states, value_states, upstream, clip_lengths):
    sharers = lax.axis_size("head")
    rows = queries.shape[0]
    pieces = cut_pieces(queries, key_states, value_states)
    pieces = [pieces[0]] + [partner_exchange(pieces[step], step) for step in range(1, sharers)]
    far_values, first, second = stack_values(pieces[0], pieces[1], upstream, rows)
    first_got, second_got = block_exchange(first, 0), block_exchange(second, 1)
    far_values = [partner_exchange(stack, 2 * pair + 2) for pair, stack in enumerate(far_values)]
    keys, query_rows, first, second = join_keys_queries(pieces, rows)
    previous, next_upstream = cut_previous_values(first_got, second_got, sharers // 2, far_values)
    first_got, second_got = block_exchange(first, 0), block_exchange(second, 1)
    previous = [partner_exchange(stack, 2 * pair) if pair else stack for pair, stack in enumerate(previous)]
    own_bias, past_bias, next_bias = masks(clip_lengths, upstream.shape[0])
    values, stats, tops, grown_t, slopes_t = own_scores(
        keys, query_rows, pieces[:2], far_values, upstream, own_bias
    )
    next_stats = to_previous(stats)
    own = own_products(keys, values, grown_t, slopes_t, next_upstream)
    own = (tops, grown_t, slopes_t, *own, past_bias, next_bias)
    return tuple(
        finish(
            keys, query_rows, upstream, first_got, second_got, next_upstream, stats, next_stats, own, previous
        )
    )


def solution(mesh):
    return jax.shard_map(
        on_device,
        mesh=mesh,
        in_specs=(
            P(("dp", "blk", "head"), None),
            P(("dp", "blk", "head"), None),
            P(("dp", "blk", "head"), None),
            P(("dp", "blk"), "head"),
            P("dp"),
        ),
        out_specs=(
            P(("dp", "blk"), "head"),
            P(("dp", "blk"), "head"),
            P(("dp", "blk"), "head"),
            P(("dp", "blk"), "head"),
        ),
        check_vma=False,
    )
```

```python
import math

import jax
import jax.numpy as jnp
from jax import lax
from jax.experimental import pallas as pl
from jax.experimental.pallas import tpu as pltpu
from jax.sharding import PartitionSpec as P

HEAD_DIM = 128
GROUP = 4

masked_fill = -1e30
score_scale = HEAD_DIM ** (-0.5)
exp2_scale = score_scale * math.log2(math.e)

VMEM = pl.BlockSpec(memory_space=pltpu.VMEM)
SMEM = pl.BlockSpec(memory_space=pltpu.SMEM)
ANY = pl.BlockSpec(memory_space=pl.ANY)


def bf16(*shape):
    return jax.ShapeDtypeStruct(shape, jnp.bfloat16)


def partner_exchange(rows, step):
    route = [(i, i ^ step) for i in range(lax.axis_size("head"))]
    return lax.ppermute(rows, "head", route)


def block_exchange(rows, parity):
    parts, blocks, sharers = lax.axis_size("dp"), lax.axis_size("blk"), lax.axis_size("head")
    route = []
    for part in range(parts):
        for block in range(blocks):
            other = block + 1 if block % 2 == parity else block - 1
            for sharer in range(sharers):
                here = (part * blocks + block) * sharers + sharer
                if 0 <= other < blocks:
                    route.append((here, (part * blocks + other) * sharers + sharer))
                else:
                    route.append((here, here ^ 1))
    return lax.ppermute(rows, ("dp", "blk", "head"), route)


def to_previous(rows):
    blocks = lax.axis_size("blk")
    return lax.ppermute(rows, "blk", [(i, i - 1) for i in range(1, blocks)])


def is_even():
    return lax.rem(lax.axis_index("blk"), 2) == 0


def place(step, size):
    owner = jnp.bitwise_xor(lax.axis_index("head"), step)
    return pl.ds(pl.multiple_of(owner * size, size), size)


def small_kernel():
    return pltpu.CompilerParams(vmem_limit_bytes=4 * 2**20)


def weighed(flops):
    return pl.CostEstimate(flops=int(flops), bytes_accessed=0, transcendentals=0)


def cut_pieces(queries, key_states, value_states):
    sharers = lax.axis_size("head")
    rows, features = queries.shape
    width = features // sharers
    heights = [(2 + sharers // 2) * rows if step < 2 else 2 * rows for step in range(sharers)]

    def kernel(q, k, v, *rest):
        pieces, sems = rest[:sharers], rest[sharers]
        copies = []

        def copy(source, target):
            copies.append(pltpu.make_async_copy(source, target, sems.at[len(copies)]))

        for step in range(sharers):
            columns = place(step, width)
            copy(k.at[:, columns], pieces[step].at[pl.ds(0, rows)])
            copy(q.at[:, columns], pieces[step].at[pl.ds(rows, rows)])
            copy(v.at[:, columns], pieces[step % 2].at[pl.ds((2 + step // 2) * rows, rows)])
        for c in copies:
            c.start()
        for c in copies:
            c.wait()

    return pl.pallas_call(
        kernel,
        out_shape=[bf16(height, width) for height in heights],
        in_specs=[ANY] * 3,
        out_specs=[VMEM] * sharers,
        scratch_shapes=[pltpu.SemaphoreType.DMA((3 * sharers,))],
        compiler_params=pltpu.CompilerParams(vmem_limit_bytes=53 * 2**20),
        name="cut_pieces",
    )(queries, key_states, value_states)


def stack_far_values(own, got, clip_lengths, rows):
    pairs = own.shape[0] // rows - 2
    width = own.shape[1]
    block_rows = 2 * pairs * rows

    def kernel(mine, theirs, lengths, own, past, ahead, *out):
        for pair in range(1, pairs):
            where = pl.ds((2 + pair) * rows, rows)
            out[pair - 1][pl.ds(0, rows), :] = mine[where, :]
            out[pair - 1][pl.ds(rows, rows), :] = theirs[where, :]
        block, blocks = lax.axis_index("blk"), lax.axis_size("blk")
        tall, wide = (block_rows, 1), (1, block_rows)
        key_ids, row_ids = clip_ids(lengths, tall, 0, block, blocks), clip_ids(lengths, wide, 1, block, blocks)
        own[...] = mask_bias(key_ids, row_ids)
        past[...] = mask_bias(clip_ids(lengths, tall, 0, block - 1, blocks), row_ids)
        ahead[...] = mask_bias(key_ids, clip_ids(lengths, wide, 1, block + 1, blocks))

    out = pl.pallas_call(
        kernel,
        out_shape=[jax.ShapeDtypeStruct((block_rows, block_rows), jnp.float32)] * 3
        + [bf16(2 * rows, width)] * (pairs - 1),
        in_specs=[VMEM] * 2 + [SMEM],
        out_specs=[VMEM] * (pairs + 2),
        compiler_params=small_kernel(),
        cost_estimate=weighed(5e9),
        name="stack_far_values",
    )(own, got, clip_lengths)
    return out[3:], out[:3]


def stack_values(own, got, upstream, rows):
    pairs = own.shape[0] // rows - 2
    width = own.shape[1]
    block_rows = upstream.shape[0]

    def kernel(mine, theirs, u, first, second):
        def spread(forward, backward):
            for pair in range(pairs):
                where = pl.ds((2 + pair) * rows, rows)
                forward[pl.ds(2 * pair * rows, rows), :] = mine[where, :]
                forward[pl.ds((2 * pair + 1) * rows, rows), :] = theirs[where, :]
            backward[...] = u[...]

        @pl.when(is_even())
        def _():
            spread(first, second)

        @pl.when(jnp.logical_not(is_even()))
        def _():
            spread(second, first)

    return pl.pallas_call(
        kernel,
        out_shape=[bf16(block_rows, width)] * 2,
        in_specs=[VMEM] * 3,
        out_specs=[VMEM] * 2,
        compiler_params=small_kernel(),
        cost_estimate=weighed(0),
        name="stack_values",
    )(own, got, upstream)


def join_keys_queries(pieces, rows):
    sharers = len(pieces)
    width = pieces[0].shape[1]
    block_rows = rows * sharers

    def kernel(*refs):
        pieces_in = refs[:sharers]
        keys, queries, first, second = refs[sharers:]
        for step in range(sharers):
            where = place(step, rows)
            keys[where, :] = pieces_in[step][pl.ds(0, rows), :]
            queries[where, :] = pieces_in[step][pl.ds(rows, rows), :]

        @pl.when(is_even())
        def _():
            first[...] = keys[...]
            second[...] = queries[...]

        @pl.when(jnp.logical_not(is_even()))
        def _():
            first[...] = queries[...]
            second[...] = keys[...]

    return pl.pallas_call(
        kernel,
        out_shape=[bf16(block_rows, width)] * 4,
        in_specs=[VMEM] * sharers,
        out_specs=[VMEM] * 4,
        compiler_params=small_kernel(),
        cost_estimate=weighed(0),
        name="join_keys_queries",
    )(*pieces)


def cut_previous_values(first_got, second_got, pairs):
    block_rows, width = first_got.shape
    rows = block_rows // pairs

    def kernel(first, second, *out):
        def split(forward, backward):
            for pair in range(pairs):
                out[pair][...] = forward[pl.ds(pair * rows, rows), :]
            out[pairs][...] = backward[...]

        @pl.when(is_even())
        def _():
            split(second, first)

        @pl.when(jnp.logical_not(is_even()))
        def _():
            split(first, second)

    out = pl.pallas_call(
        kernel,
        out_shape=[bf16(rows, width)] * pairs + [bf16(block_rows, width)],
        in_specs=[VMEM] * 2,
        out_specs=[VMEM] * (pairs + 1),
        compiler_params=small_kernel(),
        cost_estimate=weighed(0),
        name="cut_previous_values",
    )(first_got, second_got)
    return out[:pairs], out[pairs]


def clip_ids(lengths, shape, axis, block, blocks):
    position = block * shape[axis] + lax.broadcasted_iota(jnp.int32, shape, axis)
    ids, end = jnp.zeros(shape, jnp.int32), jnp.int32(0)
    for clip in range(lengths.shape[0]):
        end = end + lengths[clip]
        ids = ids + (position >= end).astype(jnp.int32)
    return jnp.where(jnp.logical_and(block >= 0, block < blocks), ids, -1)


def mask_bias(key_ids, query_ids):
    return jnp.where(key_ids == query_ids, 0.0, masked_fill).astype(jnp.float32)


def by_rows(a, b):
    return lax.dot_general(a, b, (((1,), (1,)), ((), ())), preferred_element_type=jnp.float32)


def by_columns(a, b):
    return lax.dot_general(a, b, (((0,), (0,)), ((), ())), preferred_element_type=jnp.float32)


def product(a, b):
    return jnp.dot(a, b, preferred_element_type=jnp.float32)


def own_scores(keys, queries, chip_values, far_values, upstream, bias, after):
    sharers = 2 + 2 * len(far_values)
    block_rows, width = keys.shape
    rows = block_rows // sharers
    heads = width // HEAD_DIM

    def kernel(k, q, u, bias, _, *rest):
        values_in = [ref.at[pl.ds(2 * rows, rows)] for ref in rest[:2]]
        for ref in rest[2 : 1 + sharers // 2]:
            values_in += [ref.at[pl.ds(0, rows)], ref.at[pl.ds(rows, rows)]]
        values, stats, tops, grown_t, slopes_t = rest[1 + sharers // 2 :]
        for step in range(sharers):
            values[place(step, rows), :] = values_in[step][...]
        for head in range(heads):
            columns = pl.ds(head * HEAD_DIM, HEAD_DIM)
            scores = by_rows(k[:, columns], q[:, columns]) * exp2_scale + bias[...]
            row_max = jnp.max(scores, axis=0, keepdims=True)
            grown = jnp.exp2(scores - row_max)
            total = jnp.sum(grown, axis=0, keepdims=True)
            dchances = by_rows(values[:, columns], u[:, columns])
            offset = jnp.sum(grown * dchances, axis=0, keepdims=True) / total
            stats[pl.ds(head, 1), :] = row_max + jnp.log2(total)
            stats[pl.ds(heads + head, 1), :] = offset
            tops[pl.ds(head, 1), :] = row_max
            grown_t[head] = grown.astype(jnp.bfloat16)
            slopes_t[head] = (grown * (dchances - offset)).astype(jnp.bfloat16)

    square = bf16(heads, block_rows, block_rows)
    return pl.pallas_call(
        kernel,
        out_shape=[
            bf16(block_rows, width),
            jax.ShapeDtypeStruct((2 * heads, block_rows), jnp.float32),
            jax.ShapeDtypeStruct((heads, block_rows), jnp.float32),
            square,
            square,
        ],
        in_specs=[VMEM] * (6 + sharers // 2),
        out_specs=[VMEM] * 5,
        compiler_params=pltpu.CompilerParams(vmem_limit_bytes=12 * 2**20),
        cost_estimate=weighed(0),
        name="own_scores",
    )(keys, queries, upstream, bias, after, *chip_values, *far_values)


def own_products(keys, values, grown_t, slopes_t, next_upstream):
    block_rows, width = keys.shape
    heads = width // HEAD_DIM

    def kernel(k, v, grown_t, slopes_t, nu, summed, grown_keys, slope_keys, later):
        for head in range(heads):
            columns = pl.ds(head * HEAD_DIM, HEAD_DIM)
            key, value = k[:, columns], v[:, columns]
            both = by_columns(grown_t[head], jnp.concatenate([value, key], axis=1))
            summed[:, columns] = both[:, :HEAD_DIM]
            grown_keys[:, columns] = both[:, HEAD_DIM:]
            slope_keys[:, columns] = by_columns(slopes_t[head], key)
            later[head] = by_rows(value, nu[:, columns])

    wide = jax.ShapeDtypeStruct((block_rows, width), jnp.float32)
    return pl.pallas_call(
        kernel,
        out_shape=[wide, wide, wide, jax.ShapeDtypeStruct((heads, block_rows, block_rows), jnp.float32)],
        in_specs=[VMEM] * 5,
        out_specs=[VMEM] * 4,
        compiler_params=pltpu.CompilerParams(vmem_limit_bytes=16 * 2**20),
        cost_estimate=weighed(2e10),
        name="own_products",
    )(keys, values, grown_t, slopes_t, next_upstream)


def past_keys(queries, upstream, first_got, second_got, stats, own, previous_values, past_bias):
    pairs = len(previous_values)
    block_rows, width = queries.shape
    rows = block_rows // pairs // 2
    heads = width // HEAD_DIM

    def kernel(
        q, u, first, second, own_stats, tops, grown_t, slopes_t, summed, grown_keys, slope_keys, past_bias, *rest
    ):
        pieces = rest[:pairs]
        attended, query_grads, key_part, value_part, pv, factors = rest[pairs:]
        even = is_even()
        for step in range(2 * pairs):
            pv[place(step, rows), :] = pieces[step // 2][pl.ds(step % 2 * rows, rows), :]
        factors[...] = jnp.zeros(factors.shape, jnp.float32)

        for start in range(0, heads, GROUP):
            group = range(start, min(start + GROUP, heads))
            cols = [pl.ds(head * HEAD_DIM, HEAD_DIM) for head in group]
            keys = [jnp.where(even, second[:, c], first[:, c]) for c in cols]
            scores = [by_rows(key, q[:, c]) * exp2_scale + past_bias[...] for key, c in zip(keys, cols)]
            maxes = [
                jnp.maximum(tops[pl.ds(head, 1), :], jnp.max(x, axis=0, keepdims=True)) for head, x in zip(group, scores)
            ]
            grown = [jnp.exp2(x - m) for x, m in zip(scores, maxes)]
            own = [jnp.exp2(own_stats[pl.ds(head, 1), :] - m) for head, m in zip(group, maxes)]
            shares = [1.0 / (o + jnp.sum(x, axis=0, keepdims=True)) for o, x in zip(own, grown)]
            dchances = [by_rows(pv[:, c], u[:, c]) for c in cols]
            offsets = [
                y * (own_stats[pl.ds(heads + head, 1), :] * o + jnp.sum(x * d, axis=0, keepdims=True))
                for head, o, x, y, d in zip(group, own, grown, shares, dchances)
            ]
            for n, head in enumerate(group):
                factor = jnp.exp2(tops[pl.ds(head, 1), :] - maxes[n]) * shares[n]
                factors[pl.ds(head, 1), :] = factor
                factors[pl.ds(heads + head, 1), :] = factor * (offsets[n] - own_stats[pl.ds(heads + head, 1), :])
            chances = [x * y for x, y in zip(grown, shares)]
            weights = [x.astype(jnp.bfloat16) for x in chances]
            dscores = [(x * (d - o)).astype(jnp.bfloat16) for x, d, o in zip(chances, dchances, offsets)]
            turned = jnp.transpose(factors[...])
            for n, (head, c) in enumerate(zip(group, cols)):
                factor, shift = turned[:, head : head + 1], turned[:, heads + head : heads + head + 1]
                attended[:, c] = (factor * summed[:, c] + by_columns(weights[n], pv[:, c])).astype(jnp.bfloat16)
                query_grads[:, c] = (
                    score_scale * (factor * slope_keys[:, c] - shift * grown_keys[:, c] + by_columns(dscores[n], keys[n]))
                ).astype(jnp.bfloat16)
                wide_query = q[:, c].astype(jnp.float32)
                scaled_query = (wide_query * factor).astype(jnp.bfloat16)
                shifted_query = (wide_query * shift).astype(jnp.bfloat16)
                scaled_up = (u[:, c].astype(jnp.float32) * factor).astype(jnp.bfloat16)
                key_part[:, c] = product(slopes_t[head], scaled_query) - product(grown_t[head], shifted_query)
                value_part[:, c] = product(grown_t[head], scaled_up)

    wide = jax.ShapeDtypeStruct((block_rows, width), jnp.float32)
    return pl.pallas_call(
        kernel,
        out_shape=[bf16(block_rows, width)] * 2 + [wide] * 2,
        in_specs=[VMEM] * (12 + pairs),
        out_specs=[VMEM] * 4,
        scratch_shapes=[
            pltpu.VMEM((block_rows, width), jnp.bfloat16),
            pltpu.VMEM((HEAD_DIM, block_rows), jnp.float32),
        ],
        compiler_params=pltpu.CompilerParams(vmem_limit_bytes=20 * 2**20),
        cost_estimate=weighed(0),
        name="past_keys",
    )(queries, upstream, first_got, second_got, stats, *own, past_bias, *previous_values)


def next_rows(keys, first_got, second_got, next_upstream, next_stats, later, next_bias, done, parts):
    block_rows, width = keys.shape
    heads = width // HEAD_DIM

    def kernel(k, first, second, nu, stats, later, next_bias, attended, query_grads, key_part, value_part, *rest):
        outs, (key_grads, value_grads, sems) = rest[:4], rest[4:]
        copies = [pltpu.make_async_copy(source, outs[i], sems.at[i]) for i, source in enumerate((attended, query_grads))]
        for c in copies:
            c.start()
        even = is_even()
        for start in range(0, heads, GROUP):
            group = range(start, min(start + GROUP, heads))
            cols = [pl.ds(head * HEAD_DIM, HEAD_DIM) for head in group]
            queries = [jnp.where(even, first[:, c], second[:, c]) for c in cols]
            scores = [by_rows(k[:, c], query) * exp2_scale + next_bias[...] for c, query in zip(cols, queries)]
            maxes = [jnp.max(x, axis=0, keepdims=True) for x in scores]
            grown = [jnp.exp2(x - m) for x, m in zip(scores, maxes)]
            totals = [jnp.sum(x, axis=0, keepdims=True) for x in grown]
            offsets = [
                jnp.sum(x * later[head], axis=0, keepdims=True) / total
                for x, head, total in zip(grown, group, totals)
            ]
            scales = []
            for n, head in enumerate(group):
                far_norm, far_offset = stats[pl.ds(head, 1), :], stats[pl.ds(heads + head, 1), :]
                near_norm = maxes[n] + jnp.log2(totals[n])
                top = jnp.maximum(far_norm, near_norm)
                far_part, near_part = jnp.exp2(far_norm - top), jnp.exp2(near_norm - top)
                whole = 1.0 / (far_part + near_part)
                offsets[n] = (far_part * far_offset + near_part * offsets[n]) * whole
                scales.append(jnp.exp2(maxes[n] - top) * whole)
            chances = [x * y for x, y in zip(grown, scales)]
            weights = [x.astype(jnp.bfloat16) for x in chances]
            dscores = [
                (x * (later[head] - offset)).astype(jnp.bfloat16)
                for x, head, offset in zip(chances, group, offsets)
            ]
            for n, c in enumerate(cols):
                key_grads[:, c] = (score_scale * (key_part[:, c] + product(dscores[n], queries[n]))).astype(jnp.bfloat16)
                value_grads[:, c] = (value_part[:, c] + product(weights[n], nu[:, c])).astype(jnp.bfloat16)
            wide = pl.ds(start * HEAD_DIM, len(group) * HEAD_DIM)
            for i, source in ((2, key_grads), (3, value_grads)):
                copies.append(pltpu.make_async_copy(source.at[:, wide], outs[i].at[:, wide], sems.at[len(copies)]))
                copies[-1].start()
        for c in copies:
            c.wait()

    return pl.pallas_call(
        kernel,
        out_shape=[bf16(block_rows, width)] * 4,
        in_specs=[VMEM] * 11,
        out_specs=[ANY] * 4,
        scratch_shapes=[pltpu.VMEM((block_rows, width), jnp.bfloat16)] * 2
        + [pltpu.SemaphoreType.DMA((2 + 2 * heads,))],
        compiler_params=pltpu.CompilerParams(vmem_limit_bytes=16 * 2**20),
        name="next_rows",
    )(keys, first_got, second_got, next_upstream, next_stats, later, next_bias, *done, *parts)


def on_device(queries, key_states, value_states, upstream, clip_lengths):
    sharers = lax.axis_size("head")
    rows = queries.shape[0]
    pieces = cut_pieces(queries, key_states, value_states)
    pieces = [pieces[0]] + [partner_exchange(pieces[step], step) for step in range(1, sharers)]
    first, second = stack_values(pieces[0], pieces[1], upstream, rows)
    first_got, second_got = block_exchange(first, 0), block_exchange(second, 1)
    far_values, (own_bias, past_bias, next_bias) = stack_far_values(pieces[0], pieces[1], clip_lengths, rows)
    far_values = [partner_exchange(stack, 2 * pair + 2) for pair, stack in enumerate(far_values)]
    keys, query_rows, first, second = join_keys_queries(pieces, rows)
    previous, next_upstream = cut_previous_values(first_got, second_got, sharers // 2)
    first_got, second_got = block_exchange(first, 0), block_exchange(second, 1)
    previous = [partner_exchange(stack, 2 * pair) if pair else stack for pair, stack in enumerate(previous)]
    values, stats, tops, grown_t, slopes_t = own_scores(
        keys, query_rows, pieces[:2], far_values, upstream, own_bias, next_upstream
    )
    next_stats = to_previous(stats)
    summed, grown_keys, slope_keys, later = own_products(keys, values, grown_t, slopes_t, next_upstream)
    own = (tops, grown_t, slopes_t, summed, grown_keys, slope_keys)
    attended, query_grads, key_part, value_part = past_keys(
        query_rows, upstream, first_got, second_got, stats, own, previous, past_bias
    )
    return tuple(
        next_rows(
            keys, first_got, second_got, next_upstream, next_stats, later, next_bias,
            (attended, query_grads), (key_part, value_part),
        )
    )


def solution(mesh):
    return jax.shard_map(
        on_device,
        mesh=mesh,
        in_specs=(
            P(("dp", "blk", "head"), None),
            P(("dp", "blk", "head"), None),
            P(("dp", "blk", "head"), None),
            P(("dp", "blk"), "head"),
            P("dp"),
        ),
        out_specs=(
            P(("dp", "blk"), "head"),
            P(("dp", "blk"), "head"),
            P(("dp", "blk"), "head"),
            P(("dp", "blk"), "head"),
        ),
        check_vma=False,
    )
```

```python
import math

import jax
import jax.numpy as jnp
from jax import lax
from jax.experimental import pallas as pl
from jax.experimental.pallas import tpu as pltpu
from jax.sharding import PartitionSpec as P

HEAD_DIM = 128
GROUP = 4
PAIR = 2

masked_fill = -1e30
score_scale = HEAD_DIM ** (-0.5)
exp2_scale = score_scale * math.log2(math.e)

VMEM = pl.BlockSpec(memory_space=pltpu.VMEM)
SMEM = pl.BlockSpec(memory_space=pltpu.SMEM)
ANY = pl.BlockSpec(memory_space=pl.ANY)


def bf16(*shape):
    return jax.ShapeDtypeStruct(shape, jnp.bfloat16)


def partner_exchange(rows, step):
    route = [(i, i ^ step) for i in range(lax.axis_size("head"))]
    return lax.ppermute(rows, "head", route)


def block_exchange(rows, parity):
    parts, blocks, sharers = lax.axis_size("dp"), lax.axis_size("blk"), lax.axis_size("head")
    route = []
    for part in range(parts):
        for block in range(blocks):
            other = block + 1 if block % 2 == parity else block - 1
            for sharer in range(sharers):
                here = (part * blocks + block) * sharers + sharer
                if 0 <= other < blocks:
                    route.append((here, (part * blocks + other) * sharers + sharer))
                else:
                    route.append((here, here ^ 1))
    return lax.ppermute(rows, ("dp", "blk", "head"), route)


def is_even():
    return lax.rem(lax.axis_index("blk"), 2) == 0


def place(step, size):
    owner = jnp.bitwise_xor(lax.axis_index("head"), step)
    return pl.ds(pl.multiple_of(owner * size, size), size)


def small_kernel():
    return pltpu.CompilerParams(vmem_limit_bytes=4 * 2**20)


def weighed(flops):
    return pl.CostEstimate(flops=int(flops), bytes_accessed=0, transcendentals=0)


def cut_pieces(queries, key_states, value_states):
    sharers = lax.axis_size("head")
    rows, features = queries.shape
    width = features // sharers
    heights = [(2 + sharers // 2) * rows if step < 2 else 2 * rows for step in range(sharers)]

    def kernel(q, k, v, *rest):
        pieces, sems = rest[:sharers], rest[sharers]
        copies = []

        def copy(source, target):
            copies.append(pltpu.make_async_copy(source, target, sems.at[len(copies)]))

        for step in range(sharers):
            columns = place(step, width)
            copy(k.at[:, columns], pieces[step].at[pl.ds(0, rows)])
            copy(q.at[:, columns], pieces[step].at[pl.ds(rows, rows)])
            copy(v.at[:, columns], pieces[step % 2].at[pl.ds((2 + step // 2) * rows, rows)])
        for c in copies:
            c.start()
        for c in copies:
            c.wait()

    return pl.pallas_call(
        kernel,
        out_shape=[bf16(height, width) for height in heights],
        in_specs=[ANY] * 3,
        out_specs=[VMEM] * sharers,
        scratch_shapes=[pltpu.SemaphoreType.DMA((3 * sharers,))],
        compiler_params=pltpu.CompilerParams(vmem_limit_bytes=53 * 2**20),
        name="cut_pieces",
    )(queries, key_states, value_states)


def stack_far_values(own, got, clip_lengths, rows):
    pairs = own.shape[0] // rows - 2
    width = own.shape[1]
    block_rows = 2 * pairs * rows

    def kernel(mine, theirs, lengths, own, past, ahead, *out):
        for pair in range(1, pairs):
            where = pl.ds((2 + pair) * rows, rows)
            out[pair - 1][pl.ds(0, rows), :] = mine[where, :]
            out[pair - 1][pl.ds(rows, rows), :] = theirs[where, :]
        block, blocks = lax.axis_index("blk"), lax.axis_size("blk")
        tall, wide = (block_rows, 1), (1, block_rows)
        key_ids, row_ids = clip_ids(lengths, tall, 0, block, blocks), clip_ids(lengths, wide, 1, block, blocks)
        own[...] = mask_bias(key_ids, row_ids)
        past[...] = mask_bias(clip_ids(lengths, tall, 0, block - 1, blocks), row_ids)
        ahead[...] = mask_bias(key_ids, clip_ids(lengths, wide, 1, block + 1, blocks))

    out = pl.pallas_call(
        kernel,
        out_shape=[jax.ShapeDtypeStruct((block_rows, block_rows), jnp.float32)] * 3
        + [bf16(2 * rows, width)] * (pairs - 1),
        in_specs=[VMEM] * 2 + [SMEM],
        out_specs=[VMEM] * (pairs + 2),
        compiler_params=small_kernel(),
        cost_estimate=weighed(5e9),
        name="stack_far_values",
    )(own, got, clip_lengths)
    return out[3:], out[:3]


def stack_values(own, got, upstream, rows):
    pairs = own.shape[0] // rows - 2
    width = own.shape[1]
    block_rows = upstream.shape[0]

    def kernel(mine, theirs, u, first, second):
        def spread(forward, backward):
            for pair in range(pairs):
                where = pl.ds((2 + pair) * rows, rows)
                forward[pl.ds(2 * pair * rows, rows), :] = mine[where, :]
                forward[pl.ds((2 * pair + 1) * rows, rows), :] = theirs[where, :]
            backward[...] = u[...]

        @pl.when(is_even())
        def _():
            spread(first, second)

        @pl.when(jnp.logical_not(is_even()))
        def _():
            spread(second, first)

    return pl.pallas_call(
        kernel,
        out_shape=[bf16(block_rows, width)] * 2,
        in_specs=[VMEM] * 3,
        out_specs=[VMEM] * 2,
        compiler_params=small_kernel(),
        cost_estimate=weighed(0),
        name="stack_values",
    )(own, got, upstream)


def join_keys_queries(pieces, rows):
    sharers = len(pieces)
    width = pieces[0].shape[1]
    block_rows = rows * sharers

    def kernel(*refs):
        pieces_in = refs[:sharers]
        keys, queries, first, second = refs[sharers:]
        for step in range(sharers):
            where = place(step, rows)
            keys[where, :] = pieces_in[step][pl.ds(0, rows), :]
            queries[where, :] = pieces_in[step][pl.ds(rows, rows), :]

        @pl.when(is_even())
        def _():
            first[...] = keys[...]
            second[...] = queries[...]

        @pl.when(jnp.logical_not(is_even()))
        def _():
            first[...] = queries[...]
            second[...] = keys[...]

    return pl.pallas_call(
        kernel,
        out_shape=[bf16(block_rows, width)] * 4,
        in_specs=[VMEM] * sharers,
        out_specs=[VMEM] * 4,
        compiler_params=small_kernel(),
        cost_estimate=weighed(0),
        name="join_keys_queries",
    )(*pieces)


def cut_previous_values(first_got, second_got, pairs):
    block_rows, width = first_got.shape
    rows = block_rows // pairs

    def kernel(first, second, *out):
        def split(forward, backward):
            for pair in range(pairs):
                out[pair][...] = forward[pl.ds(pair * rows, rows), :]
            out[pairs][...] = backward[...]

        @pl.when(is_even())
        def _():
            split(second, first)

        @pl.when(jnp.logical_not(is_even()))
        def _():
            split(first, second)

    out = pl.pallas_call(
        kernel,
        out_shape=[bf16(rows, width)] * pairs + [bf16(block_rows, width)],
        in_specs=[VMEM] * 2,
        out_specs=[VMEM] * (pairs + 1),
        compiler_params=small_kernel(),
        cost_estimate=weighed(0),
        name="cut_previous_values",
    )(first_got, second_got)
    return out[:pairs], out[pairs]


def clip_ids(lengths, shape, axis, block, blocks):
    position = block * shape[axis] + lax.broadcasted_iota(jnp.int32, shape, axis)
    ids, end = jnp.zeros(shape, jnp.int32), jnp.int32(0)
    for clip in range(lengths.shape[0]):
        end = end + lengths[clip]
        ids = ids + (position >= end).astype(jnp.int32)
    return jnp.where(jnp.logical_and(block >= 0, block < blocks), ids, -1)


def mask_bias(key_ids, query_ids):
    return jnp.where(key_ids == query_ids, 0.0, masked_fill).astype(jnp.float32)


def by_rows(a, b):
    return lax.dot_general(a, b, (((1,), (1,)), ((), ())), preferred_element_type=jnp.float32)


def by_columns(a, b):
    return lax.dot_general(a, b, (((0,), (0,)), ((), ())), preferred_element_type=jnp.float32)


def product(a, b):
    return jnp.dot(a, b, preferred_element_type=jnp.float32)


def own_scores(keys, queries, chip_values, far_values, upstream, bias, after):
    sharers = 2 + 2 * len(far_values)
    block_rows, width = keys.shape
    rows = block_rows // sharers
    heads = width // HEAD_DIM

    def kernel(k, q, u, bias, _, *rest):
        values_in = [ref.at[pl.ds(2 * rows, rows)] for ref in rest[:2]]
        for ref in rest[2 : 1 + sharers // 2]:
            values_in += [ref.at[pl.ds(0, rows)], ref.at[pl.ds(rows, rows)]]
        values, stats, tops, grown_t, slopes_t = rest[1 + sharers // 2 :]
        for step in range(sharers):
            values[place(step, rows), :] = values_in[step][...]
        for start in range(0, heads, GROUP):
            group = range(start, min(start + GROUP, heads))
            cols = [pl.ds(head * HEAD_DIM, HEAD_DIM) for head in group]
            scores = [by_rows(k[:, c], q[:, c]) * exp2_scale + bias[...] for c in cols]
            maxes = [jnp.max(x, axis=0, keepdims=True) for x in scores]
            grown = [jnp.exp2(x - m) for x, m in zip(scores, maxes)]
            totals = [jnp.sum(x, axis=0, keepdims=True) for x in grown]
            dchances = [by_rows(values[:, c], u[:, c]) for c in cols]
            offsets = [
                jnp.sum(x * d, axis=0, keepdims=True) / total for x, d, total in zip(grown, dchances, totals)
            ]
            for n, head in enumerate(group):
                stats[pl.ds(head, 1), :] = maxes[n] + jnp.log2(totals[n])
                stats[pl.ds(heads + head, 1), :] = offsets[n]
                tops[pl.ds(head, 1), :] = maxes[n]
                grown_t[head] = grown[n].astype(jnp.bfloat16)
                slopes_t[head] = (grown[n] * (dchances[n] - offsets[n])).astype(jnp.bfloat16)

    square = bf16(heads, block_rows, block_rows)
    return pl.pallas_call(
        kernel,
        out_shape=[
            bf16(block_rows, width),
            jax.ShapeDtypeStruct((2 * heads, block_rows), jnp.float32),
            jax.ShapeDtypeStruct((heads, block_rows), jnp.float32),
            square,
            square,
        ],
        in_specs=[VMEM] * (6 + sharers // 2),
        out_specs=[VMEM] * 5,
        compiler_params=pltpu.CompilerParams(vmem_limit_bytes=12 * 2**20),
        cost_estimate=weighed(2e10),
        name="own_scores",
    )(keys, queries, upstream, bias, after, *chip_values, *far_values)


def own_products(keys, queries, upstream, values, grown_t, slopes_t, next_upstream):
    block_rows, width = keys.shape
    heads = width // HEAD_DIM

    def kernel(k, q, u, v, grown_t, slopes_t, nu, sums, slope_keys, query_t, up_t, later):
        for head in range(heads):
            columns = pl.ds(head * HEAD_DIM, HEAD_DIM)
            key, value = k[:, columns], v[:, columns]
            sums[head] = by_columns(jnp.concatenate([value, key], axis=1), grown_t[head])
            slope_keys[head] = by_columns(key, slopes_t[head])
            query_t[head] = jnp.transpose(q[:, columns]).astype(jnp.float32)
            up_t[head] = jnp.transpose(u[:, columns]).astype(jnp.float32)
            later[head] = by_rows(value, nu[:, columns])

    def turned(tall):
        return jax.ShapeDtypeStruct((heads, tall, block_rows), jnp.float32)

    return pl.pallas_call(
        kernel,
        out_shape=[turned(2 * HEAD_DIM)] + [turned(HEAD_DIM)] * 3 + [turned(block_rows)],
        in_specs=[VMEM] * 7,
        out_specs=[VMEM] * 5,
        compiler_params=pltpu.CompilerParams(vmem_limit_bytes=16 * 2**20),
        cost_estimate=weighed(0),
        name="own_products",
    )(keys, queries, upstream, values, grown_t, slopes_t, next_upstream)


def past_dchances(upstream, previous_values):
    pairs = len(previous_values)
    block_rows, width = upstream.shape
    rows = block_rows // pairs // 2
    heads = width // HEAD_DIM

    def kernel(u, *rest):
        pieces, (values, dchances) = rest[:pairs], rest[pairs:]
        for step in range(2 * pairs):
            values[place(step, rows), :] = pieces[step // 2][pl.ds(step % 2 * rows, rows), :]
        for head in range(heads):
            columns = pl.ds(head * HEAD_DIM, HEAD_DIM)
            dchances[head] = by_rows(values[:, columns], u[:, columns])

    return pl.pallas_call(
        kernel,
        out_shape=[bf16(block_rows, width), jax.ShapeDtypeStruct((heads, block_rows, block_rows), jnp.float32)],
        in_specs=[VMEM] * (1 + pairs),
        out_specs=[VMEM] * 2,
        compiler_params=small_kernel(),
        cost_estimate=weighed(0),
        name="past_dchances",
    )(upstream, *previous_values)


def past_keys(queries, first_got, second_got, stats, tops, own, past_values, dchances, past_bias):
    block_rows, width = queries.shape
    heads = width // HEAD_DIM

    def kernel(
        q, first, second, own_stats, tops, sums, slope_keys, query_t, up_t, pv, dchances, past_bias,
        attended, query_grads, scaled_query, shifted_query, scaled_up
    ):
        even = is_even()
        for start in range(0, heads, GROUP):
            group = range(start, min(start + GROUP, heads))
            cols = [pl.ds(head * HEAD_DIM, HEAD_DIM) for head in group]
            keys = [jnp.where(even, second[:, c], first[:, c]) for c in cols]
            scores = [by_rows(key, q[:, c]) * exp2_scale + past_bias[...] for key, c in zip(keys, cols)]
            maxes = [
                jnp.maximum(tops[pl.ds(head, 1), :], jnp.max(x, axis=0, keepdims=True)) for head, x in zip(group, scores)
            ]
            grown = [jnp.exp2(x - m) for x, m in zip(scores, maxes)]
            own = [jnp.exp2(own_stats[pl.ds(head, 1), :] - m) for head, m in zip(group, maxes)]
            shares = [1.0 / (o + jnp.sum(x, axis=0, keepdims=True)) for o, x in zip(own, grown)]
            offsets = [
                y * (own_stats[pl.ds(heads + head, 1), :] * o + jnp.sum(x * dchances[head], axis=0, keepdims=True))
                for head, o, x, y in zip(group, own, grown, shares)
            ]
            factors = [jnp.exp2(tops[pl.ds(head, 1), :] - m) * y for head, m, y in zip(group, maxes, shares)]
            shifts = [
                f * (o - own_stats[pl.ds(heads + head, 1), :]) for head, f, o in zip(group, factors, offsets)
            ]
            chances = [x * y for x, y in zip(grown, shares)]
            weights = [x.astype(jnp.bfloat16) for x in chances]
            dscores = [(x * (dchances[head] - o)).astype(jnp.bfloat16) for x, head, o in zip(chances, group, offsets)]
            for n, (head, c) in enumerate(zip(group, cols)):
                factor, shift = factors[n], shifts[n]
                attended_t = factor * sums[head, :HEAD_DIM] + by_columns(pv[:, c], weights[n])
                attended[:, c] = jnp.transpose(attended_t.astype(jnp.bfloat16))
                grads_t = (
                    factor * slope_keys[head] - shift * sums[head, HEAD_DIM:] + by_columns(keys[n], dscores[n])
                )
                query_grads[:, c] = jnp.transpose((score_scale * grads_t).astype(jnp.bfloat16))
                scaled_query[head] = (query_t[head] * factor).astype(jnp.bfloat16)
                shifted_query[head] = (query_t[head] * -shift).astype(jnp.bfloat16)
                scaled_up[head] = (up_t[head] * factor).astype(jnp.bfloat16)

    return pl.pallas_call(
        kernel,
        out_shape=[bf16(block_rows, width)] * 2 + [bf16(heads, HEAD_DIM, block_rows)] * 3,
        in_specs=[VMEM] * 12,
        out_specs=[VMEM] * 5,
        compiler_params=pltpu.CompilerParams(vmem_limit_bytes=20 * 2**20),
        cost_estimate=weighed(0),
        name="past_keys",
    )(queries, first_got, second_got, stats, tops, *own, past_values, dchances, past_bias)


def next_rows(
    keys, first_got, second_got, next_upstream, first_stats, second_stats, later, next_bias, grown_t, slopes_t,
    done, scaled
):
    block_rows, width = keys.shape
    heads = width // HEAD_DIM

    def kernel(
        k, first, second, nu, first_stats, second_stats, later, next_bias, grown_t, slopes_t,
        attended, query_grads, scaled_query, shifted_query, scaled_up, *rest
    ):
        outs, (key_grads, value_grads, sems) = rest[:4], rest[4:]
        copies = [pltpu.make_async_copy(source, outs[i], sems.at[i]) for i, source in enumerate((attended, query_grads))]
        for c in copies:
            c.start()
        even = is_even()
        stats = jnp.where(even, first_stats[...], second_stats[...])
        for start in range(0, heads, PAIR):
            group = range(start, min(start + PAIR, heads))
            cols = [pl.ds(head * HEAD_DIM, HEAD_DIM) for head in group]
            queries = [jnp.where(even, first[:, c], second[:, c]) for c in cols]
            scores = [by_rows(k[:, c], query) * exp2_scale + next_bias[...] for c, query in zip(cols, queries)]
            mixed = [
                by_rows(grown_t[head], jnp.concatenate([scaled_up[head], shifted_query[head]], axis=0)) for head in group
            ]
            sloped = [by_rows(slopes_t[head], scaled_query[head]) for head in group]
            far = [stats[head : head + 1] for head in group]
            maxes = [jnp.maximum(f, jnp.max(x, axis=0, keepdims=True)) for f, x in zip(far, scores)]
            grown = [jnp.exp2(x - m) for x, m in zip(scores, maxes)]
            far = [jnp.exp2(f - m) for f, m in zip(far, maxes)]
            shares = [1.0 / (f + jnp.sum(x, axis=0, keepdims=True)) for f, x in zip(far, grown)]
            offsets = [
                y * (stats[heads + head : heads + head + 1] * f + jnp.sum(x * later[head], axis=0, keepdims=True))
                for head, f, x, y in zip(group, far, grown, shares)
            ]
            chances = [x * y for x, y in zip(grown, shares)]
            weights = [x.astype(jnp.bfloat16) for x in chances]
            dscores = [
                (x * (later[head] - offset)).astype(jnp.bfloat16)
                for x, head, offset in zip(chances, group, offsets)
            ]
            for n, (head, c) in enumerate(zip(group, cols)):
                value_grads[:, c] = (mixed[n][:, :HEAD_DIM] + product(weights[n], nu[:, c])).astype(jnp.bfloat16)
                key_grads[:, c] = (
                    score_scale
                    * (mixed[n][:, HEAD_DIM:] + sloped[n] + product(dscores[n], queries[n]))
                ).astype(jnp.bfloat16)
            wide = pl.ds(start * HEAD_DIM, len(group) * HEAD_DIM)
            for i, source in ((2, key_grads), (3, value_grads)):
                copies.append(pltpu.make_async_copy(source.at[:, wide], outs[i].at[:, wide], sems.at[len(copies)]))
                copies[-1].start()
        for c in copies:
            c.wait()

    return pl.pallas_call(
        kernel,
        out_shape=[bf16(block_rows, width)] * 4,
        in_specs=[VMEM] * 15,
        out_specs=[ANY] * 4,
        scratch_shapes=[pltpu.VMEM((block_rows, width), jnp.bfloat16)] * 2
        + [pltpu.SemaphoreType.DMA((2 + 2 * heads,))],
        compiler_params=pltpu.CompilerParams(vmem_limit_bytes=16 * 2**20),
        name="next_rows",
    )(
        keys, first_got, second_got, next_upstream, first_stats, second_stats, later, next_bias, grown_t, slopes_t,
        *done, *scaled,
    )


def on_device(queries, key_states, value_states, upstream, clip_lengths):
    sharers = lax.axis_size("head")
    rows = queries.shape[0]
    pieces = cut_pieces(queries, key_states, value_states)
    pieces = [pieces[0]] + [partner_exchange(pieces[step], step) for step in range(1, sharers)]
    first, second = stack_values(pieces[0], pieces[1], upstream, rows)
    first_got, second_got = block_exchange(first, 0), block_exchange(second, 1)
    far_values, (own_bias, past_bias, next_bias) = stack_far_values(pieces[0], pieces[1], clip_lengths, rows)
    far_values = [partner_exchange(stack, 2 * pair + 2) for pair, stack in enumerate(far_values)]
    keys, query_rows, first, second = join_keys_queries(pieces, rows)
    previous, next_upstream = cut_previous_values(first_got, second_got, sharers // 2)
    first_got, second_got = block_exchange(first, 0), block_exchange(second, 1)
    previous = [partner_exchange(stack, 2 * pair) if pair else stack for pair, stack in enumerate(previous)]
    values, stats, tops, grown_t, slopes_t = own_scores(
        keys, query_rows, pieces[:2], far_values, upstream, own_bias, next_upstream
    )
    first_stats, second_stats = block_exchange(stats, 0), block_exchange(stats, 1)
    *own, later = own_products(keys, query_rows, upstream, values, grown_t, slopes_t, next_upstream)
    past_values, dchances = past_dchances(upstream, previous)
    attended, query_grads, *scaled = past_keys(
        query_rows, first_got, second_got, stats, tops, own, past_values, dchances, past_bias
    )
    return tuple(
        next_rows(
            keys, first_got, second_got, next_upstream, first_stats, second_stats, later, next_bias, grown_t,
            slopes_t, (attended, query_grads), scaled,
        )
    )


def solution(mesh):
    return jax.shard_map(
        on_device,
        mesh=mesh,
        in_specs=(
            P(("dp", "blk", "head"), None),
            P(("dp", "blk", "head"), None),
            P(("dp", "blk", "head"), None),
            P(("dp", "blk"), "head"),
            P("dp"),
        ),
        out_specs=(
            P(("dp", "blk"), "head"),
            P(("dp", "blk"), "head"),
            P(("dp", "blk"), "head"),
            P(("dp", "blk"), "head"),
        ),
        check_vma=False,
    )
```

```python
import math

import jax
import jax.numpy as jnp
from jax import lax
from jax.experimental import pallas as pl
from jax.experimental.pallas import tpu as pltpu
from jax.sharding import PartitionSpec as P

HEAD_DIM = 128
GROUP = 4
PAIR = 2

masked_fill = -1e30
score_scale = HEAD_DIM ** (-0.5)
exp2_scale = score_scale * math.log2(math.e)

VMEM = pl.BlockSpec(memory_space=pltpu.VMEM)
SMEM = pl.BlockSpec(memory_space=pltpu.SMEM)
ANY = pl.BlockSpec(memory_space=pl.ANY)


def bf16(*shape):
    return jax.ShapeDtypeStruct(shape, jnp.bfloat16)


def partner_exchange(rows, step):
    route = [(i, i ^ step) for i in range(lax.axis_size("head"))]
    return lax.ppermute(rows, "head", route)


def block_exchange(rows, parity):
    parts, blocks, sharers = lax.axis_size("dp"), lax.axis_size("blk"), lax.axis_size("head")
    route = []
    for part in range(parts):
        for block in range(blocks):
            other = block + 1 if block % 2 == parity else block - 1
            for sharer in range(sharers):
                here = (part * blocks + block) * sharers + sharer
                if 0 <= other < blocks:
                    route.append((here, (part * blocks + other) * sharers + sharer))
                else:
                    route.append((here, here ^ 1))
    return lax.ppermute(rows, ("dp", "blk", "head"), route)


def is_even():
    return lax.rem(lax.axis_index("blk"), 2) == 0


def place(step, size):
    owner = jnp.bitwise_xor(lax.axis_index("head"), step)
    return pl.ds(pl.multiple_of(owner * size, size), size)


def small_kernel():
    return pltpu.CompilerParams(vmem_limit_bytes=4 * 2**20)


def weighed(flops):
    return pl.CostEstimate(flops=int(flops), bytes_accessed=0, transcendentals=0)


def cut_pieces(queries, key_states, value_states):
    sharers = lax.axis_size("head")
    rows, features = queries.shape
    width = features // sharers
    heights = [(2 + sharers // 2) * rows if step < 2 else 2 * rows for step in range(sharers)]

    def kernel(q, k, v, *rest):
        pieces, sems = rest[:sharers], rest[sharers]
        copies = []

        def copy(source, target):
            copies.append(pltpu.make_async_copy(source, target, sems.at[len(copies)]))

        for step in range(sharers):
            columns = place(step, width)
            copy(k.at[:, columns], pieces[step].at[pl.ds(0, rows)])
            copy(q.at[:, columns], pieces[step].at[pl.ds(rows, rows)])
            copy(v.at[:, columns], pieces[step % 2].at[pl.ds((2 + step // 2) * rows, rows)])
        for c in copies:
            c.start()
        for c in copies:
            c.wait()

    return pl.pallas_call(
        kernel,
        out_shape=[bf16(height, width) for height in heights],
        in_specs=[ANY] * 3,
        out_specs=[VMEM] * sharers,
        scratch_shapes=[pltpu.SemaphoreType.DMA((3 * sharers,))],
        compiler_params=pltpu.CompilerParams(vmem_limit_bytes=53 * 2**20),
        name="cut_pieces",
    )(queries, key_states, value_states)


def stack_far_values(own, got, clip_lengths, rows):
    pairs = own.shape[0] // rows - 2
    width = own.shape[1]
    block_rows = 2 * pairs * rows

    def kernel(mine, theirs, lengths, own, past, ahead, *out):
        for pair in range(1, pairs):
            where = pl.ds((2 + pair) * rows, rows)
            out[pair - 1][pl.ds(0, rows), :] = mine[where, :]
            out[pair - 1][pl.ds(rows, rows), :] = theirs[where, :]
        block, blocks = lax.axis_index("blk"), lax.axis_size("blk")
        tall, wide = (block_rows, 1), (1, block_rows)
        key_ids, row_ids = clip_ids(lengths, tall, 0, block, blocks), clip_ids(lengths, wide, 1, block, blocks)
        own[...] = mask_bias(key_ids, row_ids)
        past[...] = mask_bias(clip_ids(lengths, tall, 0, block - 1, blocks), row_ids)
        ahead[...] = mask_bias(key_ids, clip_ids(lengths, wide, 1, block + 1, blocks))

    out = pl.pallas_call(
        kernel,
        out_shape=[jax.ShapeDtypeStruct((block_rows, block_rows), jnp.float32)] * 3
        + [bf16(2 * rows, width)] * (pairs - 1),
        in_specs=[VMEM] * 2 + [SMEM],
        out_specs=[VMEM] * (pairs + 2),
        compiler_params=small_kernel(),
        cost_estimate=weighed(5e9),
        name="stack_far_values",
    )(own, got, clip_lengths)
    return out[3:], out[:3]


def stack_values(own, got, upstream, rows):
    pairs = own.shape[0] // rows - 2
    width = own.shape[1]
    block_rows = upstream.shape[0]

    def kernel(mine, theirs, u, first, second):
        def spread(forward, backward):
            for pair in range(pairs):
                where = pl.ds((2 + pair) * rows, rows)
                forward[pl.ds(2 * pair * rows, rows), :] = mine[where, :]
                forward[pl.ds((2 * pair + 1) * rows, rows), :] = theirs[where, :]
            backward[...] = u[...]

        @pl.when(is_even())
        def _():
            spread(first, second)

        @pl.when(jnp.logical_not(is_even()))
        def _():
            spread(second, first)

    return pl.pallas_call(
        kernel,
        out_shape=[bf16(block_rows, width)] * 2,
        in_specs=[VMEM] * 3,
        out_specs=[VMEM] * 2,
        compiler_params=small_kernel(),
        cost_estimate=weighed(0),
        name="stack_values",
    )(own, got, upstream)


def join_keys_queries(pieces, rows):
    sharers = len(pieces)
    width = pieces[0].shape[1]
    block_rows = rows * sharers

    def kernel(*refs):
        pieces_in = refs[:sharers]
        keys, queries, first, second = refs[sharers:]
        for step in range(sharers):
            where = place(step, rows)
            keys[where, :] = pieces_in[step][pl.ds(0, rows), :]
            queries[where, :] = pieces_in[step][pl.ds(rows, rows), :]

        @pl.when(is_even())
        def _():
            first[...] = keys[...]
            second[...] = queries[...]

        @pl.when(jnp.logical_not(is_even()))
        def _():
            first[...] = queries[...]
            second[...] = keys[...]

    return pl.pallas_call(
        kernel,
        out_shape=[bf16(block_rows, width)] * 4,
        in_specs=[VMEM] * sharers,
        out_specs=[VMEM] * 4,
        compiler_params=small_kernel(),
        cost_estimate=weighed(0),
        name="join_keys_queries",
    )(*pieces)


def cut_previous_values(first_got, second_got, pairs):
    block_rows, width = first_got.shape
    rows = block_rows // pairs

    def kernel(first, second, *out):
        def split(forward, backward):
            for pair in range(pairs):
                out[pair][...] = forward[pl.ds(pair * rows, rows), :]
            out[pairs][...] = backward[...]

        @pl.when(is_even())
        def _():
            split(second, first)

        @pl.when(jnp.logical_not(is_even()))
        def _():
            split(first, second)

    out = pl.pallas_call(
        kernel,
        out_shape=[bf16(rows, width)] * pairs + [bf16(block_rows, width)],
        in_specs=[VMEM] * 2,
        out_specs=[VMEM] * (pairs + 1),
        compiler_params=small_kernel(),
        cost_estimate=weighed(0),
        name="cut_previous_values",
    )(first_got, second_got)
    return out[:pairs], out[pairs]


def clip_ids(lengths, shape, axis, block, blocks):
    position = block * shape[axis] + lax.broadcasted_iota(jnp.int32, shape, axis)
    ids, end = jnp.zeros(shape, jnp.int32), jnp.int32(0)
    for clip in range(lengths.shape[0]):
        end = end + lengths[clip]
        ids = ids + (position >= end).astype(jnp.int32)
    return jnp.where(jnp.logical_and(block >= 0, block < blocks), ids, -1)


def mask_bias(key_ids, query_ids):
    return jnp.where(key_ids == query_ids, 0.0, masked_fill).astype(jnp.float32)


def by_rows(a, b):
    return lax.dot_general(a, b, (((1,), (1,)), ((), ())), preferred_element_type=jnp.float32)


def by_columns(a, b):
    return lax.dot_general(a, b, (((0,), (0,)), ((), ())), preferred_element_type=jnp.float32)


def product(a, b):
    return jnp.dot(a, b, preferred_element_type=jnp.float32)


def own_scores(keys, queries, chip_values, far_values, upstream, bias, after):
    sharers = 2 + 2 * len(far_values)
    block_rows, width = keys.shape
    rows = block_rows // sharers
    heads = width // HEAD_DIM

    def kernel(k, q, u, bias, _, *rest):
        values_in = [ref.at[pl.ds(2 * rows, rows)] for ref in rest[:2]]
        for ref in rest[2 : 1 + sharers // 2]:
            values_in += [ref.at[pl.ds(0, rows)], ref.at[pl.ds(rows, rows)]]
        values, stats, tops, grown_t, slopes_t = rest[1 + sharers // 2 :]
        for step in range(sharers):
            values[place(step, rows), :] = values_in[step][...]
        for start in range(0, heads, GROUP):
            group = range(start, min(start + GROUP, heads))
            cols = [pl.ds(head * HEAD_DIM, HEAD_DIM) for head in group]
            scores = [by_rows(k[:, c], q[:, c]) * exp2_scale + bias[...] for c in cols]
            maxes = [jnp.max(x, axis=0, keepdims=True) for x in scores]
            grown = [jnp.exp2(x - m) for x, m in zip(scores, maxes)]
            totals = [jnp.sum(x, axis=0, keepdims=True) for x in grown]
            dchances = [by_rows(values[:, c], u[:, c]) for c in cols]
            offsets = [
                jnp.sum(x * d, axis=0, keepdims=True) / total for x, d, total in zip(grown, dchances, totals)
            ]
            for n, head in enumerate(group):
                stats[pl.ds(head, 1), :] = maxes[n] + jnp.log2(totals[n])
                stats[pl.ds(heads + head, 1), :] = offsets[n]
                tops[pl.ds(head, 1), :] = maxes[n]
                grown_t[head] = grown[n].astype(jnp.bfloat16)
                slopes_t[head] = (grown[n] * (dchances[n] - offsets[n])).astype(jnp.bfloat16)

    square = bf16(heads, block_rows, block_rows)
    return pl.pallas_call(
        kernel,
        out_shape=[
            bf16(block_rows, width),
            jax.ShapeDtypeStruct((2 * heads, block_rows), jnp.float32),
            jax.ShapeDtypeStruct((heads, block_rows), jnp.float32),
            square,
            square,
        ],
        in_specs=[VMEM] * (6 + sharers // 2),
        out_specs=[VMEM] * 5,
        compiler_params=pltpu.CompilerParams(vmem_limit_bytes=12 * 2**20),
        cost_estimate=weighed(0),
        name="own_scores",
    )(keys, queries, upstream, bias, after, *chip_values, *far_values)


def own_products(keys, queries, upstream, values, grown_t, slopes_t, next_upstream):
    block_rows, width = keys.shape
    heads = width // HEAD_DIM

    def kernel(k, q, u, v, grown_t, slopes_t, nu, sums, slope_keys, query_t, up_t, later):
        for head in range(heads):
            columns = pl.ds(head * HEAD_DIM, HEAD_DIM)
            key, value = k[:, columns], v[:, columns]
            sums[head] = by_columns(jnp.concatenate([value, key], axis=1), grown_t[head])
            slope_keys[head] = by_columns(key, slopes_t[head])
            query_t[head] = jnp.transpose(q[:, columns]).astype(jnp.float32)
            up_t[head] = jnp.transpose(u[:, columns]).astype(jnp.float32)
            later[head] = by_rows(value, nu[:, columns])

    def turned(tall):
        return jax.ShapeDtypeStruct((heads, tall, block_rows), jnp.float32)

    return pl.pallas_call(
        kernel,
        out_shape=[turned(2 * HEAD_DIM)] + [turned(HEAD_DIM)] * 3 + [turned(block_rows)],
        in_specs=[VMEM] * 7,
        out_specs=[VMEM] * 5,
        compiler_params=pltpu.CompilerParams(vmem_limit_bytes=16 * 2**20),
        cost_estimate=weighed(1e9),
        name="own_products",
    )(keys, queries, upstream, values, grown_t, slopes_t, next_upstream)


def past_dchances(upstream, previous_values):
    pairs = len(previous_values)
    block_rows, width = upstream.shape
    rows = block_rows // pairs // 2
    heads = width // HEAD_DIM

    def kernel(u, *rest):
        pieces, (values, dchances) = rest[:pairs], rest[pairs:]
        for step in range(2 * pairs):
            values[place(step, rows), :] = pieces[step // 2][pl.ds(step % 2 * rows, rows), :]
        for head in range(heads):
            columns = pl.ds(head * HEAD_DIM, HEAD_DIM)
            dchances[head] = by_rows(values[:, columns], u[:, columns])

    return pl.pallas_call(
        kernel,
        out_shape=[bf16(block_rows, width), jax.ShapeDtypeStruct((heads, block_rows, block_rows), jnp.float32)],
        in_specs=[VMEM] * (1 + pairs),
        out_specs=[VMEM] * 2,
        compiler_params=small_kernel(),
        cost_estimate=weighed(1e9),
        name="past_dchances",
    )(upstream, *previous_values)


def add_past(refs, past_key, results, heads):
    q, own_stats, tops, sums, slope_keys, query_t, up_t, pv, dchances, bias = refs
    attended, query_grads, scaled_query, shifted_query, scaled_up = results
    for start in range(0, heads, GROUP):
        group = range(start, min(start + GROUP, heads))
        cols = [pl.ds(head * HEAD_DIM, HEAD_DIM) for head in group]
        tops_here = [tops[pl.ds(head, 1), :] for head in group]
        own_offsets = [own_stats[pl.ds(heads + head, 1), :] for head in group]
        if past_key is None:
            factors = [jnp.exp2(top - own_stats[pl.ds(head, 1), :]) for head, top in zip(group, tops_here)]
        else:
            keys = [past_key[:, c] for c in cols]
            scores = [by_rows(key, q[:, c]) * exp2_scale + bias[...] for key, c in zip(keys, cols)]
            maxes = [jnp.maximum(top, jnp.max(x, axis=0, keepdims=True)) for top, x in zip(tops_here, scores)]
            grown = [jnp.exp2(x - m) for x, m in zip(scores, maxes)]
            own = [jnp.exp2(own_stats[pl.ds(head, 1), :] - m) for head, m in zip(group, maxes)]
            shares = [1.0 / (o + jnp.sum(x, axis=0, keepdims=True)) for o, x in zip(own, grown)]
            offsets = [
                y * (offset * o + jnp.sum(x * dchances[head], axis=0, keepdims=True))
                for head, offset, o, x, y in zip(group, own_offsets, own, grown, shares)
            ]
            factors = [jnp.exp2(top - m) * y for top, m, y in zip(tops_here, maxes, shares)]
            shifts = [f * (o - offset) for f, o, offset in zip(factors, offsets, own_offsets)]
            chances = [x * y for x, y in zip(grown, shares)]
            weights = [x.astype(jnp.bfloat16) for x in chances]
            dscores = [(x * (dchances[head] - o)).astype(jnp.bfloat16) for x, head, o in zip(chances, group, offsets)]
        for n, (head, c) in enumerate(zip(group, cols)):
            factor = factors[n]
            attended_t = factor * sums[head, :HEAD_DIM]
            grads_t = factor * slope_keys[head]
            if past_key is None:
                shifted_query[head] = jnp.zeros(shifted_query.shape[1:], jnp.bfloat16)
            else:
                attended_t = attended_t + by_columns(pv[:, c], weights[n])
                grads_t = grads_t - shifts[n] * sums[head, HEAD_DIM:] + by_columns(keys[n], dscores[n])
                shifted_query[head] = (query_t[head] * -shifts[n]).astype(jnp.bfloat16)
            attended[:, c] = jnp.transpose(attended_t.astype(jnp.bfloat16))
            query_grads[:, c] = jnp.transpose((score_scale * grads_t).astype(jnp.bfloat16))
            scaled_query[head] = (query_t[head] * factor).astype(jnp.bfloat16)
            scaled_up[head] = (up_t[head] * factor).astype(jnp.bfloat16)


def own_gradients(grown_t, slopes_t, scaled, head):
    scaled_query, shifted_query, scaled_up = scaled
    mixed = by_rows(grown_t[head], jnp.concatenate([scaled_up[head], shifted_query[head]], axis=0))
    return mixed[:, :HEAD_DIM], mixed[:, HEAD_DIM:] + by_rows(slopes_t[head], scaled_query[head])


def next_part(refs, later_query, group, heads, extra=None):
    k, nu, stats, later, bias = refs
    cols = [pl.ds(head * HEAD_DIM, HEAD_DIM) for head in group]
    scores = [by_rows(k[:, c], later_query[:, c]) * exp2_scale + bias[...] for c in cols]
    more = [extra(head) for head in group] if extra else None
    far = [stats[pl.ds(head, 1), :] for head in group]
    maxes = [jnp.maximum(f, jnp.max(x, axis=0, keepdims=True)) for f, x in zip(far, scores)]
    grown = [jnp.exp2(x - m) for x, m in zip(scores, maxes)]
    far = [jnp.exp2(f - m) for f, m in zip(far, maxes)]
    shares = [1.0 / (f + jnp.sum(x, axis=0, keepdims=True)) for f, x in zip(far, grown)]
    offsets = [
        y * (stats[pl.ds(heads + head, 1), :] * f + jnp.sum(x * later[head], axis=0, keepdims=True))
        for head, f, x, y in zip(group, far, grown, shares)
    ]
    chances = [x * y for x, y in zip(grown, shares)]
    weights = [x.astype(jnp.bfloat16) for x in chances]
    dscores = [(x * (later[head] - o)).astype(jnp.bfloat16) for x, head, o in zip(chances, group, offsets)]
    parts = [
        [product(weights[n], nu[:, c]), product(dscores[n], later_query[:, c])] for n, c in enumerate(cols)
    ]
    if more:
        parts = [[x + y for x, y in zip(*pair)] for pair in zip(parts, more)]
    return parts


def first_half(keys, first_got, next_upstream, first_stats, later, next_bias, past_refs):
    block_rows, width = keys.shape
    heads = width // HEAD_DIM
    past_count = len(past_refs)

    def kernel(k, first, nu, stats, later, next_bias, *rest):
        past_in, results = rest[:past_count], rest[past_count : past_count + 5]
        value_part, key_part = rest[past_count + 5 :]

        @pl.when(is_even())
        def _():
            for start in range(0, heads, GROUP):
                group = range(start, min(start + GROUP, heads))
                parts = next_part((k, nu, stats, later, next_bias), first, group, heads)
                for head, (value, key) in zip(group, parts):
                    columns = pl.ds(head * HEAD_DIM, HEAD_DIM)
                    value_part[:, columns] = value
                    key_part[:, columns] = key

        @pl.when(jnp.logical_not(is_even()))
        def _():
            add_past(past_in, first, results, heads)

    wide = jax.ShapeDtypeStruct((block_rows, width), jnp.float32)
    out = pl.pallas_call(
        kernel,
        out_shape=[bf16(block_rows, width)] * 2 + [bf16(heads, HEAD_DIM, block_rows)] * 3 + [wide] * 2,
        in_specs=[VMEM] * (6 + past_count),
        out_specs=[VMEM] * 7,
        compiler_params=pltpu.CompilerParams(vmem_limit_bytes=20 * 2**20),
        cost_estimate=weighed(0),
        name="first_half",
    )(keys, first_got, next_upstream, first_stats, later, next_bias, *past_refs)
    return out[:5], out[5:]


def second_half(keys, second_got, next_upstream, second_stats, later, next_bias, grown_t, slopes_t, past_refs, done, parts):
    block_rows, width = keys.shape
    heads = width // HEAD_DIM
    past_count = len(past_refs)

    def kernel(k, second, nu, stats, later, next_bias, grown_t, slopes_t, *rest):
        past_in, rest = rest[:past_count], rest[past_count:]
        done, (value_part, key_part), outs, rest = rest[:5], rest[5:7], rest[7:11], rest[11:]
        here, (key_grads, value_grads, sems) = rest[:5], rest[5:]

        def send(rows, i, slot, columns=slice(None)):
            copy = pltpu.make_async_copy(rows.at[:, columns], outs[i].at[:, columns], sems.at[slot])
            copy.start()
            return copy

        def finish(rows, from_next):
            copies = [send(rows[0], 0, 0), send(rows[1], 1, 1)]
            for start in range(0, heads, PAIR):
                group = range(start, min(start + PAIR, heads))
                for head, (value, key) in zip(group, from_next(group, rows[2:])):
                    columns = pl.ds(head * HEAD_DIM, HEAD_DIM)
                    value_grads[:, columns] = value.astype(jnp.bfloat16)
                    key_grads[:, columns] = (score_scale * key).astype(jnp.bfloat16)
                columns = pl.ds(start * HEAD_DIM, len(group) * HEAD_DIM)
                copies.append(send(key_grads, 2, len(copies), columns))
                copies.append(send(value_grads, 3, len(copies), columns))
            for copy in copies:
                copy.wait()

        def added(group, scaled):
            parts = []
            for head in group:
                value, key = own_gradients(grown_t, slopes_t, scaled, head)
                columns = pl.ds(head * HEAD_DIM, HEAD_DIM)
                parts.append([value + value_part[:, columns], key + key_part[:, columns]])
            return parts

        def computed(group, scaled):
            return next_part(
                (k, nu, stats, later, next_bias), second, group, heads,
                lambda head: own_gradients(grown_t, slopes_t, scaled, head),
            )

        block = lax.axis_index("blk")

        @pl.when(block == 0)
        def _():
            add_past(past_in, None, here, heads)

        @pl.when(jnp.logical_and(is_even(), block > 0))
        def _():
            add_past(past_in, second, here, heads)

        @pl.when(is_even())
        def _():
            finish(here, added)

        @pl.when(jnp.logical_not(is_even()))
        def _():
            finish(done, computed)

    return pl.pallas_call(
        kernel,
        out_shape=[bf16(block_rows, width)] * 4,
        in_specs=[VMEM] * (15 + past_count),
        out_specs=[ANY] * 4,
        scratch_shapes=[pltpu.VMEM((block_rows, width), jnp.bfloat16)] * 2
        + [pltpu.VMEM((heads, HEAD_DIM, block_rows), jnp.bfloat16)] * 3
        + [pltpu.VMEM((block_rows, width), jnp.bfloat16)] * 2
        + [pltpu.SemaphoreType.DMA((2 + 2 * heads,))],
        compiler_params=pltpu.CompilerParams(vmem_limit_bytes=20 * 2**20),
        cost_estimate=weighed(0),
        name="second_half",
    )(
        keys, second_got, next_upstream, second_stats, later, next_bias, grown_t, slopes_t, *past_refs, *done, *parts,
    )


def on_device(queries, key_states, value_states, upstream, clip_lengths):
    sharers = lax.axis_size("head")
    rows = queries.shape[0]
    pieces = cut_pieces(queries, key_states, value_states)
    pieces = [pieces[0]] + [partner_exchange(pieces[step], step) for step in range(1, sharers)]
    first, second = stack_values(pieces[0], pieces[1], upstream, rows)
    first_got, second_got = block_exchange(first, 0), block_exchange(second, 1)
    far_values, (own_bias, past_bias, next_bias) = stack_far_values(pieces[0], pieces[1], clip_lengths, rows)
    far_values = [partner_exchange(stack, 2 * pair + 2) for pair, stack in enumerate(far_values)]
    keys, query_rows, first, second = join_keys_queries(pieces, rows)
    previous, next_upstream = cut_previous_values(first_got, second_got, sharers // 2)
    first_got, second_got = block_exchange(first, 0), block_exchange(second, 1)
    previous = [partner_exchange(stack, 2 * pair) if pair else stack for pair, stack in enumerate(previous)]
    values, stats, tops, grown_t, slopes_t = own_scores(
        keys, query_rows, pieces[:2], far_values, upstream, own_bias, next_upstream
    )
    first_stats, second_stats = block_exchange(stats, 0), block_exchange(stats, 1)
    *own, later = own_products(keys, query_rows, upstream, values, grown_t, slopes_t, next_upstream)
    past_values, dchances = past_dchances(upstream, previous)
    past_refs = (query_rows, stats, tops, *own, past_values, dchances, past_bias)
    done, parts = first_half(keys, first_got, next_upstream, first_stats, later, next_bias, past_refs)
    return tuple(
        second_half(
            keys, second_got, next_upstream, second_stats, later, next_bias, grown_t, slopes_t, past_refs, done, parts
        )
    )


def solution(mesh):
    return jax.shard_map(
        on_device,
        mesh=mesh,
        in_specs=(
            P(("dp", "blk", "head"), None),
            P(("dp", "blk", "head"), None),
            P(("dp", "blk", "head"), None),
            P(("dp", "blk"), "head"),
            P("dp"),
        ),
        out_specs=(
            P(("dp", "blk"), "head"),
            P(("dp", "blk"), "head"),
            P(("dp", "blk"), "head"),
            P(("dp", "blk"), "head"),
        ),
        check_vma=False,
    )
```

```python
import math

import jax
import jax.numpy as jnp
from jax import lax
from jax.experimental import pallas as pl
from jax.experimental.pallas import tpu as pltpu
from jax.sharding import PartitionSpec as P

HEAD_DIM = 128
GROUP = 4
PAIR = 2

masked_fill = -1e30
score_scale = HEAD_DIM ** (-0.5)
exp2_scale = score_scale * math.log2(math.e)

VMEM = pl.BlockSpec(memory_space=pltpu.VMEM)
SMEM = pl.BlockSpec(memory_space=pltpu.SMEM)
ANY = pl.BlockSpec(memory_space=pl.ANY)


def bf16(*shape):
    return jax.ShapeDtypeStruct(shape, jnp.bfloat16)


def partner_exchange(rows, step):
    route = [(i, i ^ step) for i in range(lax.axis_size("head"))]
    return lax.ppermute(rows, "head", route)


def block_exchange(rows, parity):
    parts, blocks, sharers = lax.axis_size("dp"), lax.axis_size("blk"), lax.axis_size("head")
    route = []
    for part in range(parts):
        for block in range(blocks):
            other = block + 1 if block % 2 == parity else block - 1
            for sharer in range(sharers):
                here = (part * blocks + block) * sharers + sharer
                if 0 <= other < blocks:
                    route.append((here, (part * blocks + other) * sharers + sharer))
                else:
                    route.append((here, here ^ 1))
    return lax.ppermute(rows, ("dp", "blk", "head"), route)


def is_even():
    return lax.rem(lax.axis_index("blk"), 2) == 0


def place(step, size):
    owner = jnp.bitwise_xor(lax.axis_index("head"), step)
    return pl.ds(pl.multiple_of(owner * size, size), size)


def small_kernel():
    return pltpu.CompilerParams(vmem_limit_bytes=4 * 2**20)


def weighed(flops):
    return pl.CostEstimate(flops=int(flops), bytes_accessed=0, transcendentals=0)


def cut_pieces(queries, key_states, value_states):
    sharers = lax.axis_size("head")
    rows, features = queries.shape
    width = features // sharers
    heights = [(2 + sharers // 2) * rows if step < 2 else 2 * rows for step in range(sharers)]

    def kernel(q, k, v, *rest):
        pieces, sems = rest[:sharers], rest[sharers]
        copies = []

        def copy(source, target):
            copies.append(pltpu.make_async_copy(source, target, sems.at[len(copies)]))

        for step in range(sharers):
            columns = place(step, width)
            copy(k.at[:, columns], pieces[step].at[pl.ds(0, rows)])
            copy(q.at[:, columns], pieces[step].at[pl.ds(rows, rows)])
            copy(v.at[:, columns], pieces[step % 2].at[pl.ds((2 + step // 2) * rows, rows)])
        for c in copies:
            c.start()
        for c in copies:
            c.wait()

    return pl.pallas_call(
        kernel,
        out_shape=[bf16(height, width) for height in heights],
        in_specs=[ANY] * 3,
        out_specs=[VMEM] * sharers,
        scratch_shapes=[pltpu.SemaphoreType.DMA((3 * sharers,))],
        compiler_params=pltpu.CompilerParams(vmem_limit_bytes=53 * 2**20),
        name="cut_pieces",
    )(queries, key_states, value_states)


def stack_far_values(own, got, clip_lengths, rows):
    pairs = own.shape[0] // rows - 2
    width = own.shape[1]
    block_rows = 2 * pairs * rows

    def kernel(mine, theirs, lengths, own, past, ahead, *out):
        for pair in range(1, pairs):
            where = pl.ds((2 + pair) * rows, rows)
            out[pair - 1][pl.ds(0, rows), :] = mine[where, :]
            out[pair - 1][pl.ds(rows, rows), :] = theirs[where, :]
        block, blocks = lax.axis_index("blk"), lax.axis_size("blk")
        tall, wide = (block_rows, 1), (1, block_rows)
        key_ids, row_ids = clip_ids(lengths, tall, 0, block, blocks), clip_ids(lengths, wide, 1, block, blocks)
        own[...] = mask_bias(key_ids, row_ids)
        past[...] = mask_bias(clip_ids(lengths, tall, 0, block - 1, blocks), row_ids)
        ahead[...] = mask_bias(key_ids, clip_ids(lengths, wide, 1, block + 1, blocks))

    out = pl.pallas_call(
        kernel,
        out_shape=[jax.ShapeDtypeStruct((block_rows, block_rows), jnp.float32)] * 3
        + [bf16(2 * rows, width)] * (pairs - 1),
        in_specs=[VMEM] * 2 + [SMEM],
        out_specs=[VMEM] * (pairs + 2),
        compiler_params=small_kernel(),
        cost_estimate=weighed(5e9),
        name="stack_far_values",
    )(own, got, clip_lengths)
    return out[3:], out[:3]


def stack_values(own, got, upstream, rows):
    pairs = own.shape[0] // rows - 2
    width = own.shape[1]
    block_rows = upstream.shape[0]

    def kernel(mine, theirs, u, first, second):
        def spread(forward, backward):
            for pair in range(pairs):
                where = pl.ds((2 + pair) * rows, rows)
                forward[pl.ds(2 * pair * rows, rows), :] = mine[where, :]
                forward[pl.ds((2 * pair + 1) * rows, rows), :] = theirs[where, :]
            backward[...] = u[...]

        @pl.when(is_even())
        def _():
            spread(first, second)

        @pl.when(jnp.logical_not(is_even()))
        def _():
            spread(second, first)

    return pl.pallas_call(
        kernel,
        out_shape=[bf16(block_rows, width)] * 2,
        in_specs=[VMEM] * 3,
        out_specs=[VMEM] * 2,
        compiler_params=small_kernel(),
        cost_estimate=weighed(0),
        name="stack_values",
    )(own, got, upstream)


def join_keys_queries(pieces, rows):
    sharers = len(pieces)
    width = pieces[0].shape[1]
    block_rows = rows * sharers

    def kernel(*refs):
        pieces_in = refs[:sharers]
        keys, queries, first, second = refs[sharers:]
        for step in range(sharers):
            where = place(step, rows)
            keys[where, :] = pieces_in[step][pl.ds(0, rows), :]
            queries[where, :] = pieces_in[step][pl.ds(rows, rows), :]

        @pl.when(is_even())
        def _():
            first[...] = keys[...]
            second[...] = queries[...]

        @pl.when(jnp.logical_not(is_even()))
        def _():
            first[...] = queries[...]
            second[...] = keys[...]

    return pl.pallas_call(
        kernel,
        out_shape=[bf16(block_rows, width)] * 4,
        in_specs=[VMEM] * sharers,
        out_specs=[VMEM] * 4,
        compiler_params=small_kernel(),
        cost_estimate=weighed(0),
        name="join_keys_queries",
    )(*pieces)


def cut_previous_values(first_got, second_got, pairs):
    block_rows, width = first_got.shape
    rows = block_rows // pairs

    def kernel(first, second, *out):
        def split(forward, backward):
            for pair in range(pairs):
                out[pair][...] = forward[pl.ds(pair * rows, rows), :]
            out[pairs][...] = backward[...]

        @pl.when(is_even())
        def _():
            split(second, first)

        @pl.when(jnp.logical_not(is_even()))
        def _():
            split(first, second)

    out = pl.pallas_call(
        kernel,
        out_shape=[bf16(rows, width)] * pairs + [bf16(block_rows, width)],
        in_specs=[VMEM] * 2,
        out_specs=[VMEM] * (pairs + 1),
        compiler_params=small_kernel(),
        cost_estimate=weighed(0),
        name="cut_previous_values",
    )(first_got, second_got)
    return out[:pairs], out[pairs]


def clip_ids(lengths, shape, axis, block, blocks):
    position = block * shape[axis] + lax.broadcasted_iota(jnp.int32, shape, axis)
    ids, end = jnp.zeros(shape, jnp.int32), jnp.int32(0)
    for clip in range(lengths.shape[0]):
        end = end + lengths[clip]
        ids = ids + (position >= end).astype(jnp.int32)
    return jnp.where(jnp.logical_and(block >= 0, block < blocks), ids, -1)


def mask_bias(key_ids, query_ids):
    return jnp.where(key_ids == query_ids, 0.0, masked_fill).astype(jnp.float32)


def by_rows(a, b):
    return lax.dot_general(a, b, (((1,), (1,)), ((), ())), preferred_element_type=jnp.float32)


def by_columns(a, b):
    return lax.dot_general(a, b, (((0,), (0,)), ((), ())), preferred_element_type=jnp.float32)


def product(a, b):
    return jnp.dot(a, b, preferred_element_type=jnp.float32)


def own_scores(keys, queries, chip_values, far_values, upstream, bias, after):
    sharers = 2 + 2 * len(far_values)
    block_rows, width = keys.shape
    rows = block_rows // sharers
    heads = width // HEAD_DIM

    def kernel(k, q, u, bias, _, *rest):
        values_in = [ref.at[pl.ds(2 * rows, rows)] for ref in rest[:2]]
        for ref in rest[2 : 1 + sharers // 2]:
            values_in += [ref.at[pl.ds(0, rows)], ref.at[pl.ds(rows, rows)]]
        values, stats, tops, grown_t, slopes_t = rest[1 + sharers // 2 :]
        for step in range(sharers):
            values[place(step, rows), :] = values_in[step][...]
        for start in range(0, heads, GROUP):
            group = range(start, min(start + GROUP, heads))
            cols = [pl.ds(head * HEAD_DIM, HEAD_DIM) for head in group]
            scores = [by_rows(k[:, c], q[:, c]) * exp2_scale + bias[...] for c in cols]
            maxes = [jnp.max(x, axis=0, keepdims=True) for x in scores]
            grown = [jnp.exp2(x - m) for x, m in zip(scores, maxes)]
            totals = [jnp.sum(x, axis=0, keepdims=True) for x in grown]
            dchances = [by_rows(values[:, c], u[:, c]) for c in cols]
            offsets = [
                jnp.sum(x * d, axis=0, keepdims=True) / total for x, d, total in zip(grown, dchances, totals)
            ]
            for n, head in enumerate(group):
                stats[pl.ds(head, 1), :] = maxes[n] + jnp.log2(totals[n])
                stats[pl.ds(heads + head, 1), :] = offsets[n]
                tops[pl.ds(head, 1), :] = maxes[n]
                grown_t[head] = grown[n].astype(jnp.bfloat16)
                slopes_t[head] = (grown[n] * (dchances[n] - offsets[n])).astype(jnp.bfloat16)

    square = bf16(heads, block_rows, block_rows)
    return pl.pallas_call(
        kernel,
        out_shape=[
            bf16(block_rows, width),
            jax.ShapeDtypeStruct((2 * heads, block_rows), jnp.float32),
            jax.ShapeDtypeStruct((heads, block_rows), jnp.float32),
            square,
            square,
        ],
        in_specs=[VMEM] * (6 + sharers // 2),
        out_specs=[VMEM] * 5,
        compiler_params=pltpu.CompilerParams(vmem_limit_bytes=12 * 2**20),
        cost_estimate=weighed(0),
        name="own_scores",
    )(keys, queries, upstream, bias, after, *chip_values, *far_values)


def own_products(keys, queries, upstream, values, grown_t, slopes_t, next_upstream):
    block_rows, width = keys.shape
    heads = width // HEAD_DIM

    def kernel(k, q, u, v, grown_t, slopes_t, nu, sums, slope_keys, query_t, up_t, later):
        for head in range(heads):
            columns = pl.ds(head * HEAD_DIM, HEAD_DIM)
            key, value = k[:, columns], v[:, columns]
            sums[head] = by_columns(jnp.concatenate([value, key], axis=1), grown_t[head])
            slope_keys[head] = by_columns(key, slopes_t[head])
            query_t[head] = jnp.transpose(q[:, columns]).astype(jnp.float32)
            up_t[head] = jnp.transpose(u[:, columns]).astype(jnp.float32)
            later[head] = by_rows(value, nu[:, columns])

    def turned(tall):
        return jax.ShapeDtypeStruct((heads, tall, block_rows), jnp.float32)

    return pl.pallas_call(
        kernel,
        out_shape=[turned(2 * HEAD_DIM)] + [turned(HEAD_DIM)] * 3 + [turned(block_rows)],
        in_specs=[VMEM] * 7,
        out_specs=[VMEM] * 5,
        compiler_params=pltpu.CompilerParams(vmem_limit_bytes=16 * 2**20),
        cost_estimate=weighed(1e9),
        name="own_products",
    )(keys, queries, upstream, values, grown_t, slopes_t, next_upstream)


def past_part(refs, past_key, group, heads):
    q, own_stats, tops, _, _, _, _, pv, dchances, bias = refs
    cols = [pl.ds(head * HEAD_DIM, HEAD_DIM) for head in group]
    tops = [tops[pl.ds(head, 1), :] for head in group]
    own_norms = [own_stats[pl.ds(head, 1), :] for head in group]
    own_offsets = [own_stats[pl.ds(heads + head, 1), :] for head in group]
    if past_key is None:
        return [(jnp.exp2(top - norm), None, None) for top, norm in zip(tops, own_norms)]
    keys = [past_key[:, c] for c in cols]
    scores = [by_rows(key, q[:, c]) * exp2_scale + bias[...] for key, c in zip(keys, cols)]
    maxes = [jnp.maximum(top, jnp.max(x, axis=0, keepdims=True)) for top, x in zip(tops, scores)]
    grown = [jnp.exp2(x - m) for x, m in zip(scores, maxes)]
    own = [jnp.exp2(norm - m) for norm, m in zip(own_norms, maxes)]
    shares = [1.0 / (o + jnp.sum(x, axis=0, keepdims=True)) for o, x in zip(own, grown)]
    offsets = [
        y * (offset * o + jnp.sum(x * dchances[head], axis=0, keepdims=True))
        for head, offset, o, x, y in zip(group, own_offsets, own, grown, shares)
    ]
    factors = [jnp.exp2(top - m) * y for top, m, y in zip(tops, maxes, shares)]
    shifts = [f * (o - offset) for f, o, offset in zip(factors, offsets, own_offsets)]
    chances = [x * y for x, y in zip(grown, shares)]
    weights = [x.astype(jnp.bfloat16) for x in chances]
    dscores = [(x * (dchances[head] - o)).astype(jnp.bfloat16) for x, head, o in zip(chances, group, offsets)]
    return list(zip(factors, shifts, zip(weights, dscores, keys)))


def scaled_rows(refs, part, head):
    _, _, _, _, _, query_t, up_t, _, _, _ = refs
    factor, shift, _ = part
    query, up = query_t[head], up_t[head]
    if shift is None:
        shifted = jnp.zeros(query.shape, jnp.bfloat16)
    else:
        shifted = (query * -shift).astype(jnp.bfloat16)
    return (query * factor).astype(jnp.bfloat16), shifted, (up * factor).astype(jnp.bfloat16)


def done_rows(refs, part, head):
    _, _, _, sums, slope_keys, _, _, pv, _, _ = refs
    factor, shift, past = part
    attended, grads = factor * sums[head, :HEAD_DIM], factor * slope_keys[head]
    if past is not None:
        weights, dscores, key = past
        attended = attended + product(pv[head], weights)
        grads = grads - shift * sums[head, HEAD_DIM:] + by_columns(key, dscores)
    return (
        jnp.transpose(attended.astype(jnp.bfloat16)),
        jnp.transpose((score_scale * grads).astype(jnp.bfloat16)),
    )


def own_gradients(grown_t, slopes_t, scaled, head):
    scaled_query, shifted_query, scaled_up = scaled
    mixed = by_rows(grown_t[head], jnp.concatenate([scaled_up, shifted_query], axis=0))
    return mixed[:, :HEAD_DIM], mixed[:, HEAD_DIM:] + by_rows(slopes_t[head], scaled_query)


def before_exchanges(upstream, previous_values, queries, stats, tops, own, grown_t, slopes_t):
    pairs = len(previous_values)
    block_rows, width = upstream.shape
    rows = block_rows // pairs // 2
    heads = width // HEAD_DIM

    def kernel(u, q, own_stats, tops, sums, slope_keys, query_t, up_t, grown_t, slopes_t, *rest):
        pieces, (turned, dchances, attended, query_grads, value_own, key_own, values) = rest[:pairs], rest[pairs:]
        first = lax.axis_index("blk") == 0

        @pl.when(jnp.logical_not(first))
        def _():
            for step in range(2 * pairs):
                values[place(step, rows), :] = pieces[step // 2][pl.ds(step % 2 * rows, rows), :]
            for head in range(heads):
                columns = pl.ds(head * HEAD_DIM, HEAD_DIM)
                dchances[head] = by_rows(values[:, columns], u[:, columns])
                turned[head] = jnp.transpose(values[:, columns])

        @pl.when(first)
        def _():
            refs = (q, own_stats, tops, sums, slope_keys, query_t, up_t, turned, dchances, None)
            for head, part in enumerate(past_part(refs, None, range(heads), heads)):
                columns = pl.ds(head * HEAD_DIM, HEAD_DIM)
                attended[:, columns], query_grads[:, columns] = done_rows(refs, part, head)
                value_own[:, columns], key_own[:, columns] = own_gradients(
                    grown_t, slopes_t, scaled_rows(refs, part, head), head
                )

    wide = jax.ShapeDtypeStruct((block_rows, width), jnp.float32)
    return pl.pallas_call(
        kernel,
        out_shape=[
            bf16(heads, HEAD_DIM, block_rows),
            jax.ShapeDtypeStruct((heads, block_rows, block_rows), jnp.float32),
            bf16(block_rows, width),
            bf16(block_rows, width),
            wide,
            wide,
        ],
        in_specs=[VMEM] * (10 + pairs),
        out_specs=[VMEM] * 6,
        scratch_shapes=[pltpu.VMEM((block_rows, width), jnp.bfloat16)],
        compiler_params=pltpu.CompilerParams(vmem_limit_bytes=12 * 2**20),
        cost_estimate=weighed(1e9),
        name="before_exchanges",
    )(upstream, queries, stats, tops, *own, grown_t, slopes_t, *previous_values)


def next_part(refs, later_query, group, heads, extra=None):
    k, nu, stats, later, bias = refs
    cols = [pl.ds(head * HEAD_DIM, HEAD_DIM) for head in group]
    scores = [by_rows(k[:, c], later_query[:, c]) * exp2_scale + bias[...] for c in cols]
    more = [extra(head) for head in group] if extra else None
    far = [stats[pl.ds(head, 1), :] for head in group]
    maxes = [jnp.maximum(f, jnp.max(x, axis=0, keepdims=True)) for f, x in zip(far, scores)]
    grown = [jnp.exp2(x - m) for x, m in zip(scores, maxes)]
    far = [jnp.exp2(f - m) for f, m in zip(far, maxes)]
    shares = [1.0 / (f + jnp.sum(x, axis=0, keepdims=True)) for f, x in zip(far, grown)]
    offsets = [
        y * (stats[pl.ds(heads + head, 1), :] * f + jnp.sum(x * later[head], axis=0, keepdims=True))
        for head, f, x, y in zip(group, far, grown, shares)
    ]
    chances = [x * y for x, y in zip(grown, shares)]
    weights = [x.astype(jnp.bfloat16) for x in chances]
    dscores = [(x * (later[head] - o)).astype(jnp.bfloat16) for x, head, o in zip(chances, group, offsets)]
    parts = [
        [product(weights[n], nu[:, c]), product(dscores[n], later_query[:, c])] for n, c in enumerate(cols)
    ]
    if more:
        parts = [[x + y for x, y in zip(*pair)] for pair in zip(parts, more)]
    return parts


def first_half(keys, first_got, next_upstream, first_stats, later, next_bias, past_refs):
    block_rows, width = keys.shape
    heads = width // HEAD_DIM
    past_count = len(past_refs)

    def kernel(k, first, nu, stats, later, next_bias, *rest):
        past_in, results = rest[:past_count], rest[past_count : past_count + 5]
        value_part, key_part = rest[past_count + 5 :]

        @pl.when(is_even())
        def _():
            for start in range(0, heads, GROUP):
                group = range(start, min(start + GROUP, heads))
                parts = next_part((k, nu, stats, later, next_bias), first, group, heads)
                for head, (value, key) in zip(group, parts):
                    columns = pl.ds(head * HEAD_DIM, HEAD_DIM)
                    value_part[:, columns] = value
                    key_part[:, columns] = key

        @pl.when(jnp.logical_not(is_even()))
        def _():
            for start in range(0, heads, GROUP):
                group = range(start, min(start + GROUP, heads))
                for head, part in zip(group, past_part(past_in, first, group, heads)):
                    columns = pl.ds(head * HEAD_DIM, HEAD_DIM)
                    results[0][:, columns], results[1][:, columns] = done_rows(past_in, part, head)
                    for target, rows in zip(results[2:], scaled_rows(past_in, part, head)):
                        target[head] = rows

    wide = jax.ShapeDtypeStruct((block_rows, width), jnp.float32)
    out = pl.pallas_call(
        kernel,
        out_shape=[bf16(block_rows, width)] * 2 + [bf16(heads, HEAD_DIM, block_rows)] * 3 + [wide] * 2,
        in_specs=[VMEM] * (6 + past_count),
        out_specs=[VMEM] * 7,
        compiler_params=pltpu.CompilerParams(vmem_limit_bytes=20 * 2**20),
        cost_estimate=weighed(0),
        name="first_half",
    )(keys, first_got, next_upstream, first_stats, later, next_bias, *past_refs)
    return out[:5], out[5:]


def second_half(keys, second_got, next_upstream, second_stats, later, next_bias, grown_t, slopes_t, past_refs, done, parts, early):
    block_rows, width = keys.shape
    heads = width // HEAD_DIM
    past_count = len(past_refs)

    def kernel(k, second, nu, stats, later, next_bias, grown_t, slopes_t, *rest):
        past_in, rest = rest[:past_count], rest[past_count:]
        done, (value_part, key_part), early, outs, rest = rest[:5], rest[5:7], rest[7:11], rest[11:15], rest[15:]
        attended, query_grads, key_grads, value_grads, sems = rest

        def send(rows, i, slot, columns=slice(None)):
            copy = pltpu.make_async_copy(rows.at[:, columns], outs[i].at[:, columns], sems.at[slot])
            copy.start()
            return copy

        def all_but_past():
            copies = [send(done[0], 0, 0), send(done[1], 1, 1)]
            for start in range(0, heads, PAIR):
                group = range(start, min(start + PAIR, heads))
                parts = next_part(
                    (k, nu, stats, later, next_bias), second, group, heads,
                    lambda head: own_gradients(grown_t, slopes_t, [rows[head] for rows in done[2:]], head),
                )
                for head, (value, key) in zip(group, parts):
                    columns = pl.ds(head * HEAD_DIM, HEAD_DIM)
                    value_grads[:, columns] = value.astype(jnp.bfloat16)
                    key_grads[:, columns] = (score_scale * key).astype(jnp.bfloat16)
                columns = pl.ds(start * HEAD_DIM, len(group) * HEAD_DIM)
                copies.append(send(key_grads, 2, len(copies), columns))
                copies.append(send(value_grads, 3, len(copies), columns))
            for copy in copies:
                copy.wait()

        def all_but_next(past_key):
            past = past_part(past_in, past_key, range(heads), heads)
            copies = []
            half = (heads + 1) // 2
            groups = (range(half), range(half, heads))

            def write_rows(group):
                for head in group:
                    columns = pl.ds(head * HEAD_DIM, HEAD_DIM)
                    attended[:, columns], query_grads[:, columns] = done_rows(past_in, past[head], head)
                columns = pl.ds(group.start * HEAD_DIM, len(group) * HEAD_DIM)
                copies.append(send(attended, 0, len(copies), columns))
                copies.append(send(query_grads, 1, len(copies), columns))

            def write_gradients(group):
                for head in group:
                    value, key = own_gradients(grown_t, slopes_t, scaled_rows(past_in, past[head], head), head)
                    columns = pl.ds(head * HEAD_DIM, HEAD_DIM)
                    value_grads[:, columns] = (value + value_part[:, columns]).astype(jnp.bfloat16)
                    key_grads[:, columns] = (score_scale * (key + key_part[:, columns])).astype(jnp.bfloat16)
                columns = pl.ds(group.start * HEAD_DIM, len(group) * HEAD_DIM)
                copies.append(send(key_grads, 2, len(copies), columns))
                copies.append(send(value_grads, 3, len(copies), columns))

            write_rows(groups[0])
            write_rows(groups[1])
            write_gradients(groups[0])
            write_gradients(groups[1])
            for copy in copies:
                copy.wait()

        block = lax.axis_index("blk")

        @pl.when(block == 0)
        def _():
            copies = [send(early[0], 0, 0), send(early[1], 1, 1)]
            value_grads[...] = (early[2][...] + value_part[...]).astype(jnp.bfloat16)
            key_grads[...] = (score_scale * (early[3][...] + key_part[...])).astype(jnp.bfloat16)
            copies += [send(key_grads, 2, 2), send(value_grads, 3, 3)]
            for copy in copies:
                copy.wait()

        @pl.when(jnp.logical_and(is_even(), block > 0))
        def _():
            all_but_next(second)

        @pl.when(jnp.logical_not(is_even()))
        def _():
            all_but_past()

    return pl.pallas_call(
        kernel,
        out_shape=[bf16(block_rows, width)] * 4,
        in_specs=[VMEM] * (19 + past_count),
        out_specs=[ANY] * 4,
        scratch_shapes=[pltpu.VMEM((block_rows, width), jnp.bfloat16)] * 4
        + [pltpu.SemaphoreType.DMA((4 * heads,))],
        compiler_params=pltpu.CompilerParams(vmem_limit_bytes=20 * 2**20),
        cost_estimate=weighed(0),
        name="second_half",
    )(
        keys, second_got, next_upstream, second_stats, later, next_bias, grown_t, slopes_t, *past_refs, *done, *parts, *early,
    )


def on_device(queries, key_states, value_states, upstream, clip_lengths):
    sharers = lax.axis_size("head")
    rows = queries.shape[0]
    pieces = cut_pieces(queries, key_states, value_states)
    pieces = [pieces[0]] + [partner_exchange(pieces[step], step) for step in range(1, sharers)]
    first, second = stack_values(pieces[0], pieces[1], upstream, rows)
    first_got, second_got = block_exchange(first, 0), block_exchange(second, 1)
    far_values, (own_bias, past_bias, next_bias) = stack_far_values(pieces[0], pieces[1], clip_lengths, rows)
    far_values = [partner_exchange(stack, 2 * pair + 2) for pair, stack in enumerate(far_values)]
    keys, query_rows, first, second = join_keys_queries(pieces, rows)
    previous, next_upstream = cut_previous_values(first_got, second_got, sharers // 2)
    first_got, second_got = block_exchange(first, 0), block_exchange(second, 1)
    previous = [partner_exchange(stack, 2 * pair) if pair else stack for pair, stack in enumerate(previous)]
    values, stats, tops, grown_t, slopes_t = own_scores(
        keys, query_rows, pieces[:2], far_values, upstream, own_bias, next_upstream
    )
    first_stats, second_stats = block_exchange(stats, 0), block_exchange(stats, 1)
    *own, later = own_products(keys, query_rows, upstream, values, grown_t, slopes_t, next_upstream)
    past_values, dchances, *early = before_exchanges(
        upstream, previous, query_rows, stats, tops, own, grown_t, slopes_t
    )
    past_refs = (query_rows, stats, tops, *own, past_values, dchances, past_bias)
    done, parts = first_half(keys, first_got, next_upstream, first_stats, later, next_bias, past_refs)
    return tuple(
        second_half(
            keys, second_got, next_upstream, second_stats, later, next_bias, grown_t, slopes_t, past_refs, done, parts,
            early,
        )
    )


def solution(mesh):
    return jax.shard_map(
        on_device,
        mesh=mesh,
        in_specs=(
            P(("dp", "blk", "head"), None),
            P(("dp", "blk", "head"), None),
            P(("dp", "blk", "head"), None),
            P(("dp", "blk"), "head"),
            P("dp"),
        ),
        out_specs=(
            P(("dp", "blk"), "head"),
            P(("dp", "blk"), "head"),
            P(("dp", "blk"), "head"),
            P(("dp", "blk"), "head"),
        ),
        check_vma=False,
    )
```

```python
import math

import jax
import jax.numpy as jnp
from jax import lax
from jax.experimental import pallas as pl
from jax.experimental.pallas import tpu as pltpu
from jax.sharding import PartitionSpec as P

HEAD_DIM = 128
GROUP = 4
PAIR = 2

masked_fill = -1e30
score_scale = HEAD_DIM ** (-0.5)
exp2_scale = score_scale * math.log2(math.e)

VMEM = pl.BlockSpec(memory_space=pltpu.VMEM)
SMEM = pl.BlockSpec(memory_space=pltpu.SMEM)
ANY = pl.BlockSpec(memory_space=pl.ANY)


def bf16(*shape):
    return jax.ShapeDtypeStruct(shape, jnp.bfloat16)


def partner_exchange(rows, step):
    route = [(i, i ^ step) for i in range(lax.axis_size("head"))]
    return lax.ppermute(rows, "head", route)


def sent_step(step, sharer):
    if step < 2:
        return step
    above = sharer // (1 << (step.bit_length() - 1)) % 2
    return step - step % 2 + (above if step % 2 == 0 else 1 - above)


def got_step(step, sharer):
    return step if step < 2 else sent_step(step ^ 1, sharer)


def pieces_exchange(rows, step):
    route = [(i, i ^ sent_step(step, i)) for i in range(lax.axis_size("head"))]
    return lax.ppermute(rows, "head", route)


def block_exchange(rows, parity):
    parts, blocks, sharers = lax.axis_size("dp"), lax.axis_size("blk"), lax.axis_size("head")
    route = []
    for part in range(parts):
        for block in range(blocks):
            other = block + 1 if block % 2 == parity else block - 1
            for sharer in range(sharers):
                here = (part * blocks + block) * sharers + sharer
                if 0 <= other < blocks:
                    route.append((here, (part * blocks + other) * sharers + sharer))
                else:
                    route.append((here, here ^ 1))
    return lax.ppermute(rows, ("dp", "blk", "head"), route)


def is_even():
    return lax.rem(lax.axis_index("blk"), 2) == 0


def place(step, size):
    owner = jnp.bitwise_xor(lax.axis_index("head"), step)
    return pl.ds(pl.multiple_of(owner * size, size), size)


def small_kernel():
    return pltpu.CompilerParams(vmem_limit_bytes=4 * 2**20)


def weighed(flops):
    return pl.CostEstimate(flops=int(flops), bytes_accessed=0, transcendentals=0)


def cut_pieces(queries, key_states, value_states):
    sharers = lax.axis_size("head")
    rows, features = queries.shape
    width = features // sharers
    heights = [(2 + sharers // 2) * rows if step < 2 else 2 * rows for step in range(sharers)]

    def kernel(q, k, v, *rest):
        pieces, sems = rest[:sharers], rest[sharers]
        copies = []

        def copy(source, target):
            copies.append(pltpu.make_async_copy(source, target, sems.at[len(copies)]))

        for step in range(sharers):
            columns = place(sent_step(step, lax.axis_index("head")), width)
            copy(k.at[:, columns], pieces[step].at[pl.ds(0, rows)])
            copy(q.at[:, columns], pieces[step].at[pl.ds(rows, rows)])
            copy(v.at[:, place(step, width)], pieces[step % 2].at[pl.ds((2 + step // 2) * rows, rows)])
        for c in copies:
            c.start()
        for c in copies:
            c.wait()

    return pl.pallas_call(
        kernel,
        out_shape=[bf16(height, width) for height in heights],
        in_specs=[ANY] * 3,
        out_specs=[VMEM] * sharers,
        scratch_shapes=[pltpu.SemaphoreType.DMA((3 * sharers,))],
        compiler_params=pltpu.CompilerParams(vmem_limit_bytes=53 * 2**20),
        name="cut_pieces",
    )(queries, key_states, value_states)


def stack_far_values(own, got, clip_lengths, rows):
    pairs = own.shape[0] // rows - 2
    width = own.shape[1]
    block_rows = 2 * pairs * rows

    def kernel(mine, theirs, lengths, own, past, ahead, *out):
        for pair in range(1, pairs):
            where = pl.ds((2 + pair) * rows, rows)
            out[pair - 1][pl.ds(0, rows), :] = mine[where, :]
            out[pair - 1][pl.ds(rows, rows), :] = theirs[where, :]
        block, blocks = lax.axis_index("blk"), lax.axis_size("blk")
        tall, wide = (block_rows, 1), (1, block_rows)
        key_ids, row_ids = clip_ids(lengths, tall, 0, block, blocks), clip_ids(lengths, wide, 1, block, blocks)
        own[...] = mask_bias(key_ids, row_ids)
        past[...] = mask_bias(clip_ids(lengths, tall, 0, block - 1, blocks), row_ids)
        ahead[...] = mask_bias(key_ids, clip_ids(lengths, wide, 1, block + 1, blocks))

    out = pl.pallas_call(
        kernel,
        out_shape=[jax.ShapeDtypeStruct((block_rows, block_rows), jnp.float32)] * 3
        + [bf16(2 * rows, width)] * (pairs - 1),
        in_specs=[VMEM] * 2 + [SMEM],
        out_specs=[VMEM] * (pairs + 2),
        compiler_params=small_kernel(),
        cost_estimate=weighed(5e9),
        name="stack_far_values",
    )(own, got, clip_lengths)
    return out[3:], out[:3]


def stack_values(own, got, upstream, rows):
    pairs = own.shape[0] // rows - 2
    width = own.shape[1]
    block_rows = upstream.shape[0]

    def kernel(mine, theirs, u, first, second):
        def spread(forward, backward):
            for pair in range(pairs):
                where = pl.ds((2 + pair) * rows, rows)
                forward[pl.ds(2 * pair * rows, rows), :] = mine[where, :]
                forward[pl.ds((2 * pair + 1) * rows, rows), :] = theirs[where, :]
            backward[...] = u[...]

        @pl.when(is_even())
        def _():
            spread(first, second)

        @pl.when(jnp.logical_not(is_even()))
        def _():
            spread(second, first)

    return pl.pallas_call(
        kernel,
        out_shape=[bf16(block_rows, width)] * 2,
        in_specs=[VMEM] * 3,
        out_specs=[VMEM] * 2,
        compiler_params=small_kernel(),
        cost_estimate=weighed(0),
        name="stack_values",
    )(own, got, upstream)


def join_keys_queries(pieces, rows):
    sharers = len(pieces)
    width = pieces[0].shape[1]
    block_rows = rows * sharers

    def kernel(*refs):
        pieces_in = refs[:sharers]
        keys, queries, first, second = refs[sharers:]
        for step in range(sharers):
            where = place(got_step(step, lax.axis_index("head")), rows)
            keys[where, :] = pieces_in[step][pl.ds(0, rows), :]
            queries[where, :] = pieces_in[step][pl.ds(rows, rows), :]

        @pl.when(is_even())
        def _():
            first[...] = keys[...]
            second[...] = queries[...]

        @pl.when(jnp.logical_not(is_even()))
        def _():
            first[...] = queries[...]
            second[...] = keys[...]

    return pl.pallas_call(
        kernel,
        out_shape=[bf16(block_rows, width)] * 4,
        in_specs=[VMEM] * sharers,
        out_specs=[VMEM] * 4,
        compiler_params=small_kernel(),
        cost_estimate=weighed(0),
        name="join_keys_queries",
    )(*pieces)


def cut_previous_values(first_got, second_got, pairs):
    block_rows, width = first_got.shape
    rows = block_rows // pairs

    def kernel(first, second, *out):
        def split(forward, backward):
            for pair in range(pairs):
                out[pair][...] = forward[pl.ds(pair * rows, rows), :]
            out[pairs][...] = backward[...]

        @pl.when(is_even())
        def _():
            split(second, first)

        @pl.when(jnp.logical_not(is_even()))
        def _():
            split(first, second)

    out = pl.pallas_call(
        kernel,
        out_shape=[bf16(rows, width)] * pairs + [bf16(block_rows, width)],
        in_specs=[VMEM] * 2,
        out_specs=[VMEM] * (pairs + 1),
        compiler_params=small_kernel(),
        cost_estimate=weighed(0),
        name="cut_previous_values",
    )(first_got, second_got)
    return out[:pairs], out[pairs]


def clip_ids(lengths, shape, axis, block, blocks):
    position = block * shape[axis] + lax.broadcasted_iota(jnp.int32, shape, axis)
    ids, end = jnp.zeros(shape, jnp.int32), jnp.int32(0)
    for clip in range(lengths.shape[0]):
        end = end + lengths[clip]
        ids = ids + (position >= end).astype(jnp.int32)
    return jnp.where(jnp.logical_and(block >= 0, block < blocks), ids, -1)


def mask_bias(key_ids, query_ids):
    return jnp.where(key_ids == query_ids, 0.0, masked_fill).astype(jnp.float32)


def by_rows(a, b):
    return lax.dot_general(a, b, (((1,), (1,)), ((), ())), preferred_element_type=jnp.float32)


def by_columns(a, b):
    return lax.dot_general(a, b, (((0,), (0,)), ((), ())), preferred_element_type=jnp.float32)


def product(a, b):
    return jnp.dot(a, b, preferred_element_type=jnp.float32)


def own_scores(keys, queries, chip_values, far_values, upstream, bias, after):
    sharers = 2 + 2 * len(far_values)
    block_rows, width = keys.shape
    rows = block_rows // sharers
    heads = width // HEAD_DIM

    def kernel(k, q, u, bias, _, *rest):
        values_in = [ref.at[pl.ds(2 * rows, rows)] for ref in rest[:2]]
        for ref in rest[2 : 1 + sharers // 2]:
            values_in += [ref.at[pl.ds(0, rows)], ref.at[pl.ds(rows, rows)]]
        values, stats, tops, grown_t, slopes_t = rest[1 + sharers // 2 :]
        for step in range(sharers):
            values[place(step, rows), :] = values_in[step][...]
        for start in range(0, heads, GROUP):
            group = range(start, min(start + GROUP, heads))
            cols = [pl.ds(head * HEAD_DIM, HEAD_DIM) for head in group]
            scores = [by_rows(k[:, c], q[:, c]) * exp2_scale + bias[...] for c in cols]
            maxes = [jnp.max(x, axis=0, keepdims=True) for x in scores]
            grown = [jnp.exp2(x - m) for x, m in zip(scores, maxes)]
            totals = [jnp.sum(x, axis=0, keepdims=True) for x in grown]
            dchances = [by_rows(values[:, c], u[:, c]) for c in cols]
            offsets = [
                jnp.sum(x * d, axis=0, keepdims=True) / total for x, d, total in zip(grown, dchances, totals)
            ]
            for n, head in enumerate(group):
                stats[pl.ds(head, 1), :] = maxes[n] + jnp.log2(totals[n])
                stats[pl.ds(heads + head, 1), :] = offsets[n]
                tops[pl.ds(head, 1), :] = maxes[n]
                grown_t[head] = grown[n].astype(jnp.bfloat16)
                slopes_t[head] = (grown[n] * (dchances[n] - offsets[n])).astype(jnp.bfloat16)

    square = bf16(heads, block_rows, block_rows)
    return pl.pallas_call(
        kernel,
        out_shape=[
            bf16(block_rows, width),
            jax.ShapeDtypeStruct((2 * heads, block_rows), jnp.float32),
            jax.ShapeDtypeStruct((heads, block_rows), jnp.float32),
            square,
            square,
        ],
        in_specs=[VMEM] * (6 + sharers // 2),
        out_specs=[VMEM] * 5,
        compiler_params=pltpu.CompilerParams(vmem_limit_bytes=12 * 2**20),
        cost_estimate=weighed(0),
        name="own_scores",
    )(keys, queries, upstream, bias, after, *chip_values, *far_values)


def own_products(keys, queries, upstream, values, grown_t, slopes_t, next_upstream):
    block_rows, width = keys.shape
    heads = width // HEAD_DIM

    def kernel(k, q, u, v, grown_t, slopes_t, nu, sums, slope_keys, query_t, up_t, later):
        for head in range(heads):
            columns = pl.ds(head * HEAD_DIM, HEAD_DIM)
            key, value = k[:, columns], v[:, columns]
            sums[head] = by_columns(jnp.concatenate([value, key], axis=1), grown_t[head])
            slope_keys[head] = by_columns(key, slopes_t[head])
            query_t[head] = jnp.transpose(q[:, columns]).astype(jnp.float32)
            up_t[head] = jnp.transpose(u[:, columns]).astype(jnp.float32)
            later[head] = by_rows(value, nu[:, columns])

    def turned(tall):
        return jax.ShapeDtypeStruct((heads, tall, block_rows), jnp.float32)

    return pl.pallas_call(
        kernel,
        out_shape=[turned(2 * HEAD_DIM)] + [turned(HEAD_DIM)] * 3 + [turned(block_rows)],
        in_specs=[VMEM] * 7,
        out_specs=[VMEM] * 5,
        compiler_params=pltpu.CompilerParams(vmem_limit_bytes=16 * 2**20),
        cost_estimate=weighed(1e9),
        name="own_products",
    )(keys, queries, upstream, values, grown_t, slopes_t, next_upstream)


def past_part(refs, past_key, group, heads):
    q, own_stats, tops, _, _, _, _, pv, dchances, bias = refs
    cols = [pl.ds(head * HEAD_DIM, HEAD_DIM) for head in group]
    tops = [tops[pl.ds(head, 1), :] for head in group]
    own_norms = [own_stats[pl.ds(head, 1), :] for head in group]
    own_offsets = [own_stats[pl.ds(heads + head, 1), :] for head in group]
    if past_key is None:
        return [(jnp.exp2(top - norm), None, None) for top, norm in zip(tops, own_norms)]
    keys = [past_key[:, c] for c in cols]
    scores = [by_rows(key, q[:, c]) * exp2_scale + bias[...] for key, c in zip(keys, cols)]
    maxes = [jnp.maximum(top, jnp.max(x, axis=0, keepdims=True)) for top, x in zip(tops, scores)]
    grown = [jnp.exp2(x - m) for x, m in zip(scores, maxes)]
    own = [jnp.exp2(norm - m) for norm, m in zip(own_norms, maxes)]
    shares = [1.0 / (o + jnp.sum(x, axis=0, keepdims=True)) for o, x in zip(own, grown)]
    offsets = [
        y * (offset * o + jnp.sum(x * dchances[head], axis=0, keepdims=True))
        for head, offset, o, x, y in zip(group, own_offsets, own, grown, shares)
    ]
    factors = [jnp.exp2(top - m) * y for top, m, y in zip(tops, maxes, shares)]
    shifts = [f * (o - offset) for f, o, offset in zip(factors, offsets, own_offsets)]
    chances = [x * y for x, y in zip(grown, shares)]
    weights = [x.astype(jnp.bfloat16) for x in chances]
    dscores = [(x * (dchances[head] - o)).astype(jnp.bfloat16) for x, head, o in zip(chances, group, offsets)]
    return list(zip(factors, shifts, zip(weights, dscores, keys)))


def scaled_rows(refs, part, head):
    _, _, _, _, _, query_t, up_t, _, _, _ = refs
    factor, shift, _ = part
    query, up = query_t[head], up_t[head]
    if shift is None:
        shifted = jnp.zeros(query.shape, jnp.bfloat16)
    else:
        shifted = (query * -shift).astype(jnp.bfloat16)
    return (query * factor).astype(jnp.bfloat16), shifted, (up * factor).astype(jnp.bfloat16)


def done_rows(refs, part, head):
    _, _, _, sums, slope_keys, _, _, pv, _, _ = refs
    factor, shift, past = part
    attended, grads = factor * sums[head, :HEAD_DIM], factor * slope_keys[head]
    if past is not None:
        weights, dscores, key = past
        attended = attended + product(pv[head], weights)
        grads = grads - shift * sums[head, HEAD_DIM:] + by_columns(key, dscores)
    return (
        jnp.transpose(attended.astype(jnp.bfloat16)),
        jnp.transpose((score_scale * grads).astype(jnp.bfloat16)),
    )


def own_gradients(grown_t, slopes_t, scaled, head):
    scaled_query, shifted_query, scaled_up = scaled
    mixed = by_rows(grown_t[head], jnp.concatenate([scaled_up, shifted_query], axis=0))
    return mixed[:, :HEAD_DIM], mixed[:, HEAD_DIM:] + by_rows(slopes_t[head], scaled_query)


def before_exchanges(upstream, previous_values, queries, stats, tops, own, grown_t, slopes_t):
    pairs = len(previous_values)
    block_rows, width = upstream.shape
    rows = block_rows // pairs // 2
    heads = width // HEAD_DIM

    def kernel(u, q, own_stats, tops, sums, slope_keys, query_t, up_t, grown_t, slopes_t, *rest):
        pieces, (turned, dchances, attended, query_grads, value_own, key_own, values) = rest[:pairs], rest[pairs:]
        first = lax.axis_index("blk") == 0

        @pl.when(jnp.logical_not(first))
        def _():
            for step in range(2 * pairs):
                values[place(step, rows), :] = pieces[step // 2][pl.ds(step % 2 * rows, rows), :]
            for head in range(heads):
                columns = pl.ds(head * HEAD_DIM, HEAD_DIM)
                dchances[head] = by_rows(values[:, columns], u[:, columns])
                turned[head] = jnp.transpose(values[:, columns])

        @pl.when(first)
        def _():
            refs = (q, own_stats, tops, sums, slope_keys, query_t, up_t, turned, dchances, None)
            for head, part in enumerate(past_part(refs, None, range(heads), heads)):
                columns = pl.ds(head * HEAD_DIM, HEAD_DIM)
                attended[:, columns], query_grads[:, columns] = done_rows(refs, part, head)
                value_own[:, columns], key_own[:, columns] = own_gradients(
                    grown_t, slopes_t, scaled_rows(refs, part, head), head
                )

    wide = jax.ShapeDtypeStruct((block_rows, width), jnp.float32)
    return pl.pallas_call(
        kernel,
        out_shape=[
            bf16(heads, HEAD_DIM, block_rows),
            jax.ShapeDtypeStruct((heads, block_rows, block_rows), jnp.float32),
            bf16(block_rows, width),
            bf16(block_rows, width),
            wide,
            wide,
        ],
        in_specs=[VMEM] * (10 + pairs),
        out_specs=[VMEM] * 6,
        scratch_shapes=[pltpu.VMEM((block_rows, width), jnp.bfloat16)],
        compiler_params=pltpu.CompilerParams(vmem_limit_bytes=12 * 2**20),
        cost_estimate=weighed(1e9),
        name="before_exchanges",
    )(upstream, queries, stats, tops, *own, grown_t, slopes_t, *previous_values)


def next_part(refs, later_query, group, heads, extra=None):
    k, nu, stats, later, bias = refs
    cols = [pl.ds(head * HEAD_DIM, HEAD_DIM) for head in group]
    scores = [by_rows(k[:, c], later_query[:, c]) * exp2_scale + bias[...] for c in cols]
    more = [extra(head) for head in group] if extra else None
    far = [stats[pl.ds(head, 1), :] for head in group]
    maxes = [jnp.maximum(f, jnp.max(x, axis=0, keepdims=True)) for f, x in zip(far, scores)]
    grown = [jnp.exp2(x - m) for x, m in zip(scores, maxes)]
    far = [jnp.exp2(f - m) for f, m in zip(far, maxes)]
    shares = [1.0 / (f + jnp.sum(x, axis=0, keepdims=True)) for f, x in zip(far, grown)]
    offsets = [
        y * (stats[pl.ds(heads + head, 1), :] * f + jnp.sum(x * later[head], axis=0, keepdims=True))
        for head, f, x, y in zip(group, far, grown, shares)
    ]
    chances = [x * y for x, y in zip(grown, shares)]
    weights = [x.astype(jnp.bfloat16) for x in chances]
    dscores = [(x * (later[head] - o)).astype(jnp.bfloat16) for x, head, o in zip(chances, group, offsets)]
    parts = [
        [product(weights[n], nu[:, c]), product(dscores[n], later_query[:, c])] for n, c in enumerate(cols)
    ]
    if more:
        parts = [[x + y for x, y in zip(*pair)] for pair in zip(parts, more)]
    return parts


def first_half(keys, first_got, next_upstream, first_stats, later, next_bias, past_refs):
    block_rows, width = keys.shape
    heads = width // HEAD_DIM
    past_count = len(past_refs)

    def kernel(k, first, nu, stats, later, next_bias, *rest):
        past_in, results = rest[:past_count], rest[past_count : past_count + 5]
        value_part, key_part = rest[past_count + 5 :]

        @pl.when(is_even())
        def _():
            for start in range(0, heads, GROUP):
                group = range(start, min(start + GROUP, heads))
                parts = next_part((k, nu, stats, later, next_bias), first, group, heads)
                for head, (value, key) in zip(group, parts):
                    columns = pl.ds(head * HEAD_DIM, HEAD_DIM)
                    value_part[:, columns] = value
                    key_part[:, columns] = key

        @pl.when(jnp.logical_not(is_even()))
        def _():
            for start in range(0, heads, GROUP):
                group = range(start, min(start + GROUP, heads))
                for head, part in zip(group, past_part(past_in, first, group, heads)):
                    columns = pl.ds(head * HEAD_DIM, HEAD_DIM)
                    results[0][:, columns], results[1][:, columns] = done_rows(past_in, part, head)
                    for target, rows in zip(results[2:], scaled_rows(past_in, part, head)):
                        target[head] = rows

    wide = jax.ShapeDtypeStruct((block_rows, width), jnp.float32)
    out = pl.pallas_call(
        kernel,
        out_shape=[bf16(block_rows, width)] * 2 + [bf16(heads, HEAD_DIM, block_rows)] * 3 + [wide] * 2,
        in_specs=[VMEM] * (6 + past_count),
        out_specs=[VMEM] * 7,
        compiler_params=pltpu.CompilerParams(vmem_limit_bytes=20 * 2**20),
        cost_estimate=weighed(0),
        name="first_half",
    )(keys, first_got, next_upstream, first_stats, later, next_bias, *past_refs)
    return out[:5], out[5:]


def second_half(keys, second_got, next_upstream, second_stats, later, next_bias, grown_t, slopes_t, past_refs, done, parts, early):
    block_rows, width = keys.shape
    heads = width // HEAD_DIM
    past_count = len(past_refs)

    def kernel(k, second, nu, stats, later, next_bias, grown_t, slopes_t, *rest):
        past_in, rest = rest[:past_count], rest[past_count:]
        done, (value_part, key_part), early, outs, rest = rest[:5], rest[5:7], rest[7:11], rest[11:15], rest[15:]
        attended, query_grads, key_grads, value_grads, sems = rest

        def send(rows, i, slot, columns=slice(None)):
            copy = pltpu.make_async_copy(rows.at[:, columns], outs[i].at[:, columns], sems.at[slot])
            copy.start()
            return copy

        def all_but_past():
            copies = [send(done[0], 0, 0), send(done[1], 1, 1)]
            for start in range(0, heads, PAIR):
                group = range(start, min(start + PAIR, heads))
                parts = next_part(
                    (k, nu, stats, later, next_bias), second, group, heads,
                    lambda head: own_gradients(grown_t, slopes_t, [rows[head] for rows in done[2:]], head),
                )
                for head, (value, key) in zip(group, parts):
                    columns = pl.ds(head * HEAD_DIM, HEAD_DIM)
                    value_grads[:, columns] = value.astype(jnp.bfloat16)
                    key_grads[:, columns] = (score_scale * key).astype(jnp.bfloat16)
                columns = pl.ds(start * HEAD_DIM, len(group) * HEAD_DIM)
                copies.append(send(key_grads, 2, len(copies), columns))
                copies.append(send(value_grads, 3, len(copies), columns))
            for copy in copies:
                copy.wait()

        def all_but_next(past_key):
            past = past_part(past_in, past_key, range(heads), heads)
            copies = []
            half = (heads + 1) // 2
            groups = (range(half), range(half, heads))

            def write_rows(group):
                for head in group:
                    columns = pl.ds(head * HEAD_DIM, HEAD_DIM)
                    attended[:, columns], query_grads[:, columns] = done_rows(past_in, past[head], head)
                columns = pl.ds(group.start * HEAD_DIM, len(group) * HEAD_DIM)
                copies.append(send(attended, 0, len(copies), columns))
                copies.append(send(query_grads, 1, len(copies), columns))

            def write_gradients(group):
                for head in group:
                    value, key = own_gradients(grown_t, slopes_t, scaled_rows(past_in, past[head], head), head)
                    columns = pl.ds(head * HEAD_DIM, HEAD_DIM)
                    value_grads[:, columns] = (value + value_part[:, columns]).astype(jnp.bfloat16)
                    key_grads[:, columns] = (score_scale * (key + key_part[:, columns])).astype(jnp.bfloat16)
                columns = pl.ds(group.start * HEAD_DIM, len(group) * HEAD_DIM)
                copies.append(send(key_grads, 2, len(copies), columns))
                copies.append(send(value_grads, 3, len(copies), columns))

            write_rows(groups[0])
            write_rows(groups[1])
            write_gradients(groups[0])
            write_gradients(groups[1])
            for copy in copies:
                copy.wait()

        block = lax.axis_index("blk")

        @pl.when(block == 0)
        def _():
            copies = [send(early[0], 0, 0), send(early[1], 1, 1)]
            value_grads[...] = (early[2][...] + value_part[...]).astype(jnp.bfloat16)
            key_grads[...] = (score_scale * (early[3][...] + key_part[...])).astype(jnp.bfloat16)
            copies += [send(key_grads, 2, 2), send(value_grads, 3, 3)]
            for copy in copies:
                copy.wait()

        @pl.when(jnp.logical_and(is_even(), block > 0))
        def _():
            all_but_next(second)

        @pl.when(jnp.logical_not(is_even()))
        def _():
            all_but_past()

    return pl.pallas_call(
        kernel,
        out_shape=[bf16(block_rows, width)] * 4,
        in_specs=[VMEM] * (19 + past_count),
        out_specs=[ANY] * 4,
        scratch_shapes=[pltpu.VMEM((block_rows, width), jnp.bfloat16)] * 4
        + [pltpu.SemaphoreType.DMA((4 * heads,))],
        compiler_params=pltpu.CompilerParams(vmem_limit_bytes=20 * 2**20),
        cost_estimate=weighed(0),
        name="second_half",
    )(
        keys, second_got, next_upstream, second_stats, later, next_bias, grown_t, slopes_t, *past_refs, *done, *parts, *early,
    )


def on_device(queries, key_states, value_states, upstream, clip_lengths):
    sharers = lax.axis_size("head")
    rows = queries.shape[0]
    pieces = cut_pieces(queries, key_states, value_states)
    pieces = [pieces[0]] + [pieces_exchange(pieces[step], step) for step in range(1, sharers)]
    first, second = stack_values(pieces[0], pieces[1], upstream, rows)
    first_got, second_got = block_exchange(first, 0), block_exchange(second, 1)
    far_values, (own_bias, past_bias, next_bias) = stack_far_values(pieces[0], pieces[1], clip_lengths, rows)
    far_values = [partner_exchange(stack, 2 * pair + 2) for pair, stack in enumerate(far_values)]
    keys, query_rows, first, second = join_keys_queries(pieces, rows)
    previous, next_upstream = cut_previous_values(first_got, second_got, sharers // 2)
    first_got, second_got = block_exchange(first, 0), block_exchange(second, 1)
    previous = [partner_exchange(stack, 2 * pair) if pair else stack for pair, stack in enumerate(previous)]
    values, stats, tops, grown_t, slopes_t = own_scores(
        keys, query_rows, pieces[:2], far_values, upstream, own_bias, next_upstream
    )
    first_stats, second_stats = block_exchange(stats, 0), block_exchange(stats, 1)
    *own, later = own_products(keys, query_rows, upstream, values, grown_t, slopes_t, next_upstream)
    past_values, dchances, *early = before_exchanges(
        upstream, previous, query_rows, stats, tops, own, grown_t, slopes_t
    )
    past_refs = (query_rows, stats, tops, *own, past_values, dchances, past_bias)
    done, parts = first_half(keys, first_got, next_upstream, first_stats, later, next_bias, past_refs)
    return tuple(
        second_half(
            keys, second_got, next_upstream, second_stats, later, next_bias, grown_t, slopes_t, past_refs, done, parts,
            early,
        )
    )


def solution(mesh):
    return jax.shard_map(
        on_device,
        mesh=mesh,
        in_specs=(
            P(("dp", "blk", "head"), None),
            P(("dp", "blk", "head"), None),
            P(("dp", "blk", "head"), None),
            P(("dp", "blk"), "head"),
            P("dp"),
        ),
        out_specs=(
            P(("dp", "blk"), "head"),
            P(("dp", "blk"), "head"),
            P(("dp", "blk"), "head"),
            P(("dp", "blk"), "head"),
        ),
        check_vma=False,
    )
```

```python
import math

import jax
import jax.numpy as jnp
from jax import lax
from jax.experimental import pallas as pl
from jax.experimental.pallas import tpu as pltpu
from jax.sharding import PartitionSpec as P

HEAD_DIM = 128
GROUP = 4
PAIR = 2

masked_fill = -1e30
score_scale = HEAD_DIM ** (-0.5)
exp2_scale = score_scale * math.log2(math.e)

VMEM = pl.BlockSpec(memory_space=pltpu.VMEM)
SMEM = pl.BlockSpec(memory_space=pltpu.SMEM)
ANY = pl.BlockSpec(memory_space=pl.ANY)


def bf16(*shape):
    return jax.ShapeDtypeStruct(shape, jnp.bfloat16)


def partner_exchange(rows, step):
    route = [(i, i ^ step) for i in range(lax.axis_size("head"))]
    return lax.ppermute(rows, "head", route)


def block_exchange(rows, parity):
    parts, blocks, sharers = lax.axis_size("dp"), lax.axis_size("blk"), lax.axis_size("head")
    route = []
    for part in range(parts):
        for block in range(blocks):
            other = block + 1 if block % 2 == parity else block - 1
            for sharer in range(sharers):
                here = (part * blocks + block) * sharers + sharer
                if 0 <= other < blocks:
                    route.append((here, (part * blocks + other) * sharers + sharer))
                else:
                    route.append((here, here ^ 1))
    return lax.ppermute(rows, ("dp", "blk", "head"), route)


def is_even():
    return lax.rem(lax.axis_index("blk"), 2) == 0


def place(step, size):
    owner = jnp.bitwise_xor(lax.axis_index("head"), step)
    return pl.ds(pl.multiple_of(owner * size, size), size)


def small_kernel():
    return pltpu.CompilerParams(vmem_limit_bytes=4 * 2**20)


def weighed(flops):
    return pl.CostEstimate(flops=int(flops), bytes_accessed=0, transcendentals=0)


def cut_pieces(queries, key_states, value_states):
    sharers = lax.axis_size("head")
    rows, features = queries.shape
    width = features // sharers
    heights = [(2 + sharers // 2) * rows if step == 1 else 2 * rows for step in range(1, sharers)]

    def kernel(q, k, v, *rest):
        pieces, sems = rest[: sharers - 1], rest[sharers - 1]
        copies = []

        def copy(source, target):
            copies.append(pltpu.make_async_copy(source, target, sems.at[len(copies)]))

        for step in range(1, sharers):
            columns = place(step, width)
            copy(k.at[:, columns], pieces[step - 1].at[pl.ds(0, rows)])
            copy(q.at[:, columns], pieces[step - 1].at[pl.ds(rows, rows)])
            if step % 2:
                copy(v.at[:, columns], pieces[0].at[pl.ds((2 + step // 2) * rows, rows)])
        for c in copies:
            c.start()
        for c in copies:
            c.wait()

    return pl.pallas_call(
        kernel,
        out_shape=[bf16(height, width) for height in heights],
        in_specs=[ANY] * 3,
        out_specs=[VMEM] * (sharers - 1),
        scratch_shapes=[pltpu.SemaphoreType.DMA((3 * sharers,))],
        compiler_params=pltpu.CompilerParams(vmem_limit_bytes=int(53.25 * 2**20)),
        name="cut_pieces",
    )(queries, key_states, value_states)


def stack_far_values(own_values, got, clip_lengths, rows):
    pairs = got.shape[0] // rows - 2
    width = got.shape[1]
    block_rows = 2 * pairs * rows

    def kernel(mine, theirs, lengths, own, past, ahead, *out):
        for pair in range(1, pairs):
            out[pair - 1][pl.ds(0, rows), :] = mine[:, place(2 * pair, width)]
            out[pair - 1][pl.ds(rows, rows), :] = theirs[pl.ds((2 + pair) * rows, rows), :]
        block, blocks = lax.axis_index("blk"), lax.axis_size("blk")
        tall, wide = (block_rows, 1), (1, block_rows)
        key_ids, row_ids = clip_ids(lengths, tall, 0, block, blocks), clip_ids(lengths, wide, 1, block, blocks)
        own[...] = mask_bias(key_ids, row_ids)
        past[...] = mask_bias(clip_ids(lengths, tall, 0, block - 1, blocks), row_ids)
        ahead[...] = mask_bias(key_ids, clip_ids(lengths, wide, 1, block + 1, blocks))

    out = pl.pallas_call(
        kernel,
        out_shape=[jax.ShapeDtypeStruct((block_rows, block_rows), jnp.float32)] * 3
        + [bf16(2 * rows, width)] * (pairs - 1),
        in_specs=[VMEM] * 2 + [SMEM],
        out_specs=[VMEM] * (pairs + 2),
        compiler_params=small_kernel(),
        cost_estimate=weighed(5e9),
        name="stack_far_values",
    )(own_values, got, clip_lengths)
    return out[3:], out[:3]


def stack_values(own_values, got, upstream, rows):
    pairs = got.shape[0] // rows - 2
    width = got.shape[1]
    block_rows = upstream.shape[0]

    def kernel(mine, theirs, u, first, second):
        def spread(forward, backward):
            for pair in range(pairs):
                where = pl.ds((2 + pair) * rows, rows)
                forward[pl.ds(2 * pair * rows, rows), :] = mine[:, place(2 * pair, width)]
                forward[pl.ds((2 * pair + 1) * rows, rows), :] = theirs[where, :]
            backward[...] = u[...]

        @pl.when(is_even())
        def _():
            spread(first, second)

        @pl.when(jnp.logical_not(is_even()))
        def _():
            spread(second, first)

    return pl.pallas_call(
        kernel,
        out_shape=[bf16(block_rows, width)] * 2,
        in_specs=[VMEM] * 3,
        out_specs=[VMEM] * 2,
        compiler_params=small_kernel(),
        cost_estimate=weighed(0),
        name="stack_values",
    )(own_values, got, upstream)


def join_keys_queries(key_states, own_queries, pieces):
    sharers = len(pieces) + 1
    rows, width = key_states.shape[0], pieces[0].shape[1]
    block_rows = rows * sharers

    def kernel(k, q, *refs):
        pieces_in = refs[: sharers - 1]
        keys, queries, first, second = refs[sharers - 1 :]
        keys[place(0, rows), :] = k[:, place(0, width)]
        queries[place(0, rows), :] = q[:, place(0, width)]
        for step in range(1, sharers):
            where = place(step, rows)
            keys[where, :] = pieces_in[step - 1][pl.ds(0, rows), :]
            queries[where, :] = pieces_in[step - 1][pl.ds(rows, rows), :]

        @pl.when(is_even())
        def _():
            first[...] = keys[...]
            second[...] = queries[...]

        @pl.when(jnp.logical_not(is_even()))
        def _():
            first[...] = queries[...]
            second[...] = keys[...]

    return pl.pallas_call(
        kernel,
        out_shape=[bf16(block_rows, width)] * 4,
        in_specs=[VMEM] * (sharers + 1),
        out_specs=[VMEM] * 4,
        compiler_params=small_kernel(),
        cost_estimate=weighed(0),
        name="join_keys_queries",
    )(key_states, own_queries, *pieces)


def cut_previous_values(first_got, second_got, pairs):
    block_rows, width = first_got.shape
    rows = block_rows // pairs

    def kernel(first, second, *out):
        def split(forward, backward):
            for pair in range(pairs):
                out[pair][...] = forward[pl.ds(pair * rows, rows), :]
            out[pairs][...] = backward[...]

        @pl.when(is_even())
        def _():
            split(second, first)

        @pl.when(jnp.logical_not(is_even()))
        def _():
            split(first, second)

    out = pl.pallas_call(
        kernel,
        out_shape=[bf16(rows, width)] * pairs + [bf16(block_rows, width)],
        in_specs=[VMEM] * 2,
        out_specs=[VMEM] * (pairs + 1),
        compiler_params=small_kernel(),
        cost_estimate=weighed(0),
        name="cut_previous_values",
    )(first_got, second_got)
    return out[:pairs], out[pairs]


def clip_ids(lengths, shape, axis, block, blocks):
    position = block * shape[axis] + lax.broadcasted_iota(jnp.int32, shape, axis)
    ids, end = jnp.zeros(shape, jnp.int32), jnp.int32(0)
    for clip in range(lengths.shape[0]):
        end = end + lengths[clip]
        ids = ids + (position >= end).astype(jnp.int32)
    return jnp.where(jnp.logical_and(block >= 0, block < blocks), ids, -1)


def mask_bias(key_ids, query_ids):
    return jnp.where(key_ids == query_ids, 0.0, masked_fill).astype(jnp.float32)


def by_rows(a, b):
    return lax.dot_general(a, b, (((1,), (1,)), ((), ())), preferred_element_type=jnp.float32)


def by_columns(a, b):
    return lax.dot_general(a, b, (((0,), (0,)), ((), ())), preferred_element_type=jnp.float32)


def product(a, b):
    return jnp.dot(a, b, preferred_element_type=jnp.float32)


def own_scores(keys, queries, chip_values, far_values, upstream, bias, after):
    sharers = 2 + 2 * len(far_values)
    block_rows, width = keys.shape
    rows = block_rows // sharers
    heads = width // HEAD_DIM

    def kernel(k, q, u, bias, _, *rest):
        values_in = [rest[0].at[:, place(0, width)], rest[1].at[pl.ds(2 * rows, rows)]]
        for ref in rest[2 : 1 + sharers // 2]:
            values_in += [ref.at[pl.ds(0, rows)], ref.at[pl.ds(rows, rows)]]
        values, stats, tops, grown_t, slopes_t = rest[1 + sharers // 2 :]
        for step in range(sharers):
            values[place(step, rows), :] = values_in[step][...]
        for start in range(0, heads, GROUP):
            group = range(start, min(start + GROUP, heads))
            cols = [pl.ds(head * HEAD_DIM, HEAD_DIM) for head in group]
            scores = [by_rows(k[:, c], q[:, c]) * exp2_scale + bias[...] for c in cols]
            maxes = [jnp.max(x, axis=0, keepdims=True) for x in scores]
            grown = [jnp.exp2(x - m) for x, m in zip(scores, maxes)]
            totals = [jnp.sum(x, axis=0, keepdims=True) for x in grown]
            dchances = [by_rows(values[:, c], u[:, c]) for c in cols]
            offsets = [
                jnp.sum(x * d, axis=0, keepdims=True) / total for x, d, total in zip(grown, dchances, totals)
            ]
            for n, head in enumerate(group):
                stats[pl.ds(head, 1), :] = maxes[n] + jnp.log2(totals[n])
                stats[pl.ds(heads + head, 1), :] = offsets[n]
                tops[pl.ds(head, 1), :] = maxes[n]
                grown_t[head] = grown[n].astype(jnp.bfloat16)
                slopes_t[head] = (grown[n] * (dchances[n] - offsets[n])).astype(jnp.bfloat16)

    square = bf16(heads, block_rows, block_rows)
    return pl.pallas_call(
        kernel,
        out_shape=[
            bf16(block_rows, width),
            jax.ShapeDtypeStruct((2 * heads, block_rows), jnp.float32),
            jax.ShapeDtypeStruct((heads, block_rows), jnp.float32),
            square,
            square,
        ],
        in_specs=[VMEM] * (6 + sharers // 2),
        out_specs=[VMEM] * 5,
        compiler_params=pltpu.CompilerParams(vmem_limit_bytes=12 * 2**20),
        cost_estimate=weighed(0),
        name="own_scores",
    )(keys, queries, upstream, bias, after, *chip_values, *far_values)


def own_products(keys, queries, upstream, values, grown_t, slopes_t, next_upstream):
    block_rows, width = keys.shape
    heads = width // HEAD_DIM

    def kernel(k, q, u, v, grown_t, slopes_t, nu, sums, slope_keys, query_t, up_t, later):
        for head in range(heads):
            columns = pl.ds(head * HEAD_DIM, HEAD_DIM)
            key, value = k[:, columns], v[:, columns]
            sums[head] = by_columns(jnp.concatenate([value, key], axis=1), grown_t[head])
            slope_keys[head] = by_columns(key, slopes_t[head])
            query_t[head] = jnp.transpose(q[:, columns]).astype(jnp.float32)
            up_t[head] = jnp.transpose(u[:, columns]).astype(jnp.float32)
            later[head] = by_rows(value, nu[:, columns])

    def turned(tall):
        return jax.ShapeDtypeStruct((heads, tall, block_rows), jnp.float32)

    return pl.pallas_call(
        kernel,
        out_shape=[turned(2 * HEAD_DIM)] + [turned(HEAD_DIM)] * 3 + [turned(block_rows)],
        in_specs=[VMEM] * 7,
        out_specs=[VMEM] * 5,
        compiler_params=pltpu.CompilerParams(vmem_limit_bytes=16 * 2**20),
        cost_estimate=weighed(1e9),
        name="own_products",
    )(keys, queries, upstream, values, grown_t, slopes_t, next_upstream)


def past_part(refs, past_key, group, heads):
    q, own_stats, tops, _, _, _, _, pv, dchances, bias = refs
    cols = [pl.ds(head * HEAD_DIM, HEAD_DIM) for head in group]
    tops = [tops[pl.ds(head, 1), :] for head in group]
    own_norms = [own_stats[pl.ds(head, 1), :] for head in group]
    own_offsets = [own_stats[pl.ds(heads + head, 1), :] for head in group]
    if past_key is None:
        return [(jnp.exp2(top - norm), None, None) for top, norm in zip(tops, own_norms)]
    keys = [past_key[:, c] for c in cols]
    scores = [by_rows(key, q[:, c]) * exp2_scale + bias[...] for key, c in zip(keys, cols)]
    maxes = [jnp.maximum(top, jnp.max(x, axis=0, keepdims=True)) for top, x in zip(tops, scores)]
    grown = [jnp.exp2(x - m) for x, m in zip(scores, maxes)]
    own = [jnp.exp2(norm - m) for norm, m in zip(own_norms, maxes)]
    shares = [1.0 / (o + jnp.sum(x, axis=0, keepdims=True)) for o, x in zip(own, grown)]
    offsets = [
        y * (offset * o + jnp.sum(x * dchances[head], axis=0, keepdims=True))
        for head, offset, o, x, y in zip(group, own_offsets, own, grown, shares)
    ]
    factors = [jnp.exp2(top - m) * y for top, m, y in zip(tops, maxes, shares)]
    shifts = [f * (o - offset) for f, o, offset in zip(factors, offsets, own_offsets)]
    chances = [x * y for x, y in zip(grown, shares)]
    weights = [x.astype(jnp.bfloat16) for x in chances]
    dscores = [(x * (dchances[head] - o)).astype(jnp.bfloat16) for x, head, o in zip(chances, group, offsets)]
    return list(zip(factors, shifts, zip(weights, dscores, keys)))


def scaled_rows(refs, part, head):
    _, _, _, _, _, query_t, up_t, _, _, _ = refs
    factor, shift, _ = part
    query, up = query_t[head], up_t[head]
    if shift is None:
        shifted = jnp.zeros(query.shape, jnp.bfloat16)
    else:
        shifted = (query * -shift).astype(jnp.bfloat16)
    return (query * factor).astype(jnp.bfloat16), shifted, (up * factor).astype(jnp.bfloat16)


def done_rows(refs, part, head):
    _, _, _, sums, slope_keys, _, _, pv, _, _ = refs
    factor, shift, past = part
    attended, grads = factor * sums[head, :HEAD_DIM], factor * slope_keys[head]
    if past is not None:
        weights, dscores, key = past
        attended = attended + product(pv[head], weights)
        grads = grads - shift * sums[head, HEAD_DIM:] + by_columns(key, dscores)
    return (
        jnp.transpose(attended.astype(jnp.bfloat16)),
        jnp.transpose((score_scale * grads).astype(jnp.bfloat16)),
    )


def own_gradients(grown_t, slopes_t, scaled, head):
    scaled_query, shifted_query, scaled_up = scaled
    mixed = by_rows(grown_t[head], jnp.concatenate([scaled_up, shifted_query], axis=0))
    return mixed[:, :HEAD_DIM], mixed[:, HEAD_DIM:] + by_rows(slopes_t[head], scaled_query)


def before_exchanges(upstream, previous_values, queries, stats, tops, own, grown_t, slopes_t):
    pairs = len(previous_values)
    block_rows, width = upstream.shape
    rows = block_rows // pairs // 2
    heads = width // HEAD_DIM

    def kernel(u, q, own_stats, tops, sums, slope_keys, query_t, up_t, grown_t, slopes_t, *rest):
        pieces, (turned, dchances, attended, query_grads, value_own, key_own, values) = rest[:pairs], rest[pairs:]
        first = lax.axis_index("blk") == 0

        @pl.when(jnp.logical_not(first))
        def _():
            for step in range(2 * pairs):
                values[place(step, rows), :] = pieces[step // 2][pl.ds(step % 2 * rows, rows), :]
            for head in range(heads):
                columns = pl.ds(head * HEAD_DIM, HEAD_DIM)
                dchances[head] = by_rows(values[:, columns], u[:, columns])
                turned[head] = jnp.transpose(values[:, columns])

        @pl.when(first)
        def _():
            refs = (q, own_stats, tops, sums, slope_keys, query_t, up_t, turned, dchances, None)
            for head, part in enumerate(past_part(refs, None, range(heads), heads)):
                columns = pl.ds(head * HEAD_DIM, HEAD_DIM)
                attended[:, columns], query_grads[:, columns] = done_rows(refs, part, head)
                value_own[:, columns], key_own[:, columns] = own_gradients(
                    grown_t, slopes_t, scaled_rows(refs, part, head), head
                )

    wide = jax.ShapeDtypeStruct((block_rows, width), jnp.float32)
    return pl.pallas_call(
        kernel,
        out_shape=[
            bf16(heads, HEAD_DIM, block_rows),
            jax.ShapeDtypeStruct((heads, block_rows, block_rows), jnp.float32),
            bf16(block_rows, width),
            bf16(block_rows, width),
            wide,
            wide,
        ],
        in_specs=[VMEM] * (10 + pairs),
        out_specs=[VMEM] * 6,
        scratch_shapes=[pltpu.VMEM((block_rows, width), jnp.bfloat16)],
        compiler_params=pltpu.CompilerParams(vmem_limit_bytes=12 * 2**20),
        cost_estimate=weighed(1e9),
        name="before_exchanges",
    )(upstream, queries, stats, tops, *own, grown_t, slopes_t, *previous_values)


def next_part(refs, later_query, group, heads, extra=None):
    k, nu, stats, later, bias = refs
    cols = [pl.ds(head * HEAD_DIM, HEAD_DIM) for head in group]
    scores = [by_rows(k[:, c], later_query[:, c]) * exp2_scale + bias[...] for c in cols]
    more = [extra(head) for head in group] if extra else None
    far = [stats[pl.ds(head, 1), :] for head in group]
    maxes = [jnp.maximum(f, jnp.max(x, axis=0, keepdims=True)) for f, x in zip(far, scores)]
    grown = [jnp.exp2(x - m) for x, m in zip(scores, maxes)]
    far = [jnp.exp2(f - m) for f, m in zip(far, maxes)]
    shares = [1.0 / (f + jnp.sum(x, axis=0, keepdims=True)) for f, x in zip(far, grown)]
    offsets = [
        y * (stats[pl.ds(heads + head, 1), :] * f + jnp.sum(x * later[head], axis=0, keepdims=True))
        for head, f, x, y in zip(group, far, grown, shares)
    ]
    chances = [x * y for x, y in zip(grown, shares)]
    weights = [x.astype(jnp.bfloat16) for x in chances]
    dscores = [(x * (later[head] - o)).astype(jnp.bfloat16) for x, head, o in zip(chances, group, offsets)]
    parts = [
        [product(weights[n], nu[:, c]), product(dscores[n], later_query[:, c])] for n, c in enumerate(cols)
    ]
    if more:
        parts = [[x + y for x, y in zip(*pair)] for pair in zip(parts, more)]
    return parts


def first_half(keys, first_got, next_upstream, first_stats, later, next_bias, past_refs):
    block_rows, width = keys.shape
    heads = width // HEAD_DIM
    past_count = len(past_refs)

    def kernel(k, first, nu, stats, later, next_bias, *rest):
        past_in, results = rest[:past_count], rest[past_count : past_count + 5]
        value_part, key_part = rest[past_count + 5 :]

        @pl.when(is_even())
        def _():
            for start in range(0, heads, GROUP):
                group = range(start, min(start + GROUP, heads))
                parts = next_part((k, nu, stats, later, next_bias), first, group, heads)
                for head, (value, key) in zip(group, parts):
                    columns = pl.ds(head * HEAD_DIM, HEAD_DIM)
                    value_part[:, columns] = value
                    key_part[:, columns] = key

        @pl.when(jnp.logical_not(is_even()))
        def _():
            for start in range(0, heads, GROUP):
                group = range(start, min(start + GROUP, heads))
                for head, part in zip(group, past_part(past_in, first, group, heads)):
                    columns = pl.ds(head * HEAD_DIM, HEAD_DIM)
                    results[0][:, columns], results[1][:, columns] = done_rows(past_in, part, head)
                    for target, rows in zip(results[2:], scaled_rows(past_in, part, head)):
                        target[head] = rows

    wide = jax.ShapeDtypeStruct((block_rows, width), jnp.float32)
    out = pl.pallas_call(
        kernel,
        out_shape=[bf16(block_rows, width)] * 2 + [bf16(heads, HEAD_DIM, block_rows)] * 3 + [wide] * 2,
        in_specs=[VMEM] * (6 + past_count),
        out_specs=[VMEM] * 7,
        compiler_params=pltpu.CompilerParams(vmem_limit_bytes=20 * 2**20),
        cost_estimate=weighed(0),
        name="first_half",
    )(keys, first_got, next_upstream, first_stats, later, next_bias, *past_refs)
    return out[:5], out[5:]


def second_half(keys, second_got, next_upstream, second_stats, later, next_bias, grown_t, slopes_t, past_refs, done, parts, early):
    block_rows, width = keys.shape
    heads = width // HEAD_DIM
    past_count = len(past_refs)

    def kernel(k, second, nu, stats, later, next_bias, grown_t, slopes_t, *rest):
        past_in, rest = rest[:past_count], rest[past_count:]
        done, (value_part, key_part), early, outs, rest = rest[:5], rest[5:7], rest[7:11], rest[11:15], rest[15:]
        attended, query_grads, key_grads, value_grads, sems = rest

        def send(rows, i, slot, columns=slice(None)):
            copy = pltpu.make_async_copy(rows.at[:, columns], outs[i].at[:, columns], sems.at[slot])
            copy.start()
            return copy

        def all_but_past():
            copies = [send(done[0], 0, 0), send(done[1], 1, 1)]
            for start in range(0, heads, PAIR):
                group = range(start, min(start + PAIR, heads))
                parts = next_part(
                    (k, nu, stats, later, next_bias), second, group, heads,
                    lambda head: own_gradients(grown_t, slopes_t, [rows[head] for rows in done[2:]], head),
                )
                for head, (value, key) in zip(group, parts):
                    columns = pl.ds(head * HEAD_DIM, HEAD_DIM)
                    value_grads[:, columns] = value.astype(jnp.bfloat16)
                    key_grads[:, columns] = (score_scale * key).astype(jnp.bfloat16)
                columns = pl.ds(start * HEAD_DIM, len(group) * HEAD_DIM)
                copies.append(send(key_grads, 2, len(copies), columns))
                copies.append(send(value_grads, 3, len(copies), columns))
            for copy in copies:
                copy.wait()

        def all_but_next(past_key):
            past = past_part(past_in, past_key, range(heads), heads)
            copies = []
            half = (heads + 1) // 2
            groups = (range(half), range(half, heads))

            def write_rows(group):
                for head in group:
                    columns = pl.ds(head * HEAD_DIM, HEAD_DIM)
                    attended[:, columns], query_grads[:, columns] = done_rows(past_in, past[head], head)
                columns = pl.ds(group.start * HEAD_DIM, len(group) * HEAD_DIM)
                copies.append(send(attended, 0, len(copies), columns))
                copies.append(send(query_grads, 1, len(copies), columns))

            def write_gradients(group):
                for head in group:
                    value, key = own_gradients(grown_t, slopes_t, scaled_rows(past_in, past[head], head), head)
                    columns = pl.ds(head * HEAD_DIM, HEAD_DIM)
                    value_grads[:, columns] = (value + value_part[:, columns]).astype(jnp.bfloat16)
                    key_grads[:, columns] = (score_scale * (key + key_part[:, columns])).astype(jnp.bfloat16)
                columns = pl.ds(group.start * HEAD_DIM, len(group) * HEAD_DIM)
                copies.append(send(key_grads, 2, len(copies), columns))
                copies.append(send(value_grads, 3, len(copies), columns))

            write_rows(groups[0])
            write_rows(groups[1])
            write_gradients(groups[0])
            write_gradients(groups[1])
            for copy in copies:
                copy.wait()

        block = lax.axis_index("blk")

        @pl.when(block == 0)
        def _():
            copies = [send(early[0], 0, 0), send(early[1], 1, 1)]
            value_grads[...] = (early[2][...] + value_part[...]).astype(jnp.bfloat16)
            key_grads[...] = (score_scale * (early[3][...] + key_part[...])).astype(jnp.bfloat16)
            copies += [send(key_grads, 2, 2), send(value_grads, 3, 3)]
            for copy in copies:
                copy.wait()

        @pl.when(jnp.logical_and(is_even(), block > 0))
        def _():
            all_but_next(second)

        @pl.when(jnp.logical_not(is_even()))
        def _():
            all_but_past()

    return pl.pallas_call(
        kernel,
        out_shape=[bf16(block_rows, width)] * 4,
        in_specs=[VMEM] * (19 + past_count),
        out_specs=[ANY] * 4,
        scratch_shapes=[pltpu.VMEM((block_rows, width), jnp.bfloat16)] * 4
        + [pltpu.SemaphoreType.DMA((4 * heads,))],
        compiler_params=pltpu.CompilerParams(vmem_limit_bytes=20 * 2**20),
        cost_estimate=weighed(0),
        name="second_half",
    )(
        keys, second_got, next_upstream, second_stats, later, next_bias, grown_t, slopes_t, *past_refs, *done, *parts, *early,
    )


def on_device(queries, key_states, value_states, upstream, clip_lengths):
    sharers = lax.axis_size("head")
    rows = queries.shape[0]
    pieces = cut_pieces(queries, key_states, value_states)
    pieces = [partner_exchange(piece, step + 1) for step, piece in enumerate(pieces)]
    first, second = stack_values(value_states, pieces[0], upstream, rows)
    first_got, second_got = block_exchange(first, 0), block_exchange(second, 1)
    far_values, (own_bias, past_bias, next_bias) = stack_far_values(value_states, pieces[0], clip_lengths, rows)
    far_values = [partner_exchange(stack, 2 * pair + 2) for pair, stack in enumerate(far_values)]
    keys, query_rows, first, second = join_keys_queries(key_states, queries, pieces)
    previous, next_upstream = cut_previous_values(first_got, second_got, sharers // 2)
    first_got, second_got = block_exchange(first, 0), block_exchange(second, 1)
    previous = [partner_exchange(stack, 2 * pair) if pair else stack for pair, stack in enumerate(previous)]
    values, stats, tops, grown_t, slopes_t = own_scores(
        keys, query_rows, (value_states, pieces[0]), far_values, upstream, own_bias, next_upstream
    )
    first_stats, second_stats = block_exchange(stats, 0), block_exchange(stats, 1)
    *own, later = own_products(keys, query_rows, upstream, values, grown_t, slopes_t, next_upstream)
    past_values, dchances, *early = before_exchanges(
        upstream, previous, query_rows, stats, tops, own, grown_t, slopes_t
    )
    past_refs = (query_rows, stats, tops, *own, past_values, dchances, past_bias)
    done, parts = first_half(keys, first_got, next_upstream, first_stats, later, next_bias, past_refs)
    return tuple(
        second_half(
            keys, second_got, next_upstream, second_stats, later, next_bias, grown_t, slopes_t, past_refs, done, parts,
            early,
        )
    )


def solution(mesh):
    return jax.shard_map(
        on_device,
        mesh=mesh,
        in_specs=(
            P(("dp", "blk", "head"), None),
            P(("dp", "blk", "head"), None),
            P(("dp", "blk", "head"), None),
            P(("dp", "blk"), "head"),
            P("dp"),
        ),
        out_specs=(
            P(("dp", "blk"), "head"),
            P(("dp", "blk"), "head"),
            P(("dp", "blk"), "head"),
            P(("dp", "blk"), "head"),
        ),
        check_vma=False,
    )
```

```python
import math

import jax
import jax.numpy as jnp
from jax import lax
from jax.experimental import pallas as pl
from jax.experimental.pallas import tpu as pltpu
from jax.sharding import PartitionSpec as P

HEAD_DIM = 128
GROUP = 4
PAIR = 2

masked_fill = -1e30
score_scale = HEAD_DIM ** (-0.5)
exp2_scale = score_scale * math.log2(math.e)

VMEM = pl.BlockSpec(memory_space=pltpu.VMEM)
SMEM = pl.BlockSpec(memory_space=pltpu.SMEM)
ANY = pl.BlockSpec(memory_space=pl.ANY)


def bf16(*shape):
    return jax.ShapeDtypeStruct(shape, jnp.bfloat16)


def partner_exchange(rows, step):
    route = [(i, i ^ step) for i in range(lax.axis_size("head"))]
    return lax.ppermute(rows, "head", route)


def sent_step(step, sharer):
    if step < 2:
        return step
    above = sharer // (1 << (step.bit_length() - 1)) % 2
    return step - step % 2 + (above if step % 2 == 0 else 1 - above)


def got_step(step, sharer):
    return step if step < 2 else sent_step(step ^ 1, sharer)


def pieces_exchange(rows, step):
    route = [(i, i ^ sent_step(step, i)) for i in range(lax.axis_size("head"))]
    return lax.ppermute(rows, "head", route)


def block_exchange(rows, parity):
    parts, blocks, sharers = lax.axis_size("dp"), lax.axis_size("blk"), lax.axis_size("head")
    route = []
    for part in range(parts):
        for block in range(blocks):
            other = block + 1 if block % 2 == parity else block - 1
            for sharer in range(sharers):
                here = (part * blocks + block) * sharers + sharer
                if 0 <= other < blocks:
                    route.append((here, (part * blocks + other) * sharers + sharer))
                else:
                    route.append((here, here ^ 1))
    return lax.ppermute(rows, ("dp", "blk", "head"), route)


def is_even():
    return lax.rem(lax.axis_index("blk"), 2) == 0


def place(step, size):
    owner = jnp.bitwise_xor(lax.axis_index("head"), step)
    return pl.ds(pl.multiple_of(owner * size, size), size)


def small_kernel():
    return pltpu.CompilerParams(vmem_limit_bytes=4 * 2**20)


def weighed(flops):
    return pl.CostEstimate(flops=int(flops), bytes_accessed=0, transcendentals=0)


def cut_pieces(queries, key_states, value_states):
    sharers = lax.axis_size("head")
    rows, features = queries.shape
    width = features // sharers
    heights = [(2 + sharers // 2) * rows if step == 1 else 2 * rows for step in range(1, sharers)]

    def kernel(q, k, v, *rest):
        pieces, sems = rest[: sharers - 1], rest[sharers - 1]
        copies = []

        def copy(source, target):
            copies.append(pltpu.make_async_copy(source, target, sems.at[len(copies)]))

        for step in range(1, sharers):
            columns = place(sent_step(step, lax.axis_index("head")), width)
            copy(k.at[:, columns], pieces[step - 1].at[pl.ds(0, rows)])
            copy(q.at[:, columns], pieces[step - 1].at[pl.ds(rows, rows)])
            if step % 2:
                copy(v.at[:, place(step, width)], pieces[0].at[pl.ds((2 + step // 2) * rows, rows)])
        for c in copies:
            c.start()
        for c in copies:
            c.wait()

    return pl.pallas_call(
        kernel,
        out_shape=[bf16(height, width) for height in heights],
        in_specs=[ANY] * 3,
        out_specs=[VMEM] * (sharers - 1),
        scratch_shapes=[pltpu.SemaphoreType.DMA((3 * sharers,))],
        compiler_params=pltpu.CompilerParams(vmem_limit_bytes=int(53.25 * 2**20)),
        name="cut_pieces",
    )(queries, key_states, value_states)


def stack_far_values(own_values, got, clip_lengths, rows):
    pairs = got.shape[0] // rows - 2
    width = got.shape[1]
    block_rows = 2 * pairs * rows

    def kernel(mine, theirs, lengths, own, past, ahead, *out):
        for pair in range(1, pairs):
            out[pair - 1][pl.ds(0, rows), :] = mine[:, place(2 * pair, width)]
            out[pair - 1][pl.ds(rows, rows), :] = theirs[pl.ds((2 + pair) * rows, rows), :]
        block, blocks = lax.axis_index("blk"), lax.axis_size("blk")
        tall, wide = (block_rows, 1), (1, block_rows)
        key_ids, row_ids = clip_ids(lengths, tall, 0, block, blocks), clip_ids(lengths, wide, 1, block, blocks)
        own[...] = mask_bias(key_ids, row_ids)
        past[...] = mask_bias(clip_ids(lengths, tall, 0, block - 1, blocks), row_ids)
        ahead[...] = mask_bias(key_ids, clip_ids(lengths, wide, 1, block + 1, blocks))

    out = pl.pallas_call(
        kernel,
        out_shape=[jax.ShapeDtypeStruct((block_rows, block_rows), jnp.float32)] * 3
        + [bf16(2 * rows, width)] * (pairs - 1),
        in_specs=[VMEM] * 2 + [SMEM],
        out_specs=[VMEM] * (pairs + 2),
        compiler_params=small_kernel(),
        cost_estimate=weighed(5e9),
        name="stack_far_values",
    )(own_values, got, clip_lengths)
    return out[3:], out[:3]


def stack_values(own_values, got, upstream, rows):
    pairs = got.shape[0] // rows - 2
    width = got.shape[1]
    block_rows = upstream.shape[0]

    def kernel(mine, theirs, u, first, second):
        def spread(forward, backward):
            for pair in range(pairs):
                where = pl.ds((2 + pair) * rows, rows)
                forward[pl.ds(2 * pair * rows, rows), :] = mine[:, place(2 * pair, width)]
                forward[pl.ds((2 * pair + 1) * rows, rows), :] = theirs[where, :]
            backward[...] = u[...]

        @pl.when(is_even())
        def _():
            spread(first, second)

        @pl.when(jnp.logical_not(is_even()))
        def _():
            spread(second, first)

    return pl.pallas_call(
        kernel,
        out_shape=[bf16(block_rows, width)] * 2,
        in_specs=[VMEM] * 3,
        out_specs=[VMEM] * 2,
        compiler_params=small_kernel(),
        cost_estimate=weighed(0),
        name="stack_values",
    )(own_values, got, upstream)


def join_keys_queries(key_states, own_queries, pieces):
    sharers = len(pieces) + 1
    rows, width = key_states.shape[0], pieces[0].shape[1]
    block_rows = rows * sharers

    def kernel(k, q, *refs):
        pieces_in = refs[: sharers - 1]
        keys, queries, first, second = refs[sharers - 1 :]
        keys[place(0, rows), :] = k[:, place(0, width)]
        queries[place(0, rows), :] = q[:, place(0, width)]
        for step in range(1, sharers):
            where = place(got_step(step, lax.axis_index("head")), rows)
            keys[where, :] = pieces_in[step - 1][pl.ds(0, rows), :]
            queries[where, :] = pieces_in[step - 1][pl.ds(rows, rows), :]

        @pl.when(is_even())
        def _():
            first[...] = keys[...]
            second[...] = queries[...]

        @pl.when(jnp.logical_not(is_even()))
        def _():
            first[...] = queries[...]
            second[...] = keys[...]

    return pl.pallas_call(
        kernel,
        out_shape=[bf16(block_rows, width)] * 4,
        in_specs=[VMEM] * (sharers + 1),
        out_specs=[VMEM] * 4,
        compiler_params=small_kernel(),
        cost_estimate=weighed(0),
        name="join_keys_queries",
    )(key_states, own_queries, *pieces)


def cut_previous_values(first_got, second_got, pairs):
    block_rows, width = first_got.shape
    rows = block_rows // pairs

    def kernel(first, second, *out):
        def split(forward, backward):
            for pair in range(pairs):
                out[pair][...] = forward[pl.ds(pair * rows, rows), :]
            out[pairs][...] = backward[...]

        @pl.when(is_even())
        def _():
            split(second, first)

        @pl.when(jnp.logical_not(is_even()))
        def _():
            split(first, second)

    out = pl.pallas_call(
        kernel,
        out_shape=[bf16(rows, width)] * pairs + [bf16(block_rows, width)],
        in_specs=[VMEM] * 2,
        out_specs=[VMEM] * (pairs + 1),
        compiler_params=small_kernel(),
        cost_estimate=weighed(0),
        name="cut_previous_values",
    )(first_got, second_got)
    return out[:pairs], out[pairs]


def clip_ids(lengths, shape, axis, block, blocks):
    position = block * shape[axis] + lax.broadcasted_iota(jnp.int32, shape, axis)
    ids, end = jnp.zeros(shape, jnp.int32), jnp.int32(0)
    for clip in range(lengths.shape[0]):
        end = end + lengths[clip]
        ids = ids + (position >= end).astype(jnp.int32)
    return jnp.where(jnp.logical_and(block >= 0, block < blocks), ids, -1)


def mask_bias(key_ids, query_ids):
    return jnp.where(key_ids == query_ids, 0.0, masked_fill).astype(jnp.float32)


def by_rows(a, b):
    return lax.dot_general(a, b, (((1,), (1,)), ((), ())), preferred_element_type=jnp.float32)


def by_columns(a, b):
    return lax.dot_general(a, b, (((0,), (0,)), ((), ())), preferred_element_type=jnp.float32)


def product(a, b):
    return jnp.dot(a, b, preferred_element_type=jnp.float32)


def own_scores(keys, queries, chip_values, far_values, upstream, bias, after):
    sharers = 2 + 2 * len(far_values)
    block_rows, width = keys.shape
    rows = block_rows // sharers
    heads = width // HEAD_DIM

    def kernel(k, q, u, bias, _, *rest):
        values_in = [rest[0].at[:, place(0, width)], rest[1].at[pl.ds(2 * rows, rows)]]
        for ref in rest[2 : 1 + sharers // 2]:
            values_in += [ref.at[pl.ds(0, rows)], ref.at[pl.ds(rows, rows)]]
        values, stats, tops, grown_t, slopes_t = rest[1 + sharers // 2 :]
        for step in range(sharers):
            values[place(step, rows), :] = values_in[step][...]
        for start in range(0, heads, GROUP):
            group = range(start, min(start + GROUP, heads))
            cols = [pl.ds(head * HEAD_DIM, HEAD_DIM) for head in group]
            scores = [by_rows(k[:, c], q[:, c]) * exp2_scale + bias[...] for c in cols]
            maxes = [jnp.max(x, axis=0, keepdims=True) for x in scores]
            grown = [jnp.exp2(x - m) for x, m in zip(scores, maxes)]
            totals = [jnp.sum(x, axis=0, keepdims=True) for x in grown]
            dchances = [by_rows(values[:, c], u[:, c]) for c in cols]
            offsets = [
                jnp.sum(x * d, axis=0, keepdims=True) / total for x, d, total in zip(grown, dchances, totals)
            ]
            for n, head in enumerate(group):
                stats[pl.ds(head, 1), :] = maxes[n] + jnp.log2(totals[n])
                stats[pl.ds(heads + head, 1), :] = offsets[n]
                tops[pl.ds(head, 1), :] = maxes[n]
                grown_t[head] = grown[n].astype(jnp.bfloat16)
                slopes_t[head] = (grown[n] * (dchances[n] - offsets[n])).astype(jnp.bfloat16)

    square = bf16(heads, block_rows, block_rows)
    return pl.pallas_call(
        kernel,
        out_shape=[
            bf16(block_rows, width),
            jax.ShapeDtypeStruct((2 * heads, block_rows), jnp.float32),
            jax.ShapeDtypeStruct((heads, block_rows), jnp.float32),
            square,
            square,
        ],
        in_specs=[VMEM] * (6 + sharers // 2),
        out_specs=[VMEM] * 5,
        compiler_params=pltpu.CompilerParams(vmem_limit_bytes=12 * 2**20),
        cost_estimate=weighed(0),
        name="own_scores",
    )(keys, queries, upstream, bias, after, *chip_values, *far_values)


def own_products(keys, queries, upstream, values, grown_t, slopes_t, next_upstream):
    block_rows, width = keys.shape
    heads = width // HEAD_DIM

    def kernel(k, q, u, v, grown_t, slopes_t, nu, sums, slope_keys, query_t, up_t, later):
        for head in range(heads):
            columns = pl.ds(head * HEAD_DIM, HEAD_DIM)
            key, value = k[:, columns], v[:, columns]
            sums[head] = by_columns(jnp.concatenate([value, key], axis=1), grown_t[head])
            slope_keys[head] = by_columns(key, slopes_t[head])
            query_t[head] = jnp.transpose(q[:, columns]).astype(jnp.float32)
            up_t[head] = jnp.transpose(u[:, columns]).astype(jnp.float32)
            later[head] = by_rows(value, nu[:, columns])

    def turned(tall):
        return jax.ShapeDtypeStruct((heads, tall, block_rows), jnp.float32)

    return pl.pallas_call(
        kernel,
        out_shape=[turned(2 * HEAD_DIM)] + [turned(HEAD_DIM)] * 3 + [turned(block_rows)],
        in_specs=[VMEM] * 7,
        out_specs=[VMEM] * 5,
        compiler_params=pltpu.CompilerParams(vmem_limit_bytes=16 * 2**20),
        cost_estimate=weighed(1e9),
        name="own_products",
    )(keys, queries, upstream, values, grown_t, slopes_t, next_upstream)


def past_part(refs, past_key, group, heads):
    q, own_stats, tops, _, _, _, _, pv, dchances, bias = refs
    cols = [pl.ds(head * HEAD_DIM, HEAD_DIM) for head in group]
    tops = [tops[pl.ds(head, 1), :] for head in group]
    own_norms = [own_stats[pl.ds(head, 1), :] for head in group]
    own_offsets = [own_stats[pl.ds(heads + head, 1), :] for head in group]
    if past_key is None:
        return [(jnp.exp2(top - norm), None, None) for top, norm in zip(tops, own_norms)]
    keys = [past_key[:, c] for c in cols]
    scores = [by_rows(key, q[:, c]) * exp2_scale + bias[...] for key, c in zip(keys, cols)]
    maxes = [jnp.maximum(top, jnp.max(x, axis=0, keepdims=True)) for top, x in zip(tops, scores)]
    grown = [jnp.exp2(x - m) for x, m in zip(scores, maxes)]
    own = [jnp.exp2(norm - m) for norm, m in zip(own_norms, maxes)]
    shares = [1.0 / (o + jnp.sum(x, axis=0, keepdims=True)) for o, x in zip(own, grown)]
    offsets = [
        y * (offset * o + jnp.sum(x * dchances[head], axis=0, keepdims=True))
        for head, offset, o, x, y in zip(group, own_offsets, own, grown, shares)
    ]
    factors = [jnp.exp2(top - m) * y for top, m, y in zip(tops, maxes, shares)]
    shifts = [f * (o - offset) for f, o, offset in zip(factors, offsets, own_offsets)]
    chances = [x * y for x, y in zip(grown, shares)]
    weights = [x.astype(jnp.bfloat16) for x in chances]
    dscores = [(x * (dchances[head] - o)).astype(jnp.bfloat16) for x, head, o in zip(chances, group, offsets)]
    return list(zip(factors, shifts, zip(weights, dscores, keys)))


def scaled_rows(refs, part, head):
    _, _, _, _, _, query_t, up_t, _, _, _ = refs
    factor, shift, _ = part
    query, up = query_t[head], up_t[head]
    if shift is None:
        shifted = jnp.zeros(query.shape, jnp.bfloat16)
    else:
        shifted = (query * -shift).astype(jnp.bfloat16)
    return (query * factor).astype(jnp.bfloat16), shifted, (up * factor).astype(jnp.bfloat16)


def done_rows(refs, part, head):
    _, _, _, sums, slope_keys, _, _, pv, _, _ = refs
    factor, shift, past = part
    attended, grads = factor * sums[head, :HEAD_DIM], factor * slope_keys[head]
    if past is not None:
        weights, dscores, key = past
        attended = attended + product(pv[head], weights)
        grads = grads - shift * sums[head, HEAD_DIM:] + by_columns(key, dscores)
    return (
        jnp.transpose(attended.astype(jnp.bfloat16)),
        jnp.transpose((score_scale * grads).astype(jnp.bfloat16)),
    )


def own_gradients(grown_t, slopes_t, scaled, head):
    scaled_query, shifted_query, scaled_up = scaled
    mixed = by_rows(grown_t[head], jnp.concatenate([scaled_up, shifted_query], axis=0))
    return mixed[:, :HEAD_DIM], mixed[:, HEAD_DIM:] + by_rows(slopes_t[head], scaled_query)


def before_exchanges(upstream, previous_values, queries, stats, tops, own, grown_t, slopes_t):
    pairs = len(previous_values)
    block_rows, width = upstream.shape
    rows = block_rows // pairs // 2
    heads = width // HEAD_DIM

    def kernel(u, q, own_stats, tops, sums, slope_keys, query_t, up_t, grown_t, slopes_t, *rest):
        pieces, (turned, dchances, attended, query_grads, value_own, key_own, values) = rest[:pairs], rest[pairs:]
        first = lax.axis_index("blk") == 0

        @pl.when(jnp.logical_not(first))
        def _():
            for step in range(2 * pairs):
                values[place(step, rows), :] = pieces[step // 2][pl.ds(step % 2 * rows, rows), :]
            for head in range(heads):
                columns = pl.ds(head * HEAD_DIM, HEAD_DIM)
                dchances[head] = by_rows(values[:, columns], u[:, columns])
                turned[head] = jnp.transpose(values[:, columns])

        @pl.when(first)
        def _():
            refs = (q, own_stats, tops, sums, slope_keys, query_t, up_t, turned, dchances, None)
            for head, part in enumerate(past_part(refs, None, range(heads), heads)):
                columns = pl.ds(head * HEAD_DIM, HEAD_DIM)
                attended[:, columns], query_grads[:, columns] = done_rows(refs, part, head)
                value_own[:, columns], key_own[:, columns] = own_gradients(
                    grown_t, slopes_t, scaled_rows(refs, part, head), head
                )

    wide = jax.ShapeDtypeStruct((block_rows, width), jnp.float32)
    return pl.pallas_call(
        kernel,
        out_shape=[
            bf16(heads, HEAD_DIM, block_rows),
            jax.ShapeDtypeStruct((heads, block_rows, block_rows), jnp.float32),
            bf16(block_rows, width),
            bf16(block_rows, width),
            wide,
            wide,
        ],
        in_specs=[VMEM] * (10 + pairs),
        out_specs=[VMEM] * 6,
        scratch_shapes=[pltpu.VMEM((block_rows, width), jnp.bfloat16)],
        compiler_params=pltpu.CompilerParams(vmem_limit_bytes=12 * 2**20),
        cost_estimate=weighed(1e9),
        name="before_exchanges",
    )(upstream, queries, stats, tops, *own, grown_t, slopes_t, *previous_values)


def next_part(refs, later_query, group, heads, extra=None):
    k, nu, stats, later, bias = refs
    cols = [pl.ds(head * HEAD_DIM, HEAD_DIM) for head in group]
    scores = [by_rows(k[:, c], later_query[:, c]) * exp2_scale + bias[...] for c in cols]
    more = [extra(head) for head in group] if extra else None
    far = [stats[pl.ds(head, 1), :] for head in group]
    maxes = [jnp.maximum(f, jnp.max(x, axis=0, keepdims=True)) for f, x in zip(far, scores)]
    grown = [jnp.exp2(x - m) for x, m in zip(scores, maxes)]
    far = [jnp.exp2(f - m) for f, m in zip(far, maxes)]
    shares = [1.0 / (f + jnp.sum(x, axis=0, keepdims=True)) for f, x in zip(far, grown)]
    offsets = [
        y * (stats[pl.ds(heads + head, 1), :] * f + jnp.sum(x * later[head], axis=0, keepdims=True))
        for head, f, x, y in zip(group, far, grown, shares)
    ]
    chances = [x * y for x, y in zip(grown, shares)]
    weights = [x.astype(jnp.bfloat16) for x in chances]
    dscores = [(x * (later[head] - o)).astype(jnp.bfloat16) for x, head, o in zip(chances, group, offsets)]
    parts = [
        [product(weights[n], nu[:, c]), product(dscores[n], later_query[:, c])] for n, c in enumerate(cols)
    ]
    if more:
        parts = [[x + y for x, y in zip(*pair)] for pair in zip(parts, more)]
    return parts


def first_half(keys, first_got, next_upstream, first_stats, later, next_bias, past_refs):
    block_rows, width = keys.shape
    heads = width // HEAD_DIM
    past_count = len(past_refs)

    def kernel(k, first, nu, stats, later, next_bias, *rest):
        past_in, results = rest[:past_count], rest[past_count : past_count + 5]
        value_part, key_part = rest[past_count + 5 :]

        @pl.when(is_even())
        def _():
            for start in range(0, heads, GROUP):
                group = range(start, min(start + GROUP, heads))
                parts = next_part((k, nu, stats, later, next_bias), first, group, heads)
                for head, (value, key) in zip(group, parts):
                    columns = pl.ds(head * HEAD_DIM, HEAD_DIM)
                    value_part[:, columns] = value
                    key_part[:, columns] = key

        @pl.when(jnp.logical_not(is_even()))
        def _():
            for start in range(0, heads, GROUP):
                group = range(start, min(start + GROUP, heads))
                for head, part in zip(group, past_part(past_in, first, group, heads)):
                    columns = pl.ds(head * HEAD_DIM, HEAD_DIM)
                    results[0][:, columns], results[1][:, columns] = done_rows(past_in, part, head)
                    for target, rows in zip(results[2:], scaled_rows(past_in, part, head)):
                        target[head] = rows

    wide = jax.ShapeDtypeStruct((block_rows, width), jnp.float32)
    out = pl.pallas_call(
        kernel,
        out_shape=[bf16(block_rows, width)] * 2 + [bf16(heads, HEAD_DIM, block_rows)] * 3 + [wide] * 2,
        in_specs=[VMEM] * (6 + past_count),
        out_specs=[VMEM] * 7,
        compiler_params=pltpu.CompilerParams(vmem_limit_bytes=20 * 2**20),
        cost_estimate=weighed(0),
        name="first_half",
    )(keys, first_got, next_upstream, first_stats, later, next_bias, *past_refs)
    return out[:5], out[5:]


def second_half(keys, second_got, next_upstream, second_stats, later, next_bias, grown_t, slopes_t, past_refs, done, parts, early):
    block_rows, width = keys.shape
    heads = width // HEAD_DIM
    past_count = len(past_refs)

    def kernel(k, second, nu, stats, later, next_bias, grown_t, slopes_t, *rest):
        past_in, rest = rest[:past_count], rest[past_count:]
        done, (value_part, key_part), early, outs, rest = rest[:5], rest[5:7], rest[7:11], rest[11:15], rest[15:]
        attended, query_grads, key_grads, value_grads, sems = rest

        def send(rows, i, slot, columns=slice(None)):
            copy = pltpu.make_async_copy(rows.at[:, columns], outs[i].at[:, columns], sems.at[slot])
            copy.start()
            return copy

        def all_but_past():
            copies = [send(done[0], 0, 0), send(done[1], 1, 1)]
            for start in range(0, heads, PAIR):
                group = range(start, min(start + PAIR, heads))
                parts = next_part(
                    (k, nu, stats, later, next_bias), second, group, heads,
                    lambda head: own_gradients(grown_t, slopes_t, [rows[head] for rows in done[2:]], head),
                )
                for head, (value, key) in zip(group, parts):
                    columns = pl.ds(head * HEAD_DIM, HEAD_DIM)
                    value_grads[:, columns] = value.astype(jnp.bfloat16)
                    key_grads[:, columns] = (score_scale * key).astype(jnp.bfloat16)
                columns = pl.ds(start * HEAD_DIM, len(group) * HEAD_DIM)
                copies.append(send(key_grads, 2, len(copies), columns))
                copies.append(send(value_grads, 3, len(copies), columns))
            for copy in copies:
                copy.wait()

        def all_but_next(past_key):
            past = past_part(past_in, past_key, range(heads), heads)
            copies = []
            half = (heads + 1) // 2
            groups = (range(half), range(half, heads))

            def write_rows(group):
                for head in group:
                    columns = pl.ds(head * HEAD_DIM, HEAD_DIM)
                    attended[:, columns], query_grads[:, columns] = done_rows(past_in, past[head], head)
                columns = pl.ds(group.start * HEAD_DIM, len(group) * HEAD_DIM)
                copies.append(send(attended, 0, len(copies), columns))
                copies.append(send(query_grads, 1, len(copies), columns))

            def write_gradients(group):
                for head in group:
                    value, key = own_gradients(grown_t, slopes_t, scaled_rows(past_in, past[head], head), head)
                    columns = pl.ds(head * HEAD_DIM, HEAD_DIM)
                    value_grads[:, columns] = (value + value_part[:, columns]).astype(jnp.bfloat16)
                    key_grads[:, columns] = (score_scale * (key + key_part[:, columns])).astype(jnp.bfloat16)
                columns = pl.ds(group.start * HEAD_DIM, len(group) * HEAD_DIM)
                copies.append(send(key_grads, 2, len(copies), columns))
                copies.append(send(value_grads, 3, len(copies), columns))

            write_rows(groups[0])
            write_rows(groups[1])
            write_gradients(groups[0])
            write_gradients(groups[1])
            for copy in copies:
                copy.wait()

        block = lax.axis_index("blk")

        @pl.when(block == 0)
        def _():
            copies = [send(early[0], 0, 0), send(early[1], 1, 1)]
            value_grads[...] = (early[2][...] + value_part[...]).astype(jnp.bfloat16)
            key_grads[...] = (score_scale * (early[3][...] + key_part[...])).astype(jnp.bfloat16)
            copies += [send(key_grads, 2, 2), send(value_grads, 3, 3)]
            for copy in copies:
                copy.wait()

        @pl.when(jnp.logical_and(is_even(), block > 0))
        def _():
            all_but_next(second)

        @pl.when(jnp.logical_not(is_even()))
        def _():
            all_but_past()

    return pl.pallas_call(
        kernel,
        out_shape=[bf16(block_rows, width)] * 4,
        in_specs=[VMEM] * (19 + past_count),
        out_specs=[ANY] * 4,
        scratch_shapes=[pltpu.VMEM((block_rows, width), jnp.bfloat16)] * 4
        + [pltpu.SemaphoreType.DMA((4 * heads,))],
        compiler_params=pltpu.CompilerParams(vmem_limit_bytes=20 * 2**20),
        cost_estimate=weighed(0),
        name="second_half",
    )(
        keys, second_got, next_upstream, second_stats, later, next_bias, grown_t, slopes_t, *past_refs, *done, *parts, *early,
    )


def on_device(queries, key_states, value_states, upstream, clip_lengths):
    sharers = lax.axis_size("head")
    rows = queries.shape[0]
    pieces = cut_pieces(queries, key_states, value_states)
    pieces = [pieces_exchange(piece, step + 1) for step, piece in enumerate(pieces)]
    first, second = stack_values(value_states, pieces[0], upstream, rows)
    first_got, second_got = block_exchange(first, 0), block_exchange(second, 1)
    far_values, (own_bias, past_bias, next_bias) = stack_far_values(value_states, pieces[0], clip_lengths, rows)
    far_values = [partner_exchange(stack, 2 * pair + 2) for pair, stack in enumerate(far_values)]
    keys, query_rows, first, second = join_keys_queries(key_states, queries, pieces)
    previous, next_upstream = cut_previous_values(first_got, second_got, sharers // 2)
    first_got, second_got = block_exchange(first, 0), block_exchange(second, 1)
    previous = [partner_exchange(stack, 2 * pair) if pair else stack for pair, stack in enumerate(previous)]
    values, stats, tops, grown_t, slopes_t = own_scores(
        keys, query_rows, (value_states, pieces[0]), far_values, upstream, own_bias, next_upstream
    )
    first_stats, second_stats = block_exchange(stats, 0), block_exchange(stats, 1)
    *own, later = own_products(keys, query_rows, upstream, values, grown_t, slopes_t, next_upstream)
    past_values, dchances, *early = before_exchanges(
        upstream, previous, query_rows, stats, tops, own, grown_t, slopes_t
    )
    past_refs = (query_rows, stats, tops, *own, past_values, dchances, past_bias)
    done, parts = first_half(keys, first_got, next_upstream, first_stats, later, next_bias, past_refs)
    return tuple(
        second_half(
            keys, second_got, next_upstream, second_stats, later, next_bias, grown_t, slopes_t, past_refs, done, parts,
            early,
        )
    )


def solution(mesh):
    return jax.shard_map(
        on_device,
        mesh=mesh,
        in_specs=(
            P(("dp", "blk", "head"), None),
            P(("dp", "blk", "head"), None),
            P(("dp", "blk", "head"), None),
            P(("dp", "blk"), "head"),
            P("dp"),
        ),
        out_specs=(
            P(("dp", "blk"), "head"),
            P(("dp", "blk"), "head"),
            P(("dp", "blk"), "head"),
            P(("dp", "blk"), "head"),
        ),
        check_vma=False,
    )
```
